32 devices in a mesh: batch: 4 (over z), wide: 8 (over y, x, core).
Axes of the slice: x: 2, y: 2, z: 4, core: 2. Of those that a mesh axis runs over, the one named last changes fastest.
Arguments:
- tokens: bfloat16 [2048, 8, 1024], P('wide', 'batch'), may hold values from -6 to 6
- lengths: int32 [8, 16], P('batch'), may hold values from 0 to 2048, as said below
- cotangent: bfloat16 [2048, 8, 1024], P('wide', 'batch'), may hold values from -6 to 6
- first_gain: float32 [1024], replicated, may hold values from 0.25 to 1.75
- query_heads: bfloat16 [1024, 96], replicated, may hold values from -0.4375 to 0.4375
- query_basis: bfloat16 [1024, 384], replicated, may hold values from -0.1875 to 0.1875
- key_heads: bfloat16 [1024, 32], replicated, may hold values from -0.4375 to 0.4375
- key_basis: bfloat16 [1024, 128], replicated, may hold values from -0.1875 to 0.1875
- value_heads: bfloat16 [1024, 32], replicated, may hold values from -0.1875 to 0.1875
- value_basis: bfloat16 [1024, 128], replicated, may hold values from -0.1875 to 0.1875
- output_weight: bfloat16 [1024, 1024], replicated, may hold values from -0.75 to 0.75
- second_gain: float32 [1024], replicated, may hold values from 0.25 to 1.75
- gate_weight: bfloat16 [1024, 2816], P(None, 'wide'), may hold values from -0.1875 to 0.1875
- up_weight: bfloat16 [1024, 2816], P(None, 'wide'), may hold values from -0.1875 to 0.1875
- down_projection_weight: bfloat16 [2816, 1024], P('wide'), may hold values from -0.109375 to 0.109375
Outputs:
- output: bfloat16 [2048, 8, 1024], P('wide', 'batch')
- tokens_gradient: float32 [2048, 8, 1024], P('wide', 'batch')
- first_gain_gradient: float32 [1024], P('wide')
- query_heads_gradient: float32 [1024, 96], P('wide')
- query_basis_gradient: float32 [1024, 384], P('wide')
- key_heads_gradient: float32 [1024, 32], P('wide')
- key_basis_gradient: float32 [1024, 128], P('wide')
- value_heads_gradient: float32 [1024, 32], P('wide')
- value_basis_gradient: float32 [1024, 128], P('wide')
- output_weight_gradient: float32 [1024, 1024], P('wide')
- second_gain_gradient: float32 [1024], P('wide')
- gate_weight_gradient: float32 [1024, 2816], P(None, 'wide')
- up_weight_gradient: float32 [1024, 2816], P(None, 'wide')
- down_weight_gradient: float32 [2816, 1024], P('wide')
The draws below stay inside these ranges and needn't reach their ends.
Inputs may be any that keep to these rules, and one draw needn't show every extreme that they name: In each packed row the nonzero lengths come first, each is 128 or more, and they sum to at most 2048; later slots hold 0, and the places after the last sequence are padding.
All inputs are finite; a program needn't handle non-finite values.
Results may differ from the reference program's by a relative error of at most 0.022.
The reference program's roundings to bfloat16 on the way count: a program that leaves them out, or rounds other values in their place, can miss the bound.
Values may be sent and summed in bfloat16 or wider, within the bound.
No kernel may reach another device: no remote copies, remote signals or barrier semaphores. Data moves between devices by JAX's collectives and lax.ppermute only.
A program may use at most 256 MiB of HBM per device.

```python
import jax
import jax.numpy as jnp
from jax import lax

D = 1024
HEADS = 16
HEAD_DIM = 64
Q_RANK = 6
KV_RANK = 2
FF = 2816
SEQ = 2048
LONGEST = 2048
SHORTEST = 128
SLOTS = 16
ROWS = 8


def draw_lengths(key, part):
    keys = jax.random.split(key, 3)
    span = LONGEST - SHORTEST
    first = jax.random.randint(keys[0], (ROWS, SLOTS), 0, span + 1)
    second = jax.random.randint(keys[1], (ROWS, SLOTS), 0, span + 1)
    third = jax.random.randint(keys[2], (ROWS, SLOTS), 0, span + 1)
    drawn = SHORTEST + jnp.minimum(jnp.minimum(first, second), third)
    drawn = drawn.at[0, 0].set(LONGEST)
    ends = jnp.cumsum(drawn, axis=1)
    return jnp.where(ends <= SEQ, drawn, 0).astype(jnp.int32)


def shard_levels(stream_key, shape, cuts, smallest, largest):
    level, own = 1.0, jax.random.fold_in(stream_key, 6)
    for axis_at, shards_of in cuts:
        steps = jnp.exp(jax.random.uniform(jax.random.fold_in(own, axis_at), (shards_of,), jnp.float32, smallest / len(cuts), largest / len(cuts)))
        level = level * jnp.repeat(steps, shape[axis_at] // shards_of).reshape([-1 if axis == axis_at else 1 for axis in range(len(shape))])
    return level


def scatter_about(stream_key, extent, width, limit, shards=(), kind=jnp.bfloat16):
    loudness = shard_levels(stream_key, extent, shards, -0.22, 0.18) if shards else 1.0
    array = jax.random.normal(stream_key, extent, jnp.float32) * width * loudness
    return jnp.minimum(jnp.maximum(array, -limit), limit).astype(kind)


def setup_inputs(seed: int = 0) -> dict:
    key_list = jax.random.split(jax.random.key(seed), 16)
    return {
        "tokens": scatter_about(key_list[0], (SEQ, ROWS, D), 1.0, 6.0, ((0, 8), (1, 4))),
        "lengths": draw_lengths(jax.random.fold_in(key_list[15], 71), 0),
        "cotangent": scatter_about(key_list[2], (SEQ, ROWS, D), 1.0, 6.0, ((0, 8), (1, 4))),
        "first_gain": jnp.clip(1.0 + 0.15 * jax.random.normal(key_list[3], (D,), jnp.float32), 0.25, 1.75),
        "query_heads": scatter_about(key_list[4], (D, HEADS * Q_RANK), (D // 6) ** -0.5, 0.4375),
        "query_basis": scatter_about(key_list[5], (D, Q_RANK * HEAD_DIM), D ** -0.5, 0.1875),
        "key_heads": scatter_about(key_list[6], (D, HEADS * KV_RANK), (D // 6) ** -0.5, 0.4375),
        "key_basis": scatter_about(key_list[7], (D, KV_RANK * HEAD_DIM), D ** -0.5, 0.1875),
        "value_heads": scatter_about(key_list[8], (D, HEADS * KV_RANK), D ** -0.5, 0.1875),
        "value_basis": scatter_about(key_list[9], (D, KV_RANK * HEAD_DIM), D ** -0.5, 0.1875),
        "output_weight": scatter_about(key_list[10], (HEADS * HEAD_DIM, D), (HEADS * HEAD_DIM // 16) ** -0.5, 0.75),
        "second_gain": jnp.clip(1.0 + 0.15 * jax.random.normal(key_list[11], (D,), jnp.float32), 0.25, 1.75),
        "gate_weight": scatter_about(key_list[12], (D, FF), D ** -0.5, 0.1875, ((1, 8),)),
        "up_weight": scatter_about(key_list[13], (D, FF), D ** -0.5, 0.1875, ((1, 8),)),
        "down_projection_weight": scatter_about(key_list[14], (FF, D), FF ** -0.5, 0.109375, ((0, 8),)),
    }


@jax.custom_vjp
def low(v):
    return lax.optimization_barrier(v.astype(jnp.bfloat16)).astype(jnp.float32)

@jax.custom_vjp
def low_back(v):
    return v

def low_keep(v):
    return (low(v), None)

def low_pass(kept, grad):
    return (grad,)

def back_keep(v):
    return (v, None)

def back_low(kept, grad):
    return (low(grad),)
low.defvjp(low_keep, low_pass)
low_back.defvjp(back_keep, back_low)
highest = lax.Precision.HIGHEST
masked_score = -1e+30

def matmul(left, right):
    return jnp.dot(left, right, precision=highest, preferred_element_type=jnp.float32)

def rms_norm(values, gain):
    return values * lax.rsqrt(lax.optimization_barrier(jnp.mean(values * values, axis=-1, keepdims=True)) + 1e-06) * gain

def rotate(values, cosine, sine):
    half = values.shape[-1] // 2
    first = values[..., :half]
    second = values[..., half:]
    return jnp.concatenate([first * cosine - second * sine, first * sine + second * cosine], axis=-1)

def row_layout(lengths_row, places):
    ends = jnp.cumsum(lengths_row).astype(jnp.int32)
    passed = ends[None, :] <= places[:, None]
    segment = lax.optimization_barrier(jnp.sum(passed.astype(jnp.int32), axis=1)).astype(jnp.int32)
    start = lax.optimization_barrier(jnp.max(jnp.where(passed, ends[None, :], 0), axis=1)).astype(jnp.int32)
    valid = places < ends[-1]
    return (segment, places - start, valid)

def rope_tables(position):
    half = HEAD_DIM // 2
    frequency = 10000.0 ** (-jnp.arange(half, dtype=jnp.float32) / half)
    angle = position.astype(jnp.float32)[..., None] * frequency
    return (jnp.cos(angle), jnp.sin(angle))

def row_forward(inputs, lengths_row, weights):
    first_gain, query_heads, query_basis, key_heads, key_basis, value_heads, value_basis, output_weight, second_gain, gate_weight, up_weight, down_projection_weight = weights
    places = jnp.arange(SEQ, dtype=jnp.int32)
    segment, position, valid = row_layout(lengths_row, places)
    cosine, sine = rope_tables(position)
    cosine = cosine[:, None, :]
    sine = sine[:, None, :]
    normed = low(rms_norm(inputs, first_gain))
    query_mix = low_back(matmul(normed, query_heads)).reshape(SEQ, HEADS, Q_RANK)
    query_base = rotate(low_back(matmul(normed, query_basis)).reshape(SEQ, Q_RANK, HEAD_DIM), cosine, sine)
    key_mix = low(low_back(matmul(normed, key_heads))).reshape(SEQ, HEADS, KV_RANK)
    key_base = low(rotate(low_back(matmul(normed, key_basis)).reshape(SEQ, KV_RANK, HEAD_DIM), cosine, sine))
    value_mix = low(low_back(matmul(normed, value_heads))).reshape(SEQ, HEADS, KV_RANK)
    value_base = low(low_back(matmul(normed, value_basis))).reshape(SEQ, KV_RANK, HEAD_DIM)
    query = low(jnp.einsum('thr,trd->thd', query_mix, query_base, precision=highest) / Q_RANK)
    keys = low(jnp.einsum('thr,trd->thd', key_mix, key_base, precision=highest) / KV_RANK)
    values = low(jnp.einsum('thr,trd->thd', value_mix, value_base, precision=highest) / KV_RANK)
    scale = HEAD_DIM ** (-0.5)
    block_rows = min(512, SEQ)

    def attend(block):
        begin = block * block_rows
        block_query = lax.dynamic_slice_in_dim(query, begin, block_rows, 0)
        rows = begin + jnp.arange(block_rows, dtype=jnp.int32)
        block_segment = lax.dynamic_slice_in_dim(segment, begin, block_rows, 0)
        allowed = (places[None, :] <= rows[:, None]) & (block_segment[:, None] == segment[None, :]) & (valid[None, :] | (places[None, :] == rows[:, None]))
        scores = low_back(jnp.einsum('qhd,khd->hqk', block_query, keys, precision=highest) * scale)
        scores = jnp.where(allowed[None], scores, masked_score)
        attention_weights = jax.nn.softmax(scores, axis=-1)
        return jnp.einsum('hqk,khd->qhd', low(attention_weights), values, precision=highest)
    mixed = lax.map(jax.checkpoint(attend), jnp.arange(SEQ // block_rows, dtype=jnp.int32))
    mixed = low_back(low(mixed.reshape(SEQ, HEADS * HEAD_DIM)))
    hidden_state = inputs + low_back(matmul(mixed, output_weight))
    normed_second = low(rms_norm(hidden_state, second_gain))
    gate = low_back(matmul(normed_second, gate_weight))
    lifted = low_back(matmul(normed_second, up_weight))
    silu_hidden_output = low(jax.nn.silu(gate) * lifted)
    branch = low_back(matmul(silu_hidden_output, down_projection_weight))
    return jnp.where(valid[:, None], hidden_state + branch, 0.0)

def reference(tokens, lengths, cotangent, first_gain, query_heads, query_basis, key_heads, key_basis, value_heads, value_basis, output_weight, second_gain, gate_weight, up_weight, down_projection_weight):
    inputs = jnp.transpose(tokens.astype(jnp.float32), (1, 0, 2))
    upstream = jnp.transpose(cotangent.astype(jnp.float32), (1, 0, 2))
    weights = tuple((item.astype(jnp.float32) for item in (first_gain, query_heads, query_basis, key_heads, key_basis, value_heads, value_basis, output_weight, second_gain, gate_weight, up_weight, down_projection_weight)))

    def forward(stacked, params):

        def step(carry, item):
            return (carry, jax.checkpoint(row_forward)(item[0], item[1], params))
        _, outputs = lax.scan(step, jnp.zeros((), jnp.float32), (stacked, lengths))
        return outputs
    result, pullback = jax.vjp(forward, inputs, weights)
    input_grad, grads = pullback(upstream)
    return (jnp.transpose(result, (1, 0, 2)).astype(jnp.bfloat16), jnp.transpose(input_grad, (1, 0, 2)), grads[0], grads[1], grads[2], grads[3], grads[4], grads[5], grads[6], grads[7], grads[8], grads[9], grads[10], grads[11])
```

```python
import functools

import jax
import jax.numpy as jnp
from jax import lax
from jax.experimental import pallas as pl
from jax.experimental.pallas import tpu as pltpu
from jax.sharding import PartitionSpec as P

HEADS = 16
HEAD_DIM = 64
Q_RANK = 6
KV_RANK = 2
HALF = HEAD_DIM // 2
MIX = HEADS * KV_RANK
BASE = KV_RANK * HEAD_DIM
FACTORS = 2 * MIX + 2 * BASE
QMIX = HEADS * Q_RANK
QBASE = Q_RANK * HEAD_DIM
QUAD = 4
QUADS = HEADS // QUAD
QW = QUAD * HEAD_DIM
TILE = 128
F32 = jnp.float32
BF16 = jnp.bfloat16
NEG = -1e30
MIB = 1 << 20


def mm(a, b):
    return jnp.dot(a, b, preferred_element_type=F32)


def mm_nt(a, b):
    return lax.dot_general(a, b, (((1,), (1,)), ((), ())), preferred_element_type=F32)


def mm_tn(a, b):
    return lax.dot_general(a, b, (((0,), (0,)), ((), ())), preferred_element_type=F32)


def whole(count):
    return [pl.BlockSpec(memory_space=pltpu.VMEM)] * count


def kernel_call(kernel, name, outs, scratch, smem, limit, *args):
    specs = [pl.BlockSpec(memory_space=pltpu.SMEM)] * smem + whole(len(args) - smem)
    return pl.pallas_call(
        kernel,
        out_shape=tuple(jax.ShapeDtypeStruct(s, t) for s, t in outs),
        in_specs=specs,
        out_specs=whole(len(outs)),
        scratch_shapes=scratch,
        compiler_params=pltpu.CompilerParams(vmem_limit_bytes=limit * MIB),
        name=name,
    )(*args)


def project_kernel(
    x_ref, gain_ref, qh_ref, qb_ref, kh_ref, kb_ref, vh_ref, vb_ref, cos_ref, sin_ref,
    fac_ref, qt_ref, qmix_ref, qbase_ref, normed_ref,
):
    x = x_ref[...].astype(F32)
    scale = lax.rsqrt(jnp.mean(x * x, axis=-1, keepdims=True) + 1e-06)
    normed = (x * scale * gain_ref[...]).astype(BF16)
    normed_ref[...] = normed
    cos = cos_ref[...]
    sin = sin_ref[...]

    def rope(v):
        a, b = v[:HALF], v[HALF:]
        return jnp.concatenate([a * cos - b * sin, a * sin + b * cos], axis=0)

    kb = mm(normed, kb_ref[...]).T
    fac_ref[0:MIX, :] = mm(normed, kh_ref[...]).T.astype(BF16)
    for r in range(KV_RANK):
        at = MIX + r * HEAD_DIM
        fac_ref[at : at + HEAD_DIM, :] = rope(kb[r * HEAD_DIM : (r + 1) * HEAD_DIM]).astype(BF16)
    fac_ref[MIX + BASE : 2 * MIX + BASE, :] = mm(normed, vh_ref[...]).T.astype(BF16)
    fac_ref[2 * MIX + BASE :, :] = mm(normed, vb_ref[...]).T.astype(BF16)
    qmix = mm(normed, qh_ref[...]).T
    qmix_ref[...] = qmix
    raw = mm(normed, qb_ref[...]).T
    base = [rope(raw[r * HEAD_DIM : (r + 1) * HEAD_DIM]) for r in range(Q_RANK)]
    for r in range(Q_RANK):
        qbase_ref[r * HEAD_DIM : (r + 1) * HEAD_DIM, :] = base[r]
    for h in range(HEADS):
        out = None
        for r in range(Q_RANK):
            part = qmix[h * Q_RANK + r : h * Q_RANK + r + 1, :] * base[r]
            out = part if out is None else out + part
        qt_ref[h * HEAD_DIM : (h + 1) * HEAD_DIM, :] = (
            (out * (1.0 / Q_RANK)).astype(BF16) * (HEAD_DIM ** -0.5)
        ).astype(BF16)


def project(x, gain, weights, cos, sin):
    local, d = x.shape
    width = HEADS * HEAD_DIM
    return kernel_call(
        project_kernel,
        "project",
        (
            ((FACTORS, local), BF16),
            ((width, local), BF16),
            ((QMIX, local), F32),
            ((QBASE, local), F32),
            ((local, d), BF16),
        ),
        [],
        0,
        30,
        x, gain, *weights, cos, sin,
    )


def materialize(fac, offset, head):
    base = offset + MIX
    out = None
    for r in range(KV_RANK):
        row = offset + head * KV_RANK + r
        part = fac[row : row + 1, :] * fac[base + r * HEAD_DIM : base + (r + 1) * HEAD_DIM, :]
        out = part if out is None else out + part
    return (out * (1.0 / KV_RANK)).astype(BF16)


def materialize_quad(fac, offset, quad):
    return jnp.concatenate(
        [materialize(fac, offset, quad * QUAD + i) for i in range(QUAD)], axis=0
    )


def key_range(span, tiles):
    lo = span[0]
    hi = span[1]
    for i in range(1, tiles):
        lo = jnp.minimum(lo, span[2 * i])
        hi = jnp.maximum(hi, span[2 * i + 1])
    return lo, hi


def each_block(me, lo, hi, near, far, do):
    for is_far, ref in ((0, near), (1, far)):
        for slot in range(ref.shape[0]):
            kb = jnp.bitwise_xor(me, 2 * slot + is_far)
            pl.when((kb >= lo) & (kb < hi))(functools.partial(do, slot, is_far, kb))


def forward_kernel(
    span, qt_ref, near_ref, far_ref, info_ref, x_ref, wo_ref, gain_ref,
    mixed_ref, out_t_ref, lse_ref, hidden_ref, n2_ref,
    k_s, vt_s, qbd_s, acc_s, m_s, l_s, bias_s,
):
    kb_size = near_ref.shape[2]
    tiles = qt_ref.shape[1] // TILE
    lo, hi = key_range(span, tiles)

    def prepare(slot, is_far, kb):
        fac = (far_ref if is_far else near_ref)[slot].astype(F32)
        for quad in range(QUADS):
            rows = slice(quad * QW, (quad + 1) * QW)
            k_s[kb, :, rows] = materialize_quad(fac, 0, quad).T
            vt_s[kb, rows, :] = materialize_quad(fac, MIX + BASE, quad)

    each_block(span[2 * tiles], lo, hi, near_ref, far_ref, prepare)
    qbd_s[...] = jnp.zeros_like(qbd_s)

    for tile in range(tiles):
        lanes = slice(tile * TILE, (tile + 1) * TILE)
        for h in range(HEADS):
            quad, i = h // QUAD, h % QUAD
            qbd_s[quad, i * HEAD_DIM : (i + 1) * HEAD_DIM, i * TILE : (i + 1) * TILE] = qt_ref[
                h * HEAD_DIM : (h + 1) * HEAD_DIM, lanes
            ]
        m_s[...] = jnp.full_like(m_s, NEG)
        l_s[...] = jnp.zeros_like(l_s)
        acc_s[...] = jnp.zeros_like(acc_s)
        first = info_ref[0:1, lanes]
        last = info_ref[1:2, lanes]

        def step(kb, _):
            places = kb * kb_size + lax.broadcasted_iota(jnp.int32, (kb_size, TILE), 0)
            bias_s[...] = jnp.where((places >= first) & (places <= last), 0.0, NEG)
            for quad in range(QUADS):
                s = mm(k_s[kb, :, quad * QW : (quad + 1) * QW], qbd_s[quad])
                ps = []
                alphas = []
                for i in range(QUAD):
                    h = quad * QUAD + i
                    sh = s[:, i * TILE : (i + 1) * TILE] + bias_s[...]
                    old = m_s[h : h + 1, :]
                    new = jnp.maximum(old, jnp.max(sh, axis=0, keepdims=True))
                    alpha = jnp.exp(old - new)
                    p = jnp.exp(sh - new)
                    m_s[h : h + 1, :] = new
                    l_s[h : h + 1, :] = l_s[h : h + 1, :] * alpha + jnp.sum(
                        p, axis=0, keepdims=True
                    )
                    ps.append(p.astype(BF16))
                    alphas.append(alpha)
                for j in range(QUAD // 2):
                    both = jnp.concatenate(ps[2 * j : 2 * j + 2], axis=1)
                    at = quad * QW + j * 2 * HEAD_DIM
                    o = mm(vt_s[kb, at : at + 2 * HEAD_DIM, :], both)
                    for i in range(2):
                        r = slice(at + i * HEAD_DIM, at + (i + 1) * HEAD_DIM)
                        acc_s[r, :] = (
                            acc_s[r, :] * alphas[2 * j + i]
                            + o[i * HEAD_DIM : (i + 1) * HEAD_DIM, i * TILE : (i + 1) * TILE]
                        )
            return 0

        lax.fori_loop(span[2 * tile], span[2 * tile + 1], step, 0)
        lse_ref[:, lanes] = m_s[...] + jnp.log(l_s[...])
        for h in range(HEADS):
            rows = slice(h * HEAD_DIM, (h + 1) * HEAD_DIM)
            out_t_ref[rows, lanes] = acc_s[rows, :] * (1.0 / l_s[h : h + 1, :])

    mixed = out_t_ref[...].astype(BF16).T
    mixed_ref[...] = mixed
    hidden = x_ref[...].astype(F32) + mm(mixed, wo_ref[...])
    hidden_ref[...] = hidden
    scale = lax.rsqrt(jnp.mean(hidden * hidden, axis=-1, keepdims=True) + 1e-06)
    n2_ref[...] = (hidden * scale * gain_ref[...]).astype(BF16)


def attend_forward(span, qt, near, far, info, x, wo, gain):
    width, local = qt.shape
    kb = near.shape[2]
    blocks = near.shape[0] + far.shape[0]
    d = x.shape[1]
    return kernel_call(
        forward_kernel,
        "attend_forward",
        (
            ((local, width), BF16),
            ((width, local), F32),
            ((HEADS, local), F32),
            ((local, d), F32),
            ((local, d), BF16),
        ),
        [
            pltpu.VMEM((blocks, kb, width), BF16),
            pltpu.VMEM((blocks, width, kb), BF16),
            pltpu.VMEM((QUADS, QW, QUAD * TILE), BF16),
            pltpu.VMEM((width, TILE), F32),
            pltpu.VMEM((HEADS, TILE), F32),
            pltpu.VMEM((HEADS, TILE), F32),
            pltpu.VMEM((kb, TILE), F32),
        ],
        1,
        40,
        span, qt, near, far, info, x, wo, gain,
    )


def ffn_kernel(first, *refs):
    n2n, n2f, upn, upf, own_ref, other_ref = refs[:6]
    prev = () if first else refs[6:12]
    (bn, bf, sn, sf, down_own, gate_own, lift_own, down_other, gate_other, lift_other, w_s) = refs[
        6 + len(prev) :
    ]
    hid = own_ref.shape[1]
    half = n2n.shape[0]
    w_s[:, :hid, :] = own_ref[...]
    w_s[:, hid:, :] = other_ref[...]
    n2 = jnp.concatenate([n2n[...], n2f[...]], axis=0)
    up = jnp.concatenate([upn[...], upf[...]], axis=0)
    gate = mm_nt(n2, w_s[0])
    lifted = mm_nt(n2, w_s[1])
    hidden_grad = mm_nt(up, w_s[2])
    sigmoid = jax.nn.sigmoid(gate)
    silu = gate * sigmoid
    act = (silu * lifted).astype(BF16)
    gate_grad = (hidden_grad * lifted * (sigmoid * (1.0 + gate * (1.0 - sigmoid)))).astype(BF16)
    lift_grad = (hidden_grad * silu).astype(BF16)
    sng = (mm(gate_grad, w_s[0]) + mm(lift_grad, w_s[1])).astype(BF16)
    sn[...] = sng[:half]
    sf[...] = sng[half:]
    branch = mm(act, w_s[2]).astype(BF16)
    bn[...] = branch[:half]
    bf[...] = branch[half:]
    for at, (left, right, own, other) in enumerate(
        (
            (act, up, down_own, down_other),
            (gate_grad, n2, gate_own, gate_other),
            (lift_grad, n2, lift_own, lift_other),
        )
    ):
        grad = mm_tn(left, right)
        mine, theirs = grad[:hid], grad[hid:]
        if not first:
            mine = mine + prev[at][...]
            theirs = theirs + prev[3 + at][...]
        own[...] = mine
        other[...] = theirs.astype(other.dtype)


def feed_forward(n2n, n2f, upn, upf, own, other, prev):
    half, d = n2n.shape
    hid = own.shape[1]
    first = not prev
    return kernel_call(
        functools.partial(ffn_kernel, first),
        "feed_forward",
        tuple([((half, d), BF16)] * 4)
        + tuple([((hid, d), F32)] * 3)
        + tuple([((hid, d), F32 if first else BF16)] * 3),
        [pltpu.VMEM((3, 2 * hid, d), BF16)],
        0,
        62,
        n2n, n2f, upn, upf, own, other, *prev,
    )


def residual_kernel(
    sa, sb, up_ref, hidden_ref, gain_ref, wo_ref, out_t_ref,
    res_ref, low_ref, dot_ref, delta_ref, gain_out,
):
    sng = sa[...].astype(F32) + sb[...].astype(F32)
    hidden = hidden_ref[...]
    scale = lax.rsqrt(jnp.mean(hidden * hidden, axis=-1, keepdims=True) + 1e-06)
    gain_out[...] = jnp.sum(sng * (hidden * scale), axis=0, keepdims=True)
    weighted = sng * gain_ref[...]
    inner = jnp.mean(hidden * weighted, axis=-1, keepdims=True)
    res = up_ref[...].astype(F32) + scale * weighted - hidden * (scale * scale * scale) * inner
    res_ref[...] = res
    low = res.astype(BF16)
    low_ref[...] = low
    dot = mm_nt(wo_ref[...], low).astype(BF16)
    dot_ref[...] = dot
    for h in range(HEADS):
        rows = slice(h * HEAD_DIM, (h + 1) * HEAD_DIM)
        delta_ref[h : h + 1, :] = jnp.sum(
            dot[rows].astype(F32) * out_t_ref[rows, :], axis=0, keepdims=True
        )


def residual(sa, sb, up, hidden, gain, wo, out_t):
    local, d = hidden.shape
    width = out_t.shape[0]
    return kernel_call(
        residual_kernel,
        "residual",
        (
            ((local, d), F32),
            ((local, d), BF16),
            ((width, local), BF16),
            ((HEADS, local), F32),
            ((1, d), F32),
        ),
        [],
        0,
        30,
        sa, sb, up, hidden, gain, wo, out_t,
    )


def backward_kernel(
    span, qt_ref, near_ref, far_ref, info_ref, dot_ref, lse_ref, delta_ref, qmix_ref, qbase_ref,
    cos_ref, sin_ref,
    dnear_ref, dfar_ref, dq_ref,
    k_s, kt_s, vt_s, dkt_s, dvt_s, qbd_s, qbdt_s, obd_s, obdt_s, dq_s, bias_s, lse_s, delta_s,
):
    kb_size = near_ref.shape[2]
    tiles = qt_ref.shape[1] // TILE
    lo, hi = key_range(span, tiles)
    me = span[2 * tiles]
    dnear_ref[...] = jnp.zeros_like(dnear_ref)
    dfar_ref[...] = jnp.zeros_like(dfar_ref)

    def prepare(slot, is_far, kb):
        fac = (far_ref if is_far else near_ref)[slot].astype(F32)
        for quad in range(QUADS):
            rows = slice(quad * QW, (quad + 1) * QW)
            kt = materialize_quad(fac, 0, quad)
            kt_s[kb, rows, :] = kt
            k_s[kb, :, rows] = kt.T
            vt_s[kb, rows, :] = materialize_quad(fac, MIX + BASE, quad)
            dkt_s[kb, rows, :] = jnp.zeros((QW, kb_size), F32)
            dvt_s[kb, rows, :] = jnp.zeros((QW, kb_size), F32)

    each_block(me, lo, hi, near_ref, far_ref, prepare)
    qbdt_s[...] = jnp.zeros_like(qbdt_s)
    obdt_s[...] = jnp.zeros_like(obdt_s)

    for tile in range(tiles):
        lanes = slice(tile * TILE, (tile + 1) * TILE)
        for h in range(HEADS):
            quad, i = h // QUAD, h % QUAD
            a = slice(i * HEAD_DIM, (i + 1) * HEAD_DIM)
            b = slice(i * TILE, (i + 1) * TILE)
            rows = slice(h * HEAD_DIM, (h + 1) * HEAD_DIM)
            qbdt_s[quad, a, b] = qt_ref[rows, lanes]
            obdt_s[quad, a, b] = dot_ref[rows, lanes]
        for quad in range(QUADS):
            qbd_s[quad] = qbdt_s[quad].T
            obd_s[quad] = obdt_s[quad].T
        lse_t = lse_ref[:, lanes].T
        delta_t = delta_ref[:, lanes].T
        for h in range(HEADS):
            lse_s[h] = jnp.broadcast_to(lse_t[:, h : h + 1], (TILE, TILE))
            delta_s[h] = jnp.broadcast_to(delta_t[:, h : h + 1], (TILE, TILE))
        dq_s[...] = jnp.zeros_like(dq_s)
        info_t = info_ref[:, lanes].T
        first = info_t[:, 0:1]
        last = info_t[:, 1:2]

        def step(kb, _):
            places = kb * kb_size + lax.broadcasted_iota(jnp.int32, (TILE, kb_size), 1)
            bias_s[...] = jnp.where((places >= first) & (places <= last), 0.0, NEG)
            lane = lax.broadcasted_iota(jnp.int32, (TILE, QW), 1) // HEAD_DIM
            for quad in range(QUADS):
                rows = slice(quad * QW, (quad + 1) * QW)
                s = mm(qbd_s[quad], kt_s[kb, rows, :])
                dp = mm(obd_s[quad], vt_s[kb, rows, :])
                ps = []
                dss = []
                for i in range(QUAD):
                    h = quad * QUAD + i
                    b = slice(i * TILE, (i + 1) * TILE)
                    lse = jnp.concatenate([lse_s[h]] * (kb_size // TILE), axis=1)
                    delta = jnp.concatenate([delta_s[h]] * (kb_size // TILE), axis=1)
                    p = jnp.exp((s[b] + bias_s[...]) - lse)
                    ps.append(p.astype(BF16))
                    dss.append((p * (dp[b] - delta)).astype(BF16))
                p4 = jnp.concatenate(ps, axis=0)
                ds4 = jnp.concatenate(dss, axis=0)
                dkt_s[kb, rows, :] += mm(qbdt_s[quad], ds4)
                dvt_s[kb, rows, :] += mm(obdt_s[quad], p4)
                dq = mm(ds4, k_s[kb, :, rows])
                out = dq[0:TILE]
                for i in range(1, QUAD):
                    out = jnp.where(lane == i, dq[i * TILE : (i + 1) * TILE], out)
                dq_s[:, rows] += out
            return 0

        lax.fori_loop(span[2 * tile], span[2 * tile + 1], step, 0)
        dqt = dq_s[...].T * (HEAD_DIM ** -0.5 / Q_RANK)
        qmix = qmix_ref[:, lanes]
        for h in range(HEADS):
            part = dqt[h * HEAD_DIM : (h + 1) * HEAD_DIM, :]
            dq_ref[h * Q_RANK : (h + 1) * Q_RANK, lanes] = jnp.concatenate(
                [
                    jnp.sum(
                        part * qbase_ref[r * HEAD_DIM : (r + 1) * HEAD_DIM, lanes],
                        axis=0,
                        keepdims=True,
                    )
                    for r in range(Q_RANK)
                ],
                axis=0,
            )
        cos = cos_ref[:, lanes]
        sin = sin_ref[:, lanes]
        for r in range(Q_RANK):
            out = None
            for h in range(HEADS):
                row = h * Q_RANK + r
                part = qmix[row : row + 1, :] * dqt[h * HEAD_DIM : (h + 1) * HEAD_DIM, :]
                out = part if out is None else out + part
            a, b = out[:HALF], out[HALF:]
            at = QMIX + r * HEAD_DIM
            dq_ref[at : at + HALF, lanes] = a * cos + b * sin
            dq_ref[at + HALF : at + HEAD_DIM, lanes] = b * cos - a * sin

    def fold(slot, is_far, kb):
        fac = (far_ref if is_far else near_ref)[slot].astype(F32)
        to = dfar_ref if is_far else dnear_ref
        for offset, grad in ((0, dkt_s), (MIX + BASE, dvt_s)):
            outs = [None] * KV_RANK
            mixes = []
            for h in range(HEADS):
                g = grad[kb, h * HEAD_DIM : (h + 1) * HEAD_DIM, :] * (1.0 / KV_RANK)
                for r in range(KV_RANK):
                    at = offset + MIX + r * HEAD_DIM
                    mixes.append(jnp.sum(g * fac[at : at + HEAD_DIM, :], axis=0, keepdims=True))
                    row = offset + h * KV_RANK + r
                    part = fac[row : row + 1, :] * g
                    outs[r] = part if outs[r] is None else outs[r] + part
            to[slot, offset : offset + MIX, :] = jnp.concatenate(mixes, axis=0).astype(BF16)
            for r in range(KV_RANK):
                at = offset + MIX + r * HEAD_DIM
                to[slot, at : at + HEAD_DIM, :] = outs[r].astype(BF16)

    each_block(me, lo, hi, near_ref, far_ref, fold)


def attend_backward(span, qt, near, far, info, dot, lse, delta, qmix, qbase, cos, sin):
    width, local = qt.shape
    kb = near.shape[2]
    blocks = near.shape[0] + far.shape[0]
    return kernel_call(
        backward_kernel,
        "attend_backward",
        (
            (near.shape, BF16),
            (far.shape, BF16),
            ((QMIX + QBASE, local), F32),
        ),
        [
            pltpu.VMEM((blocks, kb, width), BF16),
            pltpu.VMEM((blocks, width, kb), BF16),
            pltpu.VMEM((blocks, width, kb), BF16),
            pltpu.VMEM((blocks, width, kb), F32),
            pltpu.VMEM((blocks, width, kb), F32),
            pltpu.VMEM((QUADS, QUAD * TILE, QW), BF16),
            pltpu.VMEM((QUADS, QW, QUAD * TILE), BF16),
            pltpu.VMEM((QUADS, QUAD * TILE, QW), BF16),
            pltpu.VMEM((QUADS, QW, QUAD * TILE), BF16),
            pltpu.VMEM((TILE, width), F32),
            pltpu.VMEM((TILE, kb), F32),
            pltpu.VMEM((HEADS, TILE, TILE), F32),
            pltpu.VMEM((HEADS, TILE, TILE), F32),
        ],
        1,
        52,
        span, qt, near, far, info, dot, lse, delta, qmix, qbase, cos, sin,
    )


def finish_kernel(
    fa, f1, f2, f3, dq_ref, cos_ref, sin_ref, x_ref, gain_ref, wt_ref, res_ref,
    low_ref, grad_ref, gain_out,
):
    total = (fa[...].astype(F32) + f1[...].astype(F32)) + (
        f2[...].astype(F32) + f3[...].astype(F32)
    )
    cos = cos_ref[...]
    sin = sin_ref[...]
    query = QMIX + QBASE
    low_ref[:query, :] = dq_ref[...].astype(BF16)
    low_ref[query:, :] = total.astype(BF16)
    for r in range(KV_RANK):
        at = MIX + r * HEAD_DIM
        a, b = total[at : at + HALF], total[at + HALF : at + HEAD_DIM]
        to = query + at
        low_ref[to : to + HALF, :] = (a * cos + b * sin).astype(BF16)
        low_ref[to + HALF : to + HEAD_DIM, :] = (b * cos - a * sin).astype(BF16)
    grad = mm_tn(low_ref[...], wt_ref[...])
    x = x_ref[...].astype(F32)
    scale = lax.rsqrt(jnp.mean(x * x, axis=-1, keepdims=True) + 1e-06)
    gain_out[...] = jnp.sum(grad * (x * scale), axis=0, keepdims=True)
    weighted = grad * gain_ref[...]
    inner = jnp.mean(x * weighted, axis=-1, keepdims=True)
    grad_ref[...] = res_ref[...] + (scale * weighted - x * (scale * scale * scale) * inner)


def finish(pieces, dq, cos, sin, x, gain, wt, res):
    local, d = x.shape
    return kernel_call(
        finish_kernel,
        "finish",
        (
            ((QMIX + QBASE + FACTORS, local), BF16),
            ((local, d), F32),
            ((1, d), F32),
        ),
        [],
        0,
        30,
        *pieces, dq, cos, sin, x, gain, wt, res,
    )


def share_kernel(me, low0, low1, n0, n1, g0, g1, h0, h1, near_ref, far_ref, all_s):
    rows = low0.shape[0]
    all_s[:rows, :] = mm(
        jnp.concatenate([low0[...], low1[...]], axis=1), jnp.concatenate([n0[...], n1[...]], axis=0)
    )
    all_s[rows:, :] = jnp.concatenate(
        [g0[...] + g1[...], h0[...] + h1[...], jnp.zeros((14, g0.shape[1]), F32)], axis=0
    )
    width = near_ref.shape[2]
    for is_far, ref in ((0, near_ref), (1, far_ref)):
        for slot in range(ref.shape[0]):
            at = pl.multiple_of(jnp.bitwise_xor(me[0], 2 * slot + is_far) * width, width)
            ref[slot] = all_s[:, pl.ds(at, width)].astype(BF16)


def share(me, lows, normeds, first_gains, second_gains, slots):
    rows = lows[0].shape[0] + 16
    d = normeds[0].shape[1]
    return kernel_call(
        share_kernel,
        "share",
        (((slots // 2, rows, d // slots), BF16),) * 2,
        [pltpu.VMEM((rows, d), F32)],
        1,
        30,
        me, *lows, *normeds, *first_gains, *second_gains,
    )


highest = lax.Precision.HIGHEST
masked_score = -1e30


def rms_scale(values):
    return lax.rsqrt(jnp.mean(values * values, axis=-1, keepdims=True) + 1e-06)


def norm_backward(values, gain, scaled, upstream):
    weighted = upstream * gain
    inner = jnp.mean(values * weighted, axis=-1, keepdims=True)
    return scaled * weighted - values * (scaled * scaled * scaled) * inner


def rotate(values, cosine, sine):
    half = values.shape[-1] // 2
    first = values[..., :half]
    second = values[..., half:]
    return jnp.concatenate(
        [first * cosine - second * sine, first * sine + second * cosine], axis=-1
    )


def row_layout(lengths_row, places):
    ends = jnp.cumsum(lengths_row)
    passed = ends[None, :] <= places[:, None]
    segment = jnp.sum(passed.astype(jnp.int32), axis=1)
    start = jnp.max(jnp.where(passed, ends[None, :], 0), axis=1)
    valid = places < ends[-1]
    return (segment, places - start, valid)


def rope_tables(position):
    half = HEAD_DIM // 2
    frequency = 10000.0 ** (-jnp.arange(half, dtype=jnp.float32) / half)
    angle = position.astype(jnp.float32)[..., None] * frequency
    return (jnp.cos(angle), jnp.sin(angle))


def split_factors(factors):
    mix_width = HEADS * KV_RANK
    base_width = KV_RANK * HEAD_DIM
    count, rows = (factors.shape[0], factors.shape[1])
    key_mix = factors[..., :mix_width].reshape(count, rows, HEADS, KV_RANK)
    key_base = factors[..., mix_width : mix_width + base_width].reshape(
        count, rows, KV_RANK, HEAD_DIM
    )
    value_mix = factors[..., mix_width + base_width : 2 * mix_width + base_width].reshape(
        count, rows, HEADS, KV_RANK
    )
    value_base = factors[..., 2 * mix_width + base_width :].reshape(count, rows, KV_RANK, HEAD_DIM)
    return (key_mix, key_base, value_mix, value_base)


def pair_gradient(hidden_grad, gate, lifted):
    sigmoid = jax.nn.sigmoid(gate)
    gate_grad = hidden_grad * lifted * (sigmoid * (1.0 + gate * (1.0 - sigmoid)))
    lift_grad = hidden_grad * (gate * sigmoid)
    return jnp.concatenate([gate_grad, lift_grad], axis=-1).astype(jnp.bfloat16)


def general_body(
    tokens,
    lengths,
    cotangent,
    first_gain,
    query_heads,
    query_basis,
    key_heads,
    key_basis,
    value_heads,
    value_basis,
    output_weight,
    second_gain,
    gate_weight,
    up_weight,
    down_projection_weight,
):
    local, batch_rows, width = tokens.shape
    total = local * lax.axis_size("wide")
    offset = lax.axis_index("wide") * local
    places = jnp.arange(total, dtype=jnp.int32)
    segment, position, valid = jax.vmap(row_layout, in_axes=(0, None))(lengths, places)
    own_places = offset + jnp.arange(local, dtype=jnp.int32)
    own_segment = lax.dynamic_slice_in_dim(segment, offset, local, 1)
    own_position = lax.dynamic_slice_in_dim(position, offset, local, 1)
    own_valid = lax.dynamic_slice_in_dim(valid, offset, local, 1)
    cosine, sine = rope_tables(jnp.transpose(own_position))
    cosine = cosine[:, :, None, :]
    sine = sine[:, :, None, :]
    keep_rows = jnp.transpose(own_valid)[:, :, None]
    scale = HEAD_DIM ** (-0.5)
    block_rows = min(512, total)
    block_count = total // block_rows
    mix_width = HEADS * KV_RANK
    base_width = KV_RANK * HEAD_DIM
    flat_rows = local * batch_rows
    inputs = tokens.astype(jnp.float32)
    first_scale = rms_scale(inputs)
    normed = (inputs * first_scale * first_gain).astype(jnp.bfloat16)
    flat = normed.reshape(flat_rows, width)
    query_mix = jnp.dot(flat, query_heads, preferred_element_type=jnp.float32).reshape(
        local, batch_rows, HEADS, Q_RANK
    )
    query_raw = jnp.dot(flat, query_basis, preferred_element_type=jnp.float32).reshape(
        local, batch_rows, Q_RANK, HEAD_DIM
    )
    query_base = rotate(query_raw, cosine, sine)
    factor_weight = jnp.concatenate([key_heads, key_basis, value_heads, value_basis], axis=1)
    factor_raw = jnp.dot(flat, factor_weight, preferred_element_type=jnp.float32).reshape(
        local, batch_rows, -1
    )
    key_roped = rotate(
        factor_raw[..., mix_width : mix_width + base_width].reshape(
            local, batch_rows, KV_RANK, HEAD_DIM
        ),
        cosine,
        sine,
    ).reshape(local, batch_rows, base_width)
    factors = jnp.concatenate(
        [factor_raw[..., :mix_width], key_roped, factor_raw[..., mix_width + base_width :]], axis=-1
    ).astype(jnp.bfloat16)
    every = lax.all_gather(factors, "wide", axis=0, tiled=True)
    key_mix, key_base, value_mix, value_base = split_factors(every)
    keys = (
        jnp.einsum("trhk,trkd->trhd", key_mix, key_base, preferred_element_type=jnp.float32)
        / KV_RANK
    ).astype(jnp.bfloat16)
    values = (
        jnp.einsum("trhk,trkd->trhd", value_mix, value_base, preferred_element_type=jnp.float32)
        / KV_RANK
    ).astype(jnp.bfloat16)
    query = (
        jnp.einsum(
            "trhk,trkd->trhd",
            query_mix,
            query_base,
            precision=highest,
            preferred_element_type=jnp.float32,
        )
        / Q_RANK
    ).astype(jnp.bfloat16)

    def block_view(block):
        start = block * block_rows
        key_places = start + jnp.arange(block_rows, dtype=jnp.int32)
        key_segment = lax.dynamic_slice_in_dim(segment, start, block_rows, 1)
        key_valid = lax.dynamic_slice_in_dim(valid, start, block_rows, 1)
        causal = key_places[None, :] <= own_places[:, None]
        itself = key_places[None, :] == own_places[:, None]
        allowed = (
            causal[None]
            & (own_segment[:, :, None] == key_segment[:, None, :])
            & (key_valid[:, None, :] | itself[None])
        )
        key_block = lax.dynamic_slice_in_dim(keys, start, block_rows, 0)
        value_block = lax.dynamic_slice_in_dim(values, start, block_rows, 0)
        product = (
            jnp.einsum("qrhd,krhd->rhqk", query, key_block, preferred_element_type=jnp.float32)
            * scale
        )
        scores = jnp.where(allowed[:, None], product, masked_score)
        return (start, scores, key_block, value_block)

    def max_step(carry, block):
        top, mass = carry
        scores = block_view(block)[1]
        higher = jnp.maximum(top, jnp.max(scores, axis=-1))
        mass = mass * jnp.exp(top - higher) + jnp.sum(jnp.exp(scores - higher[..., None]), axis=-1)
        return ((higher, mass), None)

    start_top = jnp.full((batch_rows, HEADS, local), masked_score, jnp.float32)
    (top, mass), _ = lax.scan(
        max_step, (start_top, jnp.zeros_like(start_top)), jnp.arange(block_count)
    )
    log_total = top + jnp.log(mass)

    def out_step(carry, block):
        _, scores, _, value_block = block_view(block)
        chances = jnp.exp(scores - log_total[..., None]).astype(jnp.bfloat16)
        return (
            carry
            + jnp.einsum(
                "rhqk,krhd->qrhd", chances, value_block, preferred_element_type=jnp.float32
            ),
            None,
        )

    attended, _ = lax.scan(
        out_step,
        jnp.zeros((local, batch_rows, HEADS, HEAD_DIM), jnp.float32),
        jnp.arange(block_count),
    )
    mixed = attended.astype(jnp.bfloat16).reshape(flat_rows, HEADS * HEAD_DIM)
    hidden_state = inputs + jnp.dot(
        mixed, output_weight, preferred_element_type=jnp.float32
    ).reshape(local, batch_rows, width)
    second_scale = rms_scale(hidden_state)
    normed_second = (hidden_state * second_scale * second_gain).astype(jnp.bfloat16)
    normalized_token_rows = lax.all_gather(normed_second, "wide", axis=0, tiled=True)
    gate_lifted_hidden = jnp.concatenate([gate_weight, up_weight], axis=1)
    hidden_width = gate_weight.shape[1]
    projected_output = jnp.einsum(
        "zec,cx->zex", normalized_token_rows, gate_lifted_hidden, preferred_element_type=jnp.float32
    )
    gate = projected_output[..., :hidden_width]
    lifted = projected_output[..., hidden_width:]
    silu_hidden_output = (jax.nn.silu(gate) * lifted).astype(jnp.bfloat16)
    sequence_portion = silu_hidden_output
    branch = lax.psum_scatter(
        jnp.einsum(
            "zyu,uv->zyv",
            sequence_portion,
            down_projection_weight,
            preferred_element_type=jnp.float32,
        ).astype(jnp.bfloat16),
        "wide",
        scatter_dimension=0,
        tiled=True,
    ).astype(jnp.float32)
    output = jnp.where(keep_rows, hidden_state + branch, 0.0).astype(jnp.bfloat16)
    upstream = jnp.where(keep_rows, cotangent.astype(jnp.float32), 0.0)
    upstream_low = upstream.astype(jnp.bfloat16)
    upstream_token_gradient = lax.all_gather(upstream_low, "wide", axis=0, tiled=True)
    hidden_grad = jnp.einsum(
        "ajg,vg->ajv",
        upstream_token_gradient,
        down_projection_weight,
        preferred_element_type=jnp.float32,
    )
    pair_product_gradient = pair_gradient(hidden_grad, gate, lifted)
    down_gradient = jnp.einsum(
        "imj,ima->ja",
        silu_hidden_output,
        upstream_token_gradient,
        preferred_element_type=jnp.float32,
    )
    pair_weight_grad = jnp.einsum(
        "ipl,ipj->lj",
        normalized_token_rows,
        pair_product_gradient,
        preferred_element_type=jnp.float32,
    )
    sequence_portion = pair_product_gradient
    second_normed_grad = lax.psum_scatter(
        jnp.einsum(
            "ivu,bu->ivb", sequence_portion, gate_lifted_hidden, preferred_element_type=jnp.float32
        ),
        "wide",
        scatter_dimension=0,
        tiled=True,
    )
    second_gain_partial = jnp.sum(second_normed_grad * (hidden_state * second_scale), axis=(0, 1))
    residual_grad = upstream + norm_backward(
        hidden_state, second_gain, second_scale, second_normed_grad
    )
    residual_low = residual_grad.astype(jnp.bfloat16).reshape(flat_rows, width)
    output_weight_grad = jnp.einsum(
        "tk,td->kd", mixed, residual_low, preferred_element_type=jnp.float32
    )
    mixed_grad = (
        jnp.einsum("td,kd->tk", residual_low, output_weight, preferred_element_type=jnp.float32)
        .astype(jnp.bfloat16)
        .reshape(local, batch_rows, HEADS, HEAD_DIM)
    )

    def delta_step(carry, block):
        _, scores, _, value_block = block_view(block)
        chances = jnp.exp(scores - log_total[..., None])
        pressure = jnp.einsum(
            "qrhd,krhd->rhqk", mixed_grad, value_block, preferred_element_type=jnp.float32
        )
        return (carry + jnp.sum(chances * pressure, axis=-1), None)

    delta, _ = lax.scan(
        delta_step, jnp.zeros((batch_rows, HEADS, local), jnp.float32), jnp.arange(block_count)
    )

    def grad_step(carry, block):
        start, scores, key_block, value_block = block_view(block)
        chances = jnp.exp(scores - log_total[..., None])
        pressure = jnp.einsum(
            "qrhd,krhd->rhqk", mixed_grad, value_block, preferred_element_type=jnp.float32
        )
        score_grad = (chances * (pressure - delta[..., None])).astype(jnp.bfloat16)
        carry = (
            carry
            + jnp.einsum(
                "rhqk,krhd->qrhd", score_grad, key_block, preferred_element_type=jnp.float32
            )
            * scale
        )
        key_grad = (
            jnp.einsum("rhqk,qrhd->krhd", score_grad, query, preferred_element_type=jnp.float32)
            * scale
        )
        value_grad = jnp.einsum(
            "rhqk,qrhd->krhd",
            chances.astype(jnp.bfloat16),
            mixed_grad,
            preferred_element_type=jnp.float32,
        )
        block_mix, block_base, block_vmix, block_vbase = split_factors(
            lax.dynamic_slice_in_dim(every, start, block_rows, 0).astype(jnp.float32)
        )
        key_mix_grad = (
            jnp.einsum("krhd,krcd->krhc", key_grad, block_base, precision=highest) / KV_RANK
        )
        key_base_grad = (
            jnp.einsum("krhc,krhd->krcd", block_mix, key_grad, precision=highest) / KV_RANK
        )
        value_mix_grad = (
            jnp.einsum("krhd,krcd->krhc", value_grad, block_vbase, precision=highest) / KV_RANK
        )
        value_base_grad = (
            jnp.einsum("krhc,krhd->krcd", block_vmix, value_grad, precision=highest) / KV_RANK
        )
        block_grad = jnp.concatenate(
            [
                key_mix_grad.reshape(block_rows, batch_rows, mix_width),
                key_base_grad.reshape(block_rows, batch_rows, base_width),
                value_mix_grad.reshape(block_rows, batch_rows, mix_width),
                value_base_grad.reshape(block_rows, batch_rows, base_width),
            ],
            axis=-1,
        )
        return (carry, block_grad)

    query_grad, factor_blocks = lax.scan(
        grad_step,
        jnp.zeros((local, batch_rows, HEADS, HEAD_DIM), jnp.float32),
        jnp.arange(block_count),
    )
    factor_grads = factor_blocks.reshape(total, batch_rows, 2 * mix_width + 2 * base_width)
    own_factor_grads = lax.psum_scatter(
        factor_grads.astype(jnp.bfloat16), "wide", scatter_dimension=0, tiled=True
    ).astype(jnp.float32)
    key_base_back = rotate(
        own_factor_grads[..., mix_width : mix_width + base_width].reshape(
            local, batch_rows, KV_RANK, HEAD_DIM
        ),
        cosine,
        -sine,
    ).reshape(local, batch_rows, base_width)
    factor_low = (
        jnp.concatenate(
            [
                own_factor_grads[..., :mix_width],
                key_base_back,
                own_factor_grads[..., mix_width + base_width :],
            ],
            axis=-1,
        )
        .astype(jnp.bfloat16)
        .reshape(flat_rows, -1)
    )
    mix_grad = jnp.einsum("trhd,trcd->trhc", query_grad, query_base, precision=highest) / Q_RANK
    base_roped_grad = (
        jnp.einsum("trhc,trhd->trcd", query_mix, query_grad, precision=highest) / Q_RANK
    )
    base_grad = rotate(base_roped_grad, cosine, -sine)
    mix_low = mix_grad.astype(jnp.bfloat16).reshape(flat_rows, HEADS * Q_RANK)
    base_low = base_grad.astype(jnp.bfloat16).reshape(flat_rows, Q_RANK * HEAD_DIM)
    query_heads_grad = jnp.einsum("tk,tf->kf", flat, mix_low, preferred_element_type=jnp.float32)
    query_basis_grad = jnp.einsum("tk,tf->kf", flat, base_low, preferred_element_type=jnp.float32)
    factor_weight_grad = jnp.einsum(
        "tk,tf->kf", flat, factor_low, preferred_element_type=jnp.float32
    )
    first_normed_grad = (
        jnp.einsum("tf,kf->tk", mix_low, query_heads, preferred_element_type=jnp.float32)
        + jnp.einsum("tf,kf->tk", base_low, query_basis, preferred_element_type=jnp.float32)
        + jnp.einsum("tf,kf->tk", factor_low, factor_weight, preferred_element_type=jnp.float32)
    ).reshape(local, batch_rows, width)
    first_gain_partial = jnp.sum(first_normed_grad * (inputs * first_scale), axis=(0, 1))
    tokens_gradient = residual_grad + norm_backward(
        inputs, first_gain, first_scale, first_normed_grad
    )
    key_heads_grad = factor_weight_grad[:, :mix_width]
    key_basis_grad = factor_weight_grad[:, mix_width : mix_width + base_width]
    value_heads_grad = factor_weight_grad[:, mix_width + base_width : 2 * mix_width + base_width]
    value_basis_grad = factor_weight_grad[:, 2 * mix_width + base_width :]
    (
        first_share,
        qheads_share,
        qbasis_share,
        kheads_share,
        kbasis_share,
        vheads_share,
        vbasis_share,
        output_share,
        second_share,
    ) = (
        lax.psum_scatter(
            first_gain_partial.astype(jnp.bfloat16), "wide", scatter_dimension=0, tiled=True
        ).astype(jnp.float32),
        lax.psum_scatter(
            query_heads_grad.astype(jnp.bfloat16), "wide", scatter_dimension=0, tiled=True
        ).astype(jnp.float32),
        lax.psum_scatter(
            query_basis_grad.astype(jnp.bfloat16), "wide", scatter_dimension=0, tiled=True
        ).astype(jnp.float32),
        lax.psum_scatter(
            key_heads_grad.astype(jnp.bfloat16), "wide", scatter_dimension=0, tiled=True
        ).astype(jnp.float32),
        lax.psum_scatter(
            key_basis_grad.astype(jnp.bfloat16), "wide", scatter_dimension=0, tiled=True
        ).astype(jnp.float32),
        lax.psum_scatter(
            value_heads_grad.astype(jnp.bfloat16), "wide", scatter_dimension=0, tiled=True
        ).astype(jnp.float32),
        lax.psum_scatter(
            value_basis_grad.astype(jnp.bfloat16), "wide", scatter_dimension=0, tiled=True
        ).astype(jnp.float32),
        lax.psum_scatter(
            output_weight_grad.astype(jnp.bfloat16), "wide", scatter_dimension=0, tiled=True
        ).astype(jnp.float32),
        lax.psum_scatter(
            second_gain_partial.astype(jnp.bfloat16), "wide", scatter_dimension=0, tiled=True
        ).astype(jnp.float32),
    )
    gate_share = pair_weight_grad[:, :hidden_width]
    lift_share = pair_weight_grad[:, hidden_width:]
    totals = (
        lax.psum(first_share.astype(jnp.bfloat16), "batch").astype(jnp.float32),
        lax.psum(qheads_share.astype(jnp.bfloat16), "batch").astype(jnp.float32),
        lax.psum(qbasis_share.astype(jnp.bfloat16), "batch").astype(jnp.float32),
        lax.psum(kheads_share.astype(jnp.bfloat16), "batch").astype(jnp.float32),
        lax.psum(kbasis_share.astype(jnp.bfloat16), "batch").astype(jnp.float32),
        lax.psum(vheads_share.astype(jnp.bfloat16), "batch").astype(jnp.float32),
        lax.psum(vbasis_share.astype(jnp.bfloat16), "batch").astype(jnp.float32),
        lax.psum(output_share.astype(jnp.bfloat16), "batch").astype(jnp.float32),
        lax.psum(second_share.astype(jnp.bfloat16), "batch").astype(jnp.float32),
        lax.psum(gate_share.astype(jnp.bfloat16), "batch").astype(jnp.float32),
        lax.psum(lift_share.astype(jnp.bfloat16), "batch").astype(jnp.float32),
        lax.psum(down_gradient.astype(jnp.bfloat16), "batch").astype(jnp.float32),
    )
    return (
        output,
        tokens_gradient,
        totals[0],
        totals[1],
        totals[2],
        totals[3],
        totals[4],
        totals[5],
        totals[6],
        totals[7],
        totals[8],
        totals[9],
        totals[10],
        totals[11],
    )


def partners(distance, count):
    return [(i, i ^ distance) for i in range(count)]


def body(
    tokens,
    lengths,
    cotangent,
    first_gain,
    query_heads,
    query_basis,
    key_heads,
    key_basis,
    value_heads,
    value_basis,
    output_weight,
    second_gain,
    gate_weight,
    up_weight,
    down_projection_weight,
):
    local, rows, width = tokens.shape
    n = lax.axis_size("wide")
    depth = lax.axis_size("batch")
    total = local * n
    me = lax.axis_index("wide").astype(jnp.int32)
    offset = me * local

    def swap(value, distance):
        return lax.ppermute(value, "wide", partners(distance, n))

    core, across, along, diagonal = 1, 2, 4, 6
    chips = (across, along, diagonal)

    places = offset + jnp.arange(local, dtype=jnp.int32)
    ends = jnp.cumsum(lengths, axis=1)
    passed = ends[:, None, :] <= places[None, :, None]
    start = jnp.max(jnp.where(passed, ends[:, None, :], 0), axis=2)
    valid = places[None, :] < ends[:, -1:]
    position = places[None, :] - start
    first_seen = jnp.where(valid, start, places[None, :])
    frequency = 10000.0 ** (-jnp.arange(HALF, dtype=F32) / HALF)
    angle = position.astype(F32)[:, None, :] * frequency[None, :, None]
    cosine, sine = jnp.cos(angle), jnp.sin(angle)
    info = jnp.stack([first_seen, jnp.broadcast_to(places, (rows, local))], axis=1)
    info = jnp.concatenate([info, jnp.zeros((rows, 6, local), jnp.int32)], axis=1)
    tiles = local // TILE
    tile_lo = jnp.min(first_seen.reshape(rows, tiles, TILE), axis=2) // local
    tile_hi = places.reshape(tiles, TILE)[:, -1] // local + 1
    spans = jnp.stack([tile_lo, jnp.broadcast_to(tile_hi, (rows, tiles))], axis=2)
    spans = jnp.concatenate(
        [spans.reshape(rows, 2 * tiles), jnp.broadcast_to(me, (rows, 1))], axis=1
    ).astype(jnp.int32)

    gain1 = first_gain.reshape(1, width)
    gain2 = second_gain.reshape(1, width)
    projections = (query_heads, query_basis, key_heads, key_basis, value_heads, value_basis)

    xs = [tokens[:, b, :] for b in range(rows)]
    ups = [jnp.where(valid[b][:, None], cotangent[:, b, :], 0) for b in range(rows)]

    projected = []
    gathered = []
    for b in range(rows):
        fac, qt, qmix, qbase, normed = project(
            xs[b], gain1, projections, cosine[b], sine[b]
        )
        projected.append((qt, qmix, qbase, normed))
        near = jnp.stack([fac] + [swap(fac, distance) for distance in chips])
        gathered.append((near, swap(near, core)))

    def gather_rows(value):
        near = jnp.concatenate([value, swap(value, across)], axis=0)
        return near, swap(near, core)

    own_weights = jnp.stack([gate_weight.T, up_weight.T, down_projection_weight])
    other_weights = swap(own_weights, along)
    up_rows = [gather_rows(ups[b]) for b in range(rows)]

    attended = []
    second = []
    for b in range(rows):
        qt = projected[b][0]
        mixed, out_t, lse, hidden, n2 = attend_forward(
            spans[b], qt, *gathered[b], info[b], xs[b], output_weight, gain2
        )
        attended.append((mixed, out_t, lse, hidden))
        second.append(gather_rows(n2))

    def scatter_rows(near, far):
        summed = near.astype(F32) + swap(far, core).astype(F32)
        mine = summed[:local].astype(BF16)
        theirs = summed[local:].astype(BF16)
        return mine, swap(theirs, across)

    branches = []
    seconds = []
    prev = ()
    for b in range(rows):
        bn, bf, sn, sf, *prev = feed_forward(
            *second[b], *up_rows[b], own_weights, other_weights, tuple(prev)
        )
        seconds.append(scatter_rows(sn, sf))
        branches.append((bn, bf))

    residuals = []
    factor_parts = []
    query_lows = []
    for b in range(rows):
        mixed, out_t, lse, hidden = attended[b]
        qt, qmix, qbase, normed = projected[b]
        res, low, dot, delta, gain_share = residual(
            *seconds[b], ups[b], hidden, gain2, output_weight, out_t
        )
        residuals.append((res, low, gain_share))
        dnear, dfar, dq = attend_backward(
            spans[b], qt, *gathered[b], info[b], dot, lse, delta, qmix, qbase, cosine[b], sine[b]
        )
        query_lows.append(dq)
        summed = (dnear.astype(F32) + swap(dfar, core).astype(F32)).astype(BF16)
        factor_parts.append(
            [summed[0]] + [swap(summed[i + 1], chips[i]) for i in range(len(chips))]
        )

    outputs = []
    for b in range(rows):
        mine, other = scatter_rows(*branches[b])
        hidden = attended[b][3]
        branch = mine.astype(F32) + other.astype(F32)
        outputs.append(jnp.where(valid[b][:, None], hidden + branch, 0.0).astype(BF16))
    output = jnp.stack(outputs, axis=1)

    wt = jnp.concatenate(projections, axis=1).T
    lows = []
    token_grads = []
    gain_shares = []
    for b in range(rows):
        low, grad, gain_share = finish(
            factor_parts[b], query_lows[b], cosine[b], sine[b], xs[b], gain1, wt, residuals[b][0]
        )
        lows.append(low)
        token_grads.append(grad)
        gain_shares.append(gain_share)
    tokens_gradient = jnp.stack(token_grads, axis=1)

    def over_chips(near, far):
        summed = (near.astype(F32) + swap(far, core).astype(F32)).astype(BF16)
        result = summed[0].astype(F32)
        for i in range(len(chips)):
            result = result + swap(summed[i + 1], chips[i]).astype(F32)
        return result

    def over_batch(value):
        low = value.astype(BF16)
        result = low.astype(F32)
        for shift in range(1, depth):
            perm = [(i, (i + shift) % depth) for i in range(depth)]
            result = result + lax.ppermute(low, "batch", perm).astype(F32)
        return result

    def over_batch_split(value):
        low = value.astype(BF16)
        count = low.shape[0] // depth
        z = lax.axis_index("batch")
        pieces = low.reshape((depth, count) + low.shape[1:])
        part = lax.dynamic_index_in_dim(pieces, z, 0, keepdims=False).astype(F32)
        for shift in range(1, depth):
            perm = [(i, (i + shift) % depth) for i in range(depth)]
            to = lax.dynamic_index_in_dim(pieces, (z + shift) % depth, 0, keepdims=False)
            part = part + lax.ppermute(to, "batch", perm).astype(F32)
        part = part.astype(BF16)
        whole_sum = jnp.zeros_like(pieces)
        whole_sum = lax.dynamic_update_index_in_dim(whole_sum, part, z, 0)
        for shift in range(1, depth):
            perm = [(i, (i + shift) % depth) for i in range(depth)]
            got = lax.ppermute(part, "batch", perm)
            whole_sum = lax.dynamic_update_index_in_dim(
                whole_sum, got, (z - shift) % depth, 0
            )
        return whole_sum.reshape(low.shape).astype(F32)

    near, far = share(
        me.reshape(1),
        lows,
        [projected[b][3] for b in range(rows)],
        gain_shares,
        [residuals[b][2] for b in range(rows)],
        n,
    )
    small = over_batch(over_chips(near, far))
    count = width // n

    def pick(at, size):
        return small[at : at + size].T

    query_heads_grad = pick(0, QMIX)
    query_basis_grad = pick(QMIX, QBASE)
    at = QMIX + QBASE
    key_heads_grad = pick(at, MIX)
    key_basis_grad = pick(at + MIX, BASE)
    value_heads_grad = pick(at + MIX + BASE, MIX)
    value_basis_grad = pick(at + 2 * MIX + BASE, BASE)
    at = at + FACTORS
    first_gain_grad = small[at].reshape(count)
    second_gain_grad = small[at + 1].reshape(count)

    wo_grad = sum(
        lax.dot_general(
            attended[b][0],
            residuals[b][1],
            (((0,), (0,)), ((), ())),
            preferred_element_type=F32,
        )
        for b in range(rows)
    ).astype(BF16)
    slots = wo_grad.reshape(n, width // n, width)
    order = [me ^ (2 * i) for i in range(n // 2)]
    wo_near = jnp.stack([lax.dynamic_index_in_dim(slots, i, 0, keepdims=False) for i in order])
    wo_far = jnp.stack([lax.dynamic_index_in_dim(slots, i ^ 1, 0, keepdims=False) for i in order])
    output_weight_grad = over_batch(over_chips(wo_near, wo_far))

    block_grads = []
    for own, other in zip(prev[:3], prev[3:]):
        block_grads.append(over_batch_split(own + swap(other, along).astype(F32)))
    down_grad, gate_grad, lift_grad = block_grads

    return (
        output,
        tokens_gradient,
        first_gain_grad,
        query_heads_grad,
        query_basis_grad,
        key_heads_grad,
        key_basis_grad,
        value_heads_grad,
        value_basis_grad,
        output_weight_grad,
        second_gain_grad,
        gate_grad.T,
        lift_grad.T,
        down_grad,
    )


def solution(mesh):
    narrow = mesh.shape["wide"] == 8
    return jax.shard_map(
        body if narrow else general_body,
        mesh=mesh,
        in_specs=(
            P("wide", "batch", None),
            P("batch", None),
            P("wide", "batch", None),
            P(),
            P(),
            P(),
            P(),
            P(),
            P(),
            P(),
            P(),
            P(),
            P(None, "wide"),
            P(None, "wide"),
            P("wide", None),
        ),
        out_specs=(
            P("wide", "batch", None),
            P("wide", "batch", None),
            P("wide"),
            P("wide", None),
            P("wide", None),
            P("wide", None),
            P("wide", None),
            P("wide", None),
            P("wide", None),
            P("wide", None),
            P("wide"),
            P(None, "wide"),
            P(None, "wide"),
            P("wide", None),
        ),
        check_vma=False,
    )
```

```python
import functools

import jax
import jax.numpy as jnp
from jax import lax
from jax.experimental import pallas as pl
from jax.experimental.pallas import tpu as pltpu
from jax.sharding import PartitionSpec as P

HEADS = 16
HEAD_DIM = 64
Q_RANK = 6
KV_RANK = 2
HALF = HEAD_DIM // 2
MIX = HEADS * KV_RANK
BASE = KV_RANK * HEAD_DIM
FACTORS = 2 * MIX + 2 * BASE
QMIX = HEADS * Q_RANK
QBASE = Q_RANK * HEAD_DIM
QUAD = 4
QUADS = HEADS // QUAD
QW = QUAD * HEAD_DIM
TILE = 128
F32 = jnp.float32
BF16 = jnp.bfloat16
NEG = -1e30
MIB = 1 << 20


def mm(a, b):
    return jnp.dot(a, b, preferred_element_type=F32)


def mm_nt(a, b):
    return lax.dot_general(a, b, (((1,), (1,)), ((), ())), preferred_element_type=F32)


def mm_tn(a, b):
    return lax.dot_general(a, b, (((0,), (0,)), ((), ())), preferred_element_type=F32)


def whole(count):
    return [pl.BlockSpec(memory_space=pltpu.VMEM)] * count


def streamed(shape):
    return pl.BlockSpec(shape, lambda *_, rank=len(shape): (0,) * rank)


def kernel_call(
    kernel, name, outs, scratch, smem, limit, micros, *args, kept=(), far=(), aliases={}
):
    specs = [
        pl.BlockSpec(memory_space=pltpu.SMEM)
        if i < smem
        else streamed(arg.shape)
        if i in far
        else pl.BlockSpec(memory_space=pltpu.VMEM)
        for i, arg in enumerate(args)
    ]
    return pl.pallas_call(
        kernel,
        out_shape=tuple(
            pltpu.HBM(s, t) if i in kept else jax.ShapeDtypeStruct(s, t)
            for i, (s, t) in enumerate(outs)
        ),
        in_specs=specs,
        out_specs=[
            streamed(s) if i in kept else pl.BlockSpec(memory_space=pltpu.VMEM)
            for i, (s, _) in enumerate(outs)
        ],
        scratch_shapes=scratch,
        compiler_params=pltpu.CompilerParams(vmem_limit_bytes=limit * MIB),
        cost_estimate=pl.CostEstimate(
            flops=int(micros * 1e9), transcendentals=0, bytes_accessed=int(micros * 1e6)
        ),
        input_output_aliases=aliases,
        name=name,
    )(
        *(
            pltpu.with_memory_space_constraint(arg, pltpu.HBM) if i in far else arg
            for i, arg in enumerate(args)
        )
    )


def project_kernel(
    x_ref, gain_ref, qh_ref, qb_ref, kh_ref, kb_ref, vh_ref, vb_ref, cos_ref, sin_ref,
    fac_ref, qt_ref, qmix_ref, qbase_ref, normed_ref,
):
    x = x_ref[...].astype(F32)
    scale = lax.rsqrt(jnp.mean(x * x, axis=-1, keepdims=True) + 1e-06)
    normed = (x * scale * gain_ref[...]).astype(BF16)
    normed_ref[...] = normed
    cos = cos_ref[...]
    sin = sin_ref[...]

    def rope(v):
        a, b = v[:HALF], v[HALF:]
        return jnp.concatenate([a * cos - b * sin, a * sin + b * cos], axis=0)

    kb = mm(normed, kb_ref[...]).T
    fac_ref[0:MIX, :] = mm_nt(kh_ref[...], normed).astype(BF16)
    for r in range(KV_RANK):
        at = MIX + r * HEAD_DIM
        fac_ref[at : at + HEAD_DIM, :] = rope(kb[r * HEAD_DIM : (r + 1) * HEAD_DIM]).astype(BF16)
    fac_ref[MIX + BASE : 2 * MIX + BASE, :] = mm_nt(vh_ref[...], normed).astype(BF16)
    fac_ref[2 * MIX + BASE :, :] = mm(normed, vb_ref[...]).T.astype(BF16)
    qmix = mm_nt(qh_ref[...], normed)
    qmix_ref[...] = qmix
    raw = mm(normed, qb_ref[...]).T
    base = [rope(raw[r * HEAD_DIM : (r + 1) * HEAD_DIM]) for r in range(Q_RANK)]
    for r in range(Q_RANK):
        qbase_ref[r * HEAD_DIM : (r + 1) * HEAD_DIM, :] = base[r]
    for h in range(HEADS):
        out = None
        for r in range(Q_RANK):
            part = qmix[h * Q_RANK + r : h * Q_RANK + r + 1, :] * base[r]
            out = part if out is None else out + part
        qt_ref[h * HEAD_DIM : (h + 1) * HEAD_DIM, :] = (
            (out * (1.0 / Q_RANK)).astype(BF16) * (HEAD_DIM ** -0.5)
        ).astype(BF16)


def project(x, gain, weights, cos, sin):
    local, d = x.shape
    width = HEADS * HEAD_DIM
    return kernel_call(
        project_kernel,
        "project",
        (
            ((FACTORS, local), BF16),
            ((width, local), BF16),
            ((QMIX, local), F32),
            ((QBASE, local), F32),
            ((local, d), BF16),
        ),
        [],
        0,
        16,
        2,
        x, gain, *weights, cos, sin,
        kept=(1, 2, 3, 4),
    )


def materialize(fac, offset, head):
    base = offset + MIX
    out = None
    for r in range(KV_RANK):
        row = offset + head * KV_RANK + r
        part = fac[row : row + 1, :] * fac[base + r * HEAD_DIM : base + (r + 1) * HEAD_DIM, :]
        out = part if out is None else out + part
    return (out * (1.0 / KV_RANK)).astype(BF16)


def materialize_quad(fac, offset, quad):
    return jnp.concatenate(
        [materialize(fac, offset, quad * QUAD + i) for i in range(QUAD)], axis=0
    )


def each_block(me, lo, hi, slots, do):
    for slot in range(slots):
        kb = jnp.bitwise_xor(me, slot)
        pl.when((kb >= lo) & (kb < hi))(functools.partial(do, slot, kb))


def block_factors(slot, near, far):
    return (far if slot & 1 else near)[slot >> 1].astype(F32)


def forward_kernel(
    span, qt_ref, near_ref, far_ref, info_ref, x_ref, wo_ref, gain_ref,
    mixed_ref, out_t_ref, lse_ref, hidden_ref, n2_ref,
    k_s, vt_s, qbd_s, acc_s, m_s, l_s, bias_s,
):
    slots, kb_size, _ = k_s.shape
    count = qt_ref.shape[1]
    lo, hi, me = span[0], span[1], span[2]

    def prepare(slot, kb):
        fac = block_factors(slot, near_ref, far_ref)
        for quad in range(QUADS):
            rows = slice(quad * QW, (quad + 1) * QW)
            k_s[kb, :, rows] = materialize_quad(fac, 0, quad).T
            vt_s[kb, rows, :] = materialize_quad(fac, MIX + BASE, quad)

    each_block(me, lo, hi, slots, prepare)
    qbd_s[...] = jnp.zeros_like(qbd_s)
    for h in range(HEADS):
        quad, i = h // QUAD, h % QUAD
        qbd_s[quad, i * HEAD_DIM : (i + 1) * HEAD_DIM, i * count : (i + 1) * count] = qt_ref[
            h * HEAD_DIM : (h + 1) * HEAD_DIM, :
        ]
    m_s[...] = jnp.full_like(m_s, NEG)
    l_s[...] = jnp.zeros_like(l_s)
    acc_s[...] = jnp.zeros_like(acc_s)
    first = info_ref[0:1, :]
    last = info_ref[1:2, :]

    def step(kb, _):
        places = kb * kb_size + lax.broadcasted_iota(jnp.int32, (kb_size, count), 0)
        bias_s[...] = jnp.where((places >= first) & (places <= last), 0.0, NEG)
        for quad in range(QUADS):
            s = mm(k_s[kb, :, quad * QW : (quad + 1) * QW], qbd_s[quad])
            ps = []
            alphas = []
            for i in range(QUAD):
                h = quad * QUAD + i
                sh = s[:, i * count : (i + 1) * count] + bias_s[...]
                old = m_s[h : h + 1, :]
                new = jnp.maximum(old, jnp.max(sh, axis=0, keepdims=True))
                alpha = jnp.exp(old - new)
                p = jnp.exp(sh - new)
                m_s[h : h + 1, :] = new
                l_s[h : h + 1, :] = l_s[h : h + 1, :] * alpha + jnp.sum(p, axis=0, keepdims=True)
                ps.append(p.astype(BF16))
                alphas.append(alpha)
            for j in range(QUAD // 2):
                both = jnp.concatenate(ps[2 * j : 2 * j + 2], axis=1)
                at = quad * QW + j * 2 * HEAD_DIM
                o = mm(vt_s[kb, at : at + 2 * HEAD_DIM, :], both)
                for i in range(2):
                    r = slice(at + i * HEAD_DIM, at + (i + 1) * HEAD_DIM)
                    acc_s[r, :] = (
                        acc_s[r, :] * alphas[2 * j + i]
                        + o[i * HEAD_DIM : (i + 1) * HEAD_DIM, i * count : (i + 1) * count]
                    )
        return 0

    lax.fori_loop(lo, hi, step, 0)
    lse_ref[...] = m_s[...] + jnp.log(l_s[...])
    for h in range(HEADS):
        rows = slice(h * HEAD_DIM, (h + 1) * HEAD_DIM)
        out_t_ref[rows, :] = acc_s[rows, :] * (1.0 / l_s[h : h + 1, :])

    mixed = out_t_ref[...].astype(BF16).T
    mixed_ref[...] = mixed
    hidden = x_ref[...].astype(F32) + mm(mixed, wo_ref[...])
    hidden_ref[...] = hidden
    scale = lax.rsqrt(jnp.mean(hidden * hidden, axis=-1, keepdims=True) + 1e-06)
    n2_ref[...] = (hidden * scale * gain_ref[...]).astype(BF16)


def attend_forward(span, qt, near, far, info, x, wo, gain):
    width, local = qt.shape
    kb = local
    blocks = 2 * near.shape[0]
    d = x.shape[1]
    return kernel_call(
        forward_kernel,
        "attend_forward",
        (
            ((local, width), BF16),
            ((width, local), F32),
            ((HEADS, local), F32),
            ((local, d), F32),
            ((local, d), BF16),
        ),
        [
            pltpu.VMEM((blocks, kb, width), BF16),
            pltpu.VMEM((blocks, width, kb), BF16),
            pltpu.VMEM((QUADS, QW, QUAD * local), BF16),
            pltpu.VMEM((width, local), F32),
            pltpu.VMEM((HEADS, local), F32),
            pltpu.VMEM((HEADS, local), F32),
            pltpu.VMEM((kb, local), F32),
        ],
        1,
        32,
        10,
        span, qt, near, far, info, x, wo, gain,
        kept=(0, 1, 2, 3),
    )


def ffn_kernel(first, final, *refs):
    at_y, n2_ref, up_ref, w_ref = refs[:4]
    prev = None if first else refs[4]
    sng_ref, branch_ref, sums = refs[-3:]
    n2 = n2_ref[...]
    up = up_ref[...]
    hid = w_ref.shape[1]
    gate = mm_nt(n2, w_ref[0])
    lifted = mm_nt(n2, w_ref[1])
    hidden_grad = mm_nt(up, w_ref[2])
    sigmoid = jax.nn.sigmoid(gate)
    silu = gate * sigmoid
    act = (silu * lifted).astype(BF16)
    gate_grad = (hidden_grad * lifted * (sigmoid * (1.0 + gate * (1.0 - sigmoid)))).astype(BF16)
    lift_grad = (hidden_grad * silu).astype(BF16)
    sng_ref[...] = (mm(gate_grad, w_ref[0]) + mm(lift_grad, w_ref[1])).astype(BF16)
    branch_ref[...] = mm(act, w_ref[2]).astype(BF16)
    for at, (left, right) in enumerate(((act, up), (gate_grad, n2), (lift_grad, n2))):
        grad = mm_tn(left, right)
        if not first:
            grad = grad + prev[at]
        if not final:
            sums[at] = grad
        else:
            half = hid // 2
            low = grad.astype(BF16)
            sums[at_y[0], at] = low[:half]
            sums[1 - at_y[0], at] = low[half:]


def feed_forward(at_y, n2, up, weights, prev=None, final=False):
    count, d = n2.shape
    hid = weights.shape[1]
    if final:
        grads = (((2, 3, hid // 2, d), BF16),)
    else:
        grads = ((weights.shape, F32),)
    args = (at_y, n2, up, weights) if prev is None else (at_y, n2, up, weights, prev)
    return kernel_call(
        functools.partial(ffn_kernel, prev is None, final),
        "feed_forward",
        (((count, d), BF16),) * 2 + grads,
        [],
        1,
        19,
        9,
        *args,
        kept=(1, 2) if final else (1,),
        aliases={} if prev is None or final else {4: 2},
    )


def residual_kernel(
    sa, sb, up_ref, hidden_ref, gain_ref, wo_ref, out_t_ref,
    res_ref, low_ref, dot_ref, delta_ref, gain_out,
):
    sng = sa[...].astype(F32) + sb[...].astype(F32)
    hidden = hidden_ref[...]
    scale = lax.rsqrt(jnp.mean(hidden * hidden, axis=-1, keepdims=True) + 1e-06)
    gain_out[...] = jnp.sum(sng * (hidden * scale), axis=0, keepdims=True)
    weighted = sng * gain_ref[...]
    inner = jnp.mean(hidden * weighted, axis=-1, keepdims=True)
    res = up_ref[...].astype(F32) + scale * weighted - hidden * (scale * scale * scale) * inner
    res_ref[...] = res
    low = res.astype(BF16)
    low_ref[...] = low
    dot = mm_nt(wo_ref[...], low).astype(BF16)
    dot_ref[...] = dot
    for h in range(HEADS):
        rows = slice(h * HEAD_DIM, (h + 1) * HEAD_DIM)
        delta_ref[h : h + 1, :] = jnp.sum(
            dot[rows].astype(F32) * out_t_ref[rows, :], axis=0, keepdims=True
        )


def residual(sa, sb, up, hidden, gain, wo, out_t, far=()):
    local, d = hidden.shape
    width = out_t.shape[0]
    return kernel_call(
        residual_kernel,
        "residual",
        (
            ((local, d), F32),
            ((local, d), BF16),
            ((width, local), BF16),
            ((HEADS, local), F32),
            ((1, d), F32),
        ),
        [],
        0,
        16,
        3,
        sa, sb, up, hidden, gain, wo, out_t,
        kept=(0,),
        far=far,
    )


def backward_kernel(
    span, qt_ref, near_ref, far_ref, info_ref, dot_ref, lse_ref, delta_ref,
    qmix_ref, qbase_ref, cos_ref, sin_ref,
    dnear_ref, dfar_ref, dq_ref,
    k_s, kt_s, vt_s, dkt_s, dvt_s, qbd_s, qbdt_s, obd_s, obdt_s, dq_s, bias_s, lse_s, delta_s,
):
    slots, kb_size, _ = k_s.shape
    count = qt_ref.shape[1]
    lo, hi, me = span[0], span[1], span[2]
    dnear_ref[...] = jnp.zeros_like(dnear_ref)
    dfar_ref[...] = jnp.zeros_like(dfar_ref)

    def prepare(slot, kb):
        fac = block_factors(slot, near_ref, far_ref)
        for quad in range(QUADS):
            rows = slice(quad * QW, (quad + 1) * QW)
            kt = materialize_quad(fac, 0, quad)
            kt_s[kb, rows, :] = kt
            k_s[kb, :, rows] = kt.T
            vt_s[kb, rows, :] = materialize_quad(fac, MIX + BASE, quad)
            dkt_s[kb, rows, :] = jnp.zeros((QW, kb_size), F32)
            dvt_s[kb, rows, :] = jnp.zeros((QW, kb_size), F32)

    each_block(me, lo, hi, slots, prepare)
    qbdt_s[...] = jnp.zeros_like(qbdt_s)
    obdt_s[...] = jnp.zeros_like(obdt_s)

    for h in range(HEADS):
        quad, i = h // QUAD, h % QUAD
        to = slice(i * HEAD_DIM, (i + 1) * HEAD_DIM)
        at = slice(i * count, (i + 1) * count)
        rows = slice(h * HEAD_DIM, (h + 1) * HEAD_DIM)
        qbdt_s[quad, to, at] = qt_ref[rows, :]
        obdt_s[quad, to, at] = dot_ref[rows, :]
    for quad in range(QUADS):
        qbd_s[quad] = qbdt_s[quad].T
        obd_s[quad] = obdt_s[quad].T
    lse_t = lse_ref[:, :].T
    delta_t = delta_ref[:, :].T
    for h in range(HEADS):
        lse_s[h] = jnp.broadcast_to(lse_t[:, h : h + 1], (count, TILE))
        delta_s[h] = jnp.broadcast_to(delta_t[:, h : h + 1], (count, TILE))
    dq_s[...] = jnp.zeros_like(dq_s)
    info_t = info_ref[:, :].T
    first = info_t[:, 0:1]
    last = info_t[:, 1:2]

    def step(kb, _):
        places = kb * kb_size + lax.broadcasted_iota(jnp.int32, (count, kb_size), 1)
        bias_s[...] = jnp.where((places >= first) & (places <= last), 0.0, NEG)
        lane = lax.broadcasted_iota(jnp.int32, (count, QW), 1) // HEAD_DIM
        for quad in range(QUADS):
            rows = slice(quad * QW, (quad + 1) * QW)
            s = mm(qbd_s[quad], kt_s[kb, rows, :])
            dp = mm(obd_s[quad], vt_s[kb, rows, :])
            ps = []
            dss = []
            for i in range(QUAD):
                h = quad * QUAD + i
                at = slice(i * count, (i + 1) * count)
                lse = jnp.concatenate([lse_s[h]] * (kb_size // TILE), axis=1)
                delta = jnp.concatenate([delta_s[h]] * (kb_size // TILE), axis=1)
                p = jnp.exp((s[at] + bias_s[...]) - lse)
                ps.append(p.astype(BF16))
                dss.append((p * (dp[at] - delta)).astype(BF16))
            p4 = jnp.concatenate(ps, axis=0)
            ds4 = jnp.concatenate(dss, axis=0)
            dkt_s[kb, rows, :] += mm(qbdt_s[quad], ds4)
            dvt_s[kb, rows, :] += mm(obdt_s[quad], p4)
            dq = mm(ds4, k_s[kb, :, rows])
            out = dq[0:count]
            for i in range(1, QUAD):
                out = jnp.where(lane == i, dq[i * count : (i + 1) * count], out)
            dq_s[:, rows] += out
        return 0

    lax.fori_loop(lo, hi, step, 0)
    dqt = dq_s[...].T * (HEAD_DIM ** -0.5 / Q_RANK)
    qmix = qmix_ref[:, :]
    for h in range(HEADS):
        part = dqt[h * HEAD_DIM : (h + 1) * HEAD_DIM, :]
        dq_ref[h * Q_RANK : (h + 1) * Q_RANK, :] = jnp.concatenate(
            [
                jnp.sum(
                    part * qbase_ref[r * HEAD_DIM : (r + 1) * HEAD_DIM, :],
                    axis=0,
                    keepdims=True,
                )
                for r in range(Q_RANK)
            ],
            axis=0,
        )
    cos = cos_ref[:, :]
    sin = sin_ref[:, :]
    for r in range(Q_RANK):
        out = None
        for h in range(HEADS):
            row = h * Q_RANK + r
            part = qmix[row : row + 1, :] * dqt[h * HEAD_DIM : (h + 1) * HEAD_DIM, :]
            out = part if out is None else out + part
        upper, lower = out[:HALF], out[HALF:]
        at = QMIX + r * HEAD_DIM
        dq_ref[at : at + HALF, :] = upper * cos + lower * sin
        dq_ref[at + HALF : at + HEAD_DIM, :] = lower * cos - upper * sin

    def fold(slot, kb):
        fac = block_factors(slot, near_ref, far_ref)
        to = dfar_ref if slot & 1 else dnear_ref
        for offset, grad in ((0, dkt_s), (MIX + BASE, dvt_s)):
            outs = [None] * KV_RANK
            mixes = []
            for h in range(HEADS):
                g = grad[kb, h * HEAD_DIM : (h + 1) * HEAD_DIM, :] * (1.0 / KV_RANK)
                for r in range(KV_RANK):
                    at = offset + MIX + r * HEAD_DIM
                    mixes.append(jnp.sum(g * fac[at : at + HEAD_DIM, :], axis=0, keepdims=True))
                    row = offset + h * KV_RANK + r
                    part = fac[row : row + 1, :] * g
                    outs[r] = part if outs[r] is None else outs[r] + part
            to[slot >> 1, offset : offset + MIX, :] = jnp.concatenate(mixes, axis=0).astype(BF16)
            for r in range(KV_RANK):
                at = offset + MIX + r * HEAD_DIM
                to[slot >> 1, at : at + HEAD_DIM, :] = outs[r].astype(BF16)

    each_block(me, lo, hi, slots, fold)


def attend_backward(micros, span, qt, near, far, info, dot, lse, delta, qmix, qbase, cos, sin):
    width, local = qt.shape
    kb = local
    blocks = 2 * near.shape[0]
    return kernel_call(
        backward_kernel,
        "attend_backward",
        (
            (near.shape, BF16),
            (near.shape, BF16),
            ((QMIX + QBASE, local), F32),
        ),
        [
            pltpu.VMEM((blocks, kb, width), BF16),
            pltpu.VMEM((blocks, width, kb), BF16),
            pltpu.VMEM((blocks, width, kb), BF16),
            pltpu.VMEM((blocks, width, kb), F32),
            pltpu.VMEM((blocks, width, kb), F32),
            pltpu.VMEM((QUADS, QUAD * local, QW), BF16),
            pltpu.VMEM((QUADS, QW, QUAD * local), BF16),
            pltpu.VMEM((QUADS, QUAD * local, QW), BF16),
            pltpu.VMEM((QUADS, QW, QUAD * local), BF16),
            pltpu.VMEM((local, width), F32),
            pltpu.VMEM((local, kb), F32),
            pltpu.VMEM((HEADS, local, TILE), F32),
            pltpu.VMEM((HEADS, local, TILE), F32),
        ],
        1,
        56,
        micros,
        span, qt, near, far, info, dot, lse, delta, qmix, qbase, cos, sin,
        far=(1, 6, 8, 9),
    )


def finish_kernel(*refs):
    fa, f1, f2, f3, dq_ref, cos_ref, sin_ref, x_ref, gain_ref, res_ref = refs[:10]
    weights = refs[10:16]
    low_ref, grad_ref, gain_out = refs[16:]
    total = (fa[...].astype(F32) + f1[...].astype(F32)) + (
        f2[...].astype(F32) + f3[...].astype(F32)
    )
    cos = cos_ref[...]
    sin = sin_ref[...]
    query = QMIX + QBASE
    low_ref[:query, :] = dq_ref[...].astype(BF16)
    low_ref[query:, :] = total.astype(BF16)
    for r in range(KV_RANK):
        at = MIX + r * HEAD_DIM
        a, b = total[at : at + HALF], total[at + HALF : at + HEAD_DIM]
        to = query + at
        low_ref[to : to + HALF, :] = (a * cos + b * sin).astype(BF16)
        low_ref[to + HALF : to + HEAD_DIM, :] = (b * cos - a * sin).astype(BF16)
    low = low_ref[...].T
    grad = None
    at = 0
    for ref in weights:
        if ref.shape[0] == x_ref.shape[1]:
            count = ref.shape[1]
            part = mm_nt(low[:, at : at + count], ref[...])
        else:
            count = ref.shape[0]
            part = mm(low[:, at : at + count], ref[...])
        grad = part if grad is None else grad + part
        at += count
    x = x_ref[...].astype(F32)
    scale = lax.rsqrt(jnp.mean(x * x, axis=-1, keepdims=True) + 1e-06)
    gain_out[...] = jnp.sum(grad * (x * scale), axis=0, keepdims=True)
    weighted = grad * gain_ref[...]
    inner = jnp.mean(x * weighted, axis=-1, keepdims=True)
    grad_ref[...] = res_ref[...] + (scale * weighted - x * (scale * scale * scale) * inner)


def finish(pieces, dq, cos, sin, x, gain, res, weights):
    local, d = x.shape
    return kernel_call(
        finish_kernel,
        "finish",
        (
            ((QMIX + QBASE + FACTORS, local), BF16),
            ((local, d), F32),
            ((1, d), F32),
        ),
        [],
        0,
        16,
        2,
        *pieces, dq, cos, sin, x, gain, res, *weights,
    )


def share_kernel(me, low0, low1, n0, n1, g0, g1, h0, h1, near_ref, far_ref, all_s):
    rows = low0.shape[0]
    all_s[:rows, :] = mm(
        jnp.concatenate([low0[...], low1[...]], axis=1),
        jnp.concatenate([n0[...], n1[...]], axis=0),
    )
    all_s[rows:, :] = jnp.concatenate(
        [g0[...] + g1[...], h0[...] + h1[...], jnp.zeros((14, g0.shape[1]), F32)], axis=0
    )
    width = near_ref.shape[2]
    for is_far, ref in ((0, near_ref), (1, far_ref)):
        for slot in range(ref.shape[0]):
            at = pl.multiple_of(jnp.bitwise_xor(me[0], 2 * slot + is_far) * width, width)
            ref[slot] = all_s[:, pl.ds(at, width)].astype(BF16)


def share(me, lows, normeds, first_gains, second_gains, slots):
    rows = lows[0].shape[0] + 16
    d = normeds[0].shape[1]
    return kernel_call(
        share_kernel,
        "share",
        (((slots // 2, rows, d // slots), BF16),) * 2,
        [pltpu.VMEM((rows, d), F32)],
        1,
        16,
        2,
        me, *lows, *normeds, *first_gains, *second_gains,
    )


highest = lax.Precision.HIGHEST
masked_score = -1e30


def rms_scale(values):
    return lax.rsqrt(jnp.mean(values * values, axis=-1, keepdims=True) + 1e-06)


def norm_backward(values, gain, scaled, upstream):
    weighted = upstream * gain
    inner = jnp.mean(values * weighted, axis=-1, keepdims=True)
    return scaled * weighted - values * (scaled * scaled * scaled) * inner


def rotate(values, cosine, sine):
    half = values.shape[-1] // 2
    first = values[..., :half]
    second = values[..., half:]
    return jnp.concatenate(
        [first * cosine - second * sine, first * sine + second * cosine], axis=-1
    )


def row_layout(lengths_row, places):
    ends = jnp.cumsum(lengths_row)
    passed = ends[None, :] <= places[:, None]
    segment = jnp.sum(passed.astype(jnp.int32), axis=1)
    start = jnp.max(jnp.where(passed, ends[None, :], 0), axis=1)
    valid = places < ends[-1]
    return (segment, places - start, valid)


def rope_tables(position):
    half = HEAD_DIM // 2
    frequency = 10000.0 ** (-jnp.arange(half, dtype=jnp.float32) / half)
    angle = position.astype(jnp.float32)[..., None] * frequency
    return (jnp.cos(angle), jnp.sin(angle))


def split_factors(factors):
    mix_width = HEADS * KV_RANK
    base_width = KV_RANK * HEAD_DIM
    count, rows = (factors.shape[0], factors.shape[1])
    key_mix = factors[..., :mix_width].reshape(count, rows, HEADS, KV_RANK)
    key_base = factors[..., mix_width : mix_width + base_width].reshape(
        count, rows, KV_RANK, HEAD_DIM
    )
    value_mix = factors[..., mix_width + base_width : 2 * mix_width + base_width].reshape(
        count, rows, HEADS, KV_RANK
    )
    value_base = factors[..., 2 * mix_width + base_width :].reshape(count, rows, KV_RANK, HEAD_DIM)
    return (key_mix, key_base, value_mix, value_base)


def pair_gradient(hidden_grad, gate, lifted):
    sigmoid = jax.nn.sigmoid(gate)
    gate_grad = hidden_grad * lifted * (sigmoid * (1.0 + gate * (1.0 - sigmoid)))
    lift_grad = hidden_grad * (gate * sigmoid)
    return jnp.concatenate([gate_grad, lift_grad], axis=-1).astype(jnp.bfloat16)


def general_body(
    tokens,
    lengths,
    cotangent,
    first_gain,
    query_heads,
    query_basis,
    key_heads,
    key_basis,
    value_heads,
    value_basis,
    output_weight,
    second_gain,
    gate_weight,
    up_weight,
    down_projection_weight,
):
    local, batch_rows, width = tokens.shape
    total = local * lax.axis_size("wide")
    offset = lax.axis_index("wide") * local
    places = jnp.arange(total, dtype=jnp.int32)
    segment, position, valid = jax.vmap(row_layout, in_axes=(0, None))(lengths, places)
    own_places = offset + jnp.arange(local, dtype=jnp.int32)
    own_segment = lax.dynamic_slice_in_dim(segment, offset, local, 1)
    own_position = lax.dynamic_slice_in_dim(position, offset, local, 1)
    own_valid = lax.dynamic_slice_in_dim(valid, offset, local, 1)
    cosine, sine = rope_tables(jnp.transpose(own_position))
    cosine = cosine[:, :, None, :]
    sine = sine[:, :, None, :]
    keep_rows = jnp.transpose(own_valid)[:, :, None]
    scale = HEAD_DIM ** (-0.5)
    block_rows = min(512, total)
    block_count = total // block_rows
    mix_width = HEADS * KV_RANK
    base_width = KV_RANK * HEAD_DIM
    flat_rows = local * batch_rows
    inputs = tokens.astype(jnp.float32)
    first_scale = rms_scale(inputs)
    normed = (inputs * first_scale * first_gain).astype(jnp.bfloat16)
    flat = normed.reshape(flat_rows, width)
    query_mix = jnp.dot(flat, query_heads, preferred_element_type=jnp.float32).reshape(
        local, batch_rows, HEADS, Q_RANK
    )
    query_raw = jnp.dot(flat, query_basis, preferred_element_type=jnp.float32).reshape(
        local, batch_rows, Q_RANK, HEAD_DIM
    )
    query_base = rotate(query_raw, cosine, sine)
    factor_weight = jnp.concatenate([key_heads, key_basis, value_heads, value_basis], axis=1)
    factor_raw = jnp.dot(flat, factor_weight, preferred_element_type=jnp.float32).reshape(
        local, batch_rows, -1
    )
    key_roped = rotate(
        factor_raw[..., mix_width : mix_width + base_width].reshape(
            local, batch_rows, KV_RANK, HEAD_DIM
        ),
        cosine,
        sine,
    ).reshape(local, batch_rows, base_width)
    factors = jnp.concatenate(
        [factor_raw[..., :mix_width], key_roped, factor_raw[..., mix_width + base_width :]], axis=-1
    ).astype(jnp.bfloat16)
    every = lax.all_gather(factors, "wide", axis=0, tiled=True)
    key_mix, key_base, value_mix, value_base = split_factors(every)
    keys = (
        jnp.einsum("trhk,trkd->trhd", key_mix, key_base, preferred_element_type=jnp.float32)
        / KV_RANK
    ).astype(jnp.bfloat16)
    values = (
        jnp.einsum("trhk,trkd->trhd", value_mix, value_base, preferred_element_type=jnp.float32)
        / KV_RANK
    ).astype(jnp.bfloat16)
    query = (
        jnp.einsum(
            "trhk,trkd->trhd",
            query_mix,
            query_base,
            precision=highest,
            preferred_element_type=jnp.float32,
        )
        / Q_RANK
    ).astype(jnp.bfloat16)

    def block_view(block):
        start = block * block_rows
        key_places = start + jnp.arange(block_rows, dtype=jnp.int32)
        key_segment = lax.dynamic_slice_in_dim(segment, start, block_rows, 1)
        key_valid = lax.dynamic_slice_in_dim(valid, start, block_rows, 1)
        causal = key_places[None, :] <= own_places[:, None]
        itself = key_places[None, :] == own_places[:, None]
        allowed = (
            causal[None]
            & (own_segment[:, :, None] == key_segment[:, None, :])
            & (key_valid[:, None, :] | itself[None])
        )
        key_block = lax.dynamic_slice_in_dim(keys, start, block_rows, 0)
        value_block = lax.dynamic_slice_in_dim(values, start, block_rows, 0)
        product = (
            jnp.einsum("qrhd,krhd->rhqk", query, key_block, preferred_element_type=jnp.float32)
            * scale
        )
        scores = jnp.where(allowed[:, None], product, masked_score)
        return (start, scores, key_block, value_block)

    def max_step(carry, block):
        top, mass = carry
        scores = block_view(block)[1]
        higher = jnp.maximum(top, jnp.max(scores, axis=-1))
        mass = mass * jnp.exp(top - higher) + jnp.sum(jnp.exp(scores - higher[..., None]), axis=-1)
        return ((higher, mass), None)

    start_top = jnp.full((batch_rows, HEADS, local), masked_score, jnp.float32)
    (top, mass), _ = lax.scan(
        max_step, (start_top, jnp.zeros_like(start_top)), jnp.arange(block_count)
    )
    log_total = top + jnp.log(mass)

    def out_step(carry, block):
        _, scores, _, value_block = block_view(block)
        chances = jnp.exp(scores - log_total[..., None]).astype(jnp.bfloat16)
        return (
            carry
            + jnp.einsum(
                "rhqk,krhd->qrhd", chances, value_block, preferred_element_type=jnp.float32
            ),
            None,
        )

    attended, _ = lax.scan(
        out_step,
        jnp.zeros((local, batch_rows, HEADS, HEAD_DIM), jnp.float32),
        jnp.arange(block_count),
    )
    mixed = attended.astype(jnp.bfloat16).reshape(flat_rows, HEADS * HEAD_DIM)
    hidden_state = inputs + jnp.dot(
        mixed, output_weight, preferred_element_type=jnp.float32
    ).reshape(local, batch_rows, width)
    second_scale = rms_scale(hidden_state)
    normed_second = (hidden_state * second_scale * second_gain).astype(jnp.bfloat16)
    normalized_token_rows = lax.all_gather(normed_second, "wide", axis=0, tiled=True)
    gate_lifted_hidden = jnp.concatenate([gate_weight, up_weight], axis=1)
    hidden_width = gate_weight.shape[1]
    projected_output = jnp.einsum(
        "zec,cx->zex", normalized_token_rows, gate_lifted_hidden, preferred_element_type=jnp.float32
    )
    gate = projected_output[..., :hidden_width]
    lifted = projected_output[..., hidden_width:]
    silu_hidden_output = (jax.nn.silu(gate) * lifted).astype(jnp.bfloat16)
    sequence_portion = silu_hidden_output
    branch = lax.psum_scatter(
        jnp.einsum(
            "zyu,uv->zyv",
            sequence_portion,
            down_projection_weight,
            preferred_element_type=jnp.float32,
        ).astype(jnp.bfloat16),
        "wide",
        scatter_dimension=0,
        tiled=True,
    ).astype(jnp.float32)
    output = jnp.where(keep_rows, hidden_state + branch, 0.0).astype(jnp.bfloat16)
    upstream = jnp.where(keep_rows, cotangent.astype(jnp.float32), 0.0)
    upstream_low = upstream.astype(jnp.bfloat16)
    upstream_token_gradient = lax.all_gather(upstream_low, "wide", axis=0, tiled=True)
    hidden_grad = jnp.einsum(
        "ajg,vg->ajv",
        upstream_token_gradient,
        down_projection_weight,
        preferred_element_type=jnp.float32,
    )
    pair_product_gradient = pair_gradient(hidden_grad, gate, lifted)
    down_gradient = jnp.einsum(
        "imj,ima->ja",
        silu_hidden_output,
        upstream_token_gradient,
        preferred_element_type=jnp.float32,
    )
    pair_weight_grad = jnp.einsum(
        "ipl,ipj->lj",
        normalized_token_rows,
        pair_product_gradient,
        preferred_element_type=jnp.float32,
    )
    sequence_portion = pair_product_gradient
    second_normed_grad = lax.psum_scatter(
        jnp.einsum(
            "ivu,bu->ivb", sequence_portion, gate_lifted_hidden, preferred_element_type=jnp.float32
        ),
        "wide",
        scatter_dimension=0,
        tiled=True,
    )
    second_gain_partial = jnp.sum(second_normed_grad * (hidden_state * second_scale), axis=(0, 1))
    residual_grad = upstream + norm_backward(
        hidden_state, second_gain, second_scale, second_normed_grad
    )
    residual_low = residual_grad.astype(jnp.bfloat16).reshape(flat_rows, width)
    output_weight_grad = jnp.einsum(
        "tk,td->kd", mixed, residual_low, preferred_element_type=jnp.float32
    )
    mixed_grad = (
        jnp.einsum("td,kd->tk", residual_low, output_weight, preferred_element_type=jnp.float32)
        .astype(jnp.bfloat16)
        .reshape(local, batch_rows, HEADS, HEAD_DIM)
    )

    def delta_step(carry, block):
        _, scores, _, value_block = block_view(block)
        chances = jnp.exp(scores - log_total[..., None])
        pressure = jnp.einsum(
            "qrhd,krhd->rhqk", mixed_grad, value_block, preferred_element_type=jnp.float32
        )
        return (carry + jnp.sum(chances * pressure, axis=-1), None)

    delta, _ = lax.scan(
        delta_step, jnp.zeros((batch_rows, HEADS, local), jnp.float32), jnp.arange(block_count)
    )

    def grad_step(carry, block):
        start, scores, key_block, value_block = block_view(block)
        chances = jnp.exp(scores - log_total[..., None])
        pressure = jnp.einsum(
            "qrhd,krhd->rhqk", mixed_grad, value_block, preferred_element_type=jnp.float32
        )
        score_grad = (chances * (pressure - delta[..., None])).astype(jnp.bfloat16)
        carry = (
            carry
            + jnp.einsum(
                "rhqk,krhd->qrhd", score_grad, key_block, preferred_element_type=jnp.float32
            )
            * scale
        )
        key_grad = (
            jnp.einsum("rhqk,qrhd->krhd", score_grad, query, preferred_element_type=jnp.float32)
            * scale
        )
        value_grad = jnp.einsum(
            "rhqk,qrhd->krhd",
            chances.astype(jnp.bfloat16),
            mixed_grad,
            preferred_element_type=jnp.float32,
        )
        block_mix, block_base, block_vmix, block_vbase = split_factors(
            lax.dynamic_slice_in_dim(every, start, block_rows, 0).astype(jnp.float32)
        )
        key_mix_grad = (
            jnp.einsum("krhd,krcd->krhc", key_grad, block_base, precision=highest) / KV_RANK
        )
        key_base_grad = (
            jnp.einsum("krhc,krhd->krcd", block_mix, key_grad, precision=highest) / KV_RANK
        )
        value_mix_grad = (
            jnp.einsum("krhd,krcd->krhc", value_grad, block_vbase, precision=highest) / KV_RANK
        )
        value_base_grad = (
            jnp.einsum("krhc,krhd->krcd", block_vmix, value_grad, precision=highest) / KV_RANK
        )
        block_grad = jnp.concatenate(
            [
                key_mix_grad.reshape(block_rows, batch_rows, mix_width),
                key_base_grad.reshape(block_rows, batch_rows, base_width),
                value_mix_grad.reshape(block_rows, batch_rows, mix_width),
                value_base_grad.reshape(block_rows, batch_rows, base_width),
            ],
            axis=-1,
        )
        return (carry, block_grad)

    query_grad, factor_blocks = lax.scan(
        grad_step,
        jnp.zeros((local, batch_rows, HEADS, HEAD_DIM), jnp.float32),
        jnp.arange(block_count),
    )
    factor_grads = factor_blocks.reshape(total, batch_rows, 2 * mix_width + 2 * base_width)
    own_factor_grads = lax.psum_scatter(
        factor_grads.astype(jnp.bfloat16), "wide", scatter_dimension=0, tiled=True
    ).astype(jnp.float32)
    key_base_back = rotate(
        own_factor_grads[..., mix_width : mix_width + base_width].reshape(
            local, batch_rows, KV_RANK, HEAD_DIM
        ),
        cosine,
        -sine,
    ).reshape(local, batch_rows, base_width)
    factor_low = (
        jnp.concatenate(
            [
                own_factor_grads[..., :mix_width],
                key_base_back,
                own_factor_grads[..., mix_width + base_width :],
            ],
            axis=-1,
        )
        .astype(jnp.bfloat16)
        .reshape(flat_rows, -1)
    )
    mix_grad = jnp.einsum("trhd,trcd->trhc", query_grad, query_base, precision=highest) / Q_RANK
    base_roped_grad = (
        jnp.einsum("trhc,trhd->trcd", query_mix, query_grad, precision=highest) / Q_RANK
    )
    base_grad = rotate(base_roped_grad, cosine, -sine)
    mix_low = mix_grad.astype(jnp.bfloat16).reshape(flat_rows, HEADS * Q_RANK)
    base_low = base_grad.astype(jnp.bfloat16).reshape(flat_rows, Q_RANK * HEAD_DIM)
    query_heads_grad = jnp.einsum("tk,tf->kf", flat, mix_low, preferred_element_type=jnp.float32)
    query_basis_grad = jnp.einsum("tk,tf->kf", flat, base_low, preferred_element_type=jnp.float32)
    factor_weight_grad = jnp.einsum(
        "tk,tf->kf", flat, factor_low, preferred_element_type=jnp.float32
    )
    first_normed_grad = (
        jnp.einsum("tf,kf->tk", mix_low, query_heads, preferred_element_type=jnp.float32)
        + jnp.einsum("tf,kf->tk", base_low, query_basis, preferred_element_type=jnp.float32)
        + jnp.einsum("tf,kf->tk", factor_low, factor_weight, preferred_element_type=jnp.float32)
    ).reshape(local, batch_rows, width)
    first_gain_partial = jnp.sum(first_normed_grad * (inputs * first_scale), axis=(0, 1))
    tokens_gradient = residual_grad + norm_backward(
        inputs, first_gain, first_scale, first_normed_grad
    )
    key_heads_grad = factor_weight_grad[:, :mix_width]
    key_basis_grad = factor_weight_grad[:, mix_width : mix_width + base_width]
    value_heads_grad = factor_weight_grad[:, mix_width + base_width : 2 * mix_width + base_width]
    value_basis_grad = factor_weight_grad[:, 2 * mix_width + base_width :]
    (
        first_share,
        qheads_share,
        qbasis_share,
        kheads_share,
        kbasis_share,
        vheads_share,
        vbasis_share,
        output_share,
        second_share,
    ) = (
        lax.psum_scatter(
            first_gain_partial.astype(jnp.bfloat16), "wide", scatter_dimension=0, tiled=True
        ).astype(jnp.float32),
        lax.psum_scatter(
            query_heads_grad.astype(jnp.bfloat16), "wide", scatter_dimension=0, tiled=True
        ).astype(jnp.float32),
        lax.psum_scatter(
            query_basis_grad.astype(jnp.bfloat16), "wide", scatter_dimension=0, tiled=True
        ).astype(jnp.float32),
        lax.psum_scatter(
            key_heads_grad.astype(jnp.bfloat16), "wide", scatter_dimension=0, tiled=True
        ).astype(jnp.float32),
        lax.psum_scatter(
            key_basis_grad.astype(jnp.bfloat16), "wide", scatter_dimension=0, tiled=True
        ).astype(jnp.float32),
        lax.psum_scatter(
            value_heads_grad.astype(jnp.bfloat16), "wide", scatter_dimension=0, tiled=True
        ).astype(jnp.float32),
        lax.psum_scatter(
            value_basis_grad.astype(jnp.bfloat16), "wide", scatter_dimension=0, tiled=True
        ).astype(jnp.float32),
        lax.psum_scatter(
            output_weight_grad.astype(jnp.bfloat16), "wide", scatter_dimension=0, tiled=True
        ).astype(jnp.float32),
        lax.psum_scatter(
            second_gain_partial.astype(jnp.bfloat16), "wide", scatter_dimension=0, tiled=True
        ).astype(jnp.float32),
    )
    gate_share = pair_weight_grad[:, :hidden_width]
    lift_share = pair_weight_grad[:, hidden_width:]
    totals = (
        lax.psum(first_share.astype(jnp.bfloat16), "batch").astype(jnp.float32),
        lax.psum(qheads_share.astype(jnp.bfloat16), "batch").astype(jnp.float32),
        lax.psum(qbasis_share.astype(jnp.bfloat16), "batch").astype(jnp.float32),
        lax.psum(kheads_share.astype(jnp.bfloat16), "batch").astype(jnp.float32),
        lax.psum(kbasis_share.astype(jnp.bfloat16), "batch").astype(jnp.float32),
        lax.psum(vheads_share.astype(jnp.bfloat16), "batch").astype(jnp.float32),
        lax.psum(vbasis_share.astype(jnp.bfloat16), "batch").astype(jnp.float32),
        lax.psum(output_share.astype(jnp.bfloat16), "batch").astype(jnp.float32),
        lax.psum(second_share.astype(jnp.bfloat16), "batch").astype(jnp.float32),
        lax.psum(gate_share.astype(jnp.bfloat16), "batch").astype(jnp.float32),
        lax.psum(lift_share.astype(jnp.bfloat16), "batch").astype(jnp.float32),
        lax.psum(down_gradient.astype(jnp.bfloat16), "batch").astype(jnp.float32),
    )
    return (
        output,
        tokens_gradient,
        totals[0],
        totals[1],
        totals[2],
        totals[3],
        totals[4],
        totals[5],
        totals[6],
        totals[7],
        totals[8],
        totals[9],
        totals[10],
        totals[11],
    )


def partners(distance, count):
    return [(i, i ^ distance) for i in range(count)]


def fence(*values):
    return lax.optimization_barrier(values)


def after(value, *others):
    return lax.optimization_barrier((value,) + others)[0]


def body(
    tokens,
    lengths,
    cotangent,
    first_gain,
    query_heads,
    query_basis,
    key_heads,
    key_basis,
    value_heads,
    value_basis,
    output_weight,
    second_gain,
    gate_weight,
    up_weight,
    down_projection_weight,
):
    local, rows, width = tokens.shape
    wide = ("y", "x", "core")
    n = lax.axis_size(wide)
    depth = lax.axis_size("batch")
    me = lax.axis_index(wide).astype(jnp.int32)
    at_y = lax.axis_index("y").astype(jnp.int32).reshape(1)

    def swap(value, distance):
        return lax.ppermute(value, wide, partners(distance, n))

    def swap_batch(value, distance):
        return lax.ppermute(value, "batch", partners(distance, depth))

    core, across, along, diagonal = 1, 2, 4, 6
    chips = (across, along, diagonal)

    def send_chips(value):
        return [swap(value, distance) for distance in chips]

    def send_slots(sums):
        return [swap(sums[i + 1], chips[i]) for i in range(len(chips))]

    def add(*values):
        return sum(value.astype(F32) for value in values).astype(BF16)

    places = me * local + jnp.arange(local, dtype=jnp.int32)
    slots = lengths.shape[1]
    upto = jnp.arange(slots)[:, None] >= jnp.arange(slots)[None, :]
    ends = jnp.sum(jnp.where(upto[None], lengths[:, None, :], 0), axis=2)
    passed = ends[:, None, :] <= places[None, :, None]
    start = jnp.max(jnp.where(passed, ends[:, None, :], 0), axis=2)
    valid = places[None, :] < ends[:, -1:]
    position = places[None, :] - start
    first_seen = jnp.where(valid, start, places[None, :])
    frequency = 10000.0 ** (-jnp.arange(HALF, dtype=F32) / HALF)
    angle = position.astype(F32)[:, None, :] * frequency[None, :, None]
    cosine, sine = jnp.cos(angle), jnp.sin(angle)
    info = jnp.stack([first_seen, jnp.broadcast_to(places, (rows, local))], axis=1)
    info = jnp.concatenate([info, jnp.zeros((rows, 6, local), jnp.int32)], axis=1)
    spans = jnp.stack(
        [
            jnp.min(first_seen, axis=1) // local,
            jnp.broadcast_to(me + 1, (rows,)),
            jnp.broadcast_to(me, (rows,)),
        ],
        axis=1,
    ).astype(jnp.int32)

    gain1 = first_gain.reshape(1, width)
    gain2 = second_gain.reshape(1, width)
    projections = (query_heads, query_basis, key_heads, key_basis, value_heads, value_basis)
    narrow = tuple(w.T if w.shape[1] < TILE else w for w in projections)

    xs = [tokens[:, b, :] for b in range(rows)]
    projected = [project(xs[0], gain1, narrow, cosine[0], sine[0])]
    sent0 = send_chips(projected[0][0])
    x1 = after(xs[1], projected[0][0])
    projected.append(project(x1, gain1, narrow, cosine[1], sine[1]))
    sent1 = send_chips(projected[1][0])
    own_weights = jnp.stack(
        [after(gate_weight.T, projected[1][0]), up_weight.T, down_projection_weight]
    )
    other_weights = swap(own_weights, along)
    near = jnp.stack([projected[0][0]] + [after(got, own_weights) for got in sent0])
    far = swap(near, core)
    gathered = [(near, far)]
    seen = after(valid, near)
    ups = [jnp.where(seen[b][:, None], cotangent[:, b, :], 0) for b in range(rows)]
    up_pair = jnp.concatenate(ups, axis=0)
    up_got = swap(up_pair, across)

    def forward(b):
        outs = attend_forward(
            spans[b], projected[b][1], *gathered[b], info[b], xs[b], output_weight, gain2
        )
        return outs[:4], outs[4]

    gathered[0] = (near, after(far, up_pair))
    kept0, n20 = forward(0)
    n20, up_got, *sent1 = fence(n20, up_got, *sent1)
    n2_sent0 = swap(n20, across)
    near = jnp.stack([projected[1][0]] + list(sent1))
    far = swap(near, core)
    up_near = [
        jnp.concatenate([ups[b], up_got[b * local : (b + 1) * local]], axis=0)
        for b in range(rows)
    ]
    near, far, *up_near = fence(near, far, *up_near)
    gathered.append((near, far))
    up_far = [swap(up_near[b], core) for b in range(rows)]
    kept1, n21 = forward(1)
    n21, up_far0, up_far1, n2_sent0, other_weights = fence(
        n21, *up_far, n2_sent0, other_weights
    )
    weights = jnp.concatenate([own_weights, other_weights], axis=1)
    attended = (kept0, kept1)

    near0 = jnp.concatenate([n20, n2_sent0], axis=0)
    n2_sent1 = swap(n21, across)
    far0 = swap(near0, core)
    sn0, bn0, grads = feed_forward(at_y, near0, up_near[0], weights)
    sn0, bn0, grads, n2_sent1, far0 = fence(sn0, bn0, grads, n2_sent1, far0)
    near1 = jnp.concatenate([n21, n2_sent1], axis=0)
    far1 = swap(near1, core)
    sf0, bf0, grads = feed_forward(at_y, after(far0, near1), up_far0, weights, grads)
    sf0, bf0, grads, far1 = fence(sf0, bf0, grads, far1)
    sf0_got = swap(sf0, core)
    sn1, bn1, grads = feed_forward(at_y, near1, up_near[1], weights, grads)
    sn1, bn1, grads, sf0_got = fence(sn1, bn1, grads, sf0_got)
    sum0 = add(sn0, sf0_got)
    theirs = sum0[local:]
    across0 = swap(theirs, across)
    sf1, bf1, grads = feed_forward(
        at_y, after(far1, theirs), up_far1, weights, grads, True
    )
    sf1, bf1, grads, across0 = fence(sf1, bf1, grads, across0)
    block_part = lax.psum_scatter(
        grads.reshape(-1, width), ("y", "batch"), scatter_dimension=0, tiled=True
    )

    def residual_of(b, mine, got):
        mixed, out_t, lse, hidden = attended[b]
        return residual(
            mine, got, ups[b], hidden, gain2, output_weight, out_t, (2, 3, 5, 6)
        )

    sf1_got = swap(sf1, core)
    residual0 = residual_of(0, sum0[:local], across0)
    *residual0, sf1_got = fence(*residual0, sf1_got)
    sum1 = add(sn1, sf1_got)
    theirs = sum1[local:]

    def back(b, outs, *hold):
        res, low, dot, delta, gain_share = outs
        fac, qt, qmix, qbase, normed = projected[b]
        return attend_backward(
            (40, 0.1)[b], spans[b], qt, *gathered[b], info[b], after(dot, *hold), attended[b][2], delta,
            qmix, qbase, cosine[b], sine[b],
        )

    across1 = swap(theirs, across)
    bf_got = [swap(value, core) for value in (bf0, bf1)]
    dnear0, dfar0, dq0 = back(0, residual0, theirs)
    dnear0, dfar0, dq0, across1, *bf_got = fence(dnear0, dfar0, dq0, across1, *bf_got)
    dfar0_got = swap(dfar0, core)
    residual1 = residual_of(1, sum1[:local], across1)
    *residual1, dnear0, dfar0_got = fence(*residual1, dnear0, dfar0_got)
    residuals = (residual0, residual1)
    fsum0 = add(dnear0, dfar0_got)
    fparts0 = send_slots(fsum0)
    wo_grad = sum(
        mm_tn(after(attended[b][0], fsum0), residuals[b][1]) for b in range(rows)
    ).astype(BF16)
    slots = wo_grad.reshape(n, width // n, width)
    order = [me ^ (2 * i) for i in range(n // 2)]
    wo_near = jnp.stack([lax.dynamic_index_in_dim(slots, i, 0, keepdims=False) for i in order])
    wo_far = jnp.stack([lax.dynamic_index_in_dim(slots, i ^ 1, 0, keepdims=False) for i in order])
    wo_got = swap(wo_far, core)
    dnear1, dfar1, dq1 = back(1, residual1, wo_far)
    dnear1, dfar1, dq1, wo_got, *fparts0 = fence(dnear1, dfar1, dq1, wo_got, *fparts0)

    dfar1_got = swap(dfar1, core)
    branches = [
        add(near, after(got, dnear1)) for near, got in zip((bn0, bn1), bf_got)
    ]
    branch_theirs = jnp.concatenate([value[local:] for value in branches], axis=0)
    dfar1_got, dnear1, branch_theirs = fence(dfar1_got, dnear1, branch_theirs)
    fsum1 = add(dnear1, dfar1_got)
    fparts1 = send_slots(fsum1)
    low0, grad0, gain_share0 = finish(
        [fsum0[0], after(fparts0[0], fsum1)] + list(fparts0[1:]),
        dq0, cosine[0], sine[0], xs[0], gain1, residual0[0], narrow,
    )
    wo_sum = add(wo_near, after(wo_got, low0))
    *fparts1, fsum1, wo_sum, block_part = fence(*fparts1, fsum1, wo_sum, block_part)
    block_grad = lax.all_gather(block_part, "batch", axis=0, tiled=True)
    low1, grad1, gain_share1 = finish(
        [fsum1[0]] + list(fparts1),
        dq1, cosine[1], sine[1], xs[1], gain1, residual1[0], narrow,
    )
    near, far = share(
        me.reshape(1),
        (low0, low1),
        [projected[b][4] for b in range(rows)],
        (gain_share0, gain_share1),
        (residual0[4], residual1[4]),
        n,
    )
    far_got = swap(far, core)
    wo_sent = send_slots(after(wo_sum, near))
    far_got, near, wo_own = fence(far_got, near, wo_sum[0])
    small = add(near, far_got)
    small_sent = send_slots(after(small, *wo_sent))
    wo_total = add(wo_own, *wo_sent)
    wo_got = swap_batch(wo_total, 1)
    branch_got = swap(after(branch_theirs, small), across)
    *small_sent, small, wo_total, wo_got = fence(*small_sent, small, wo_total, wo_got)
    small = add(small[0], *small_sent)
    small_got = swap_batch(small, 1)
    wo_total = add(wo_total, wo_got)
    wo_got = swap_batch(wo_total, depth - 1)
    tokens_gradient = jnp.stack([after(grad0, wo_total), grad1], axis=1)
    tokens_gradient, small_got = fence(tokens_gradient, small_got)
    small = add(small, small_got)
    small_got = swap_batch(small, depth - 1)
    outputs = []
    for b in range(rows):
        mine = branches[b][:local].astype(F32)
        got = after(branch_got, small)[b * local : (b + 1) * local].astype(F32)
        outputs.append(
            jnp.where(valid[b][:, None], attended[b][3] + (mine + got), 0.0).astype(BF16)
        )
    output = jnp.stack(outputs, axis=1)
    output_weight_grad = wo_total.astype(F32) + after(wo_got, output).astype(F32)
    small = small.astype(F32) + after(small_got, output_weight_grad).astype(F32)
    hid = gate_weight.shape[1]
    block_grad = after(block_grad, small).astype(F32)
    down_grad = block_grad[:hid]
    gate_grad = block_grad[hid : 2 * hid].T
    lift_grad = block_grad[2 * hid :].T
    count = width // n

    def pick(at, size):
        return small[at : at + size].T

    query_heads_grad = pick(0, QMIX)
    query_basis_grad = pick(QMIX, QBASE)
    at = QMIX + QBASE
    key_heads_grad = pick(at, MIX)
    key_basis_grad = pick(at + MIX, BASE)
    value_heads_grad = pick(at + MIX + BASE, MIX)
    value_basis_grad = pick(at + 2 * MIX + BASE, BASE)
    at = at + FACTORS
    first_gain_grad = small[at].reshape(count)
    second_gain_grad = small[at + 1].reshape(count)

    return (
        output,
        tokens_gradient,
        first_gain_grad,
        query_heads_grad,
        query_basis_grad,
        key_heads_grad,
        key_basis_grad,
        value_heads_grad,
        value_basis_grad,
        output_weight_grad,
        second_gain_grad,
        gate_grad,
        lift_grad,
        down_grad,
    )


def solution(mesh):
    batch, wide = mesh.shape["batch"], mesh.shape["wide"]
    split = wide == 8 and batch == 4
    w = "wide"
    if split:
        mesh = jax.sharding.Mesh(
            mesh.devices.reshape(batch, 2, 2, 2), ("batch", "y", "x", "core")
        )
        w = ("y", "x", "core")
    rows = P(w, "batch", None)
    return jax.shard_map(
        body if split else general_body,
        mesh=mesh,
        in_specs=(rows, P("batch", None), rows)
        + (P(),) * 9
        + (P(None, w), P(None, w), P(w, None)),
        out_specs=(rows, rows, P(w))
        + (P(w, None),) * 7
        + (P(w), P(None, w), P(None, w), P(w, None)),
        check_vma=False,
    )
```

```python
import functools

import jax
import jax.numpy as jnp
from jax import lax
from jax.experimental import pallas as pl
from jax.experimental.pallas import tpu as pltpu
from jax.experimental.layout import Layout, with_layout_constraint
from jax.sharding import PartitionSpec as P

HEADS = 16
HEAD_DIM = 64
Q_RANK = 6
KV_RANK = 2
HALF = HEAD_DIM // 2
MIX = HEADS * KV_RANK
BASE = KV_RANK * HEAD_DIM
FACTORS = 2 * MIX + 2 * BASE
QMIX = HEADS * Q_RANK
QBASE = Q_RANK * HEAD_DIM
QUAD = 4
QUADS = HEADS // QUAD
QW = QUAD * HEAD_DIM
TILE = 128
F32 = jnp.float32
BF16 = jnp.bfloat16
NEG = -1e30
MIB = 1 << 20


def mm(a, b):
    return jnp.dot(a, b, preferred_element_type=F32)


def mm_nt(a, b):
    return lax.dot_general(a, b, (((1,), (1,)), ((), ())), preferred_element_type=F32)


def mm_tn(a, b):
    return lax.dot_general(a, b, (((0,), (0,)), ((), ())), preferred_element_type=F32)


def whole(count):
    return [pl.BlockSpec(memory_space=pltpu.VMEM)] * count


def streamed(shape):
    return pl.BlockSpec(shape, lambda *_, rank=len(shape): (0,) * rank)


def kernel_call(
    kernel, name, outs, scratch, smem, limit, micros, *args, kept=(), far=(), aliases={}
):
    specs = [
        pl.BlockSpec(memory_space=pltpu.SMEM)
        if i < smem
        else streamed(arg.shape)
        if i in far
        else pl.BlockSpec(memory_space=pltpu.VMEM)
        for i, arg in enumerate(args)
    ]
    return pl.pallas_call(
        kernel,
        out_shape=tuple(
            pltpu.HBM(s, t) if i in kept else jax.ShapeDtypeStruct(s, t)
            for i, (s, t) in enumerate(outs)
        ),
        in_specs=specs,
        out_specs=[
            streamed(s) if i in kept else pl.BlockSpec(memory_space=pltpu.VMEM)
            for i, (s, _) in enumerate(outs)
        ],
        scratch_shapes=scratch,
        compiler_params=pltpu.CompilerParams(vmem_limit_bytes=limit * MIB),
        cost_estimate=pl.CostEstimate(
            flops=int(micros * 1e9), transcendentals=0, bytes_accessed=int(micros * 1e6)
        ),
        input_output_aliases=aliases,
        name=name,
    )(
        *(
            pltpu.with_memory_space_constraint(arg, pltpu.HBM) if i in far else arg
            for i, arg in enumerate(args)
        )
    )


def project_kernel(
    x_ref, gain_ref, qh_ref, qb_ref, kh_ref, kb_ref, vh_ref, vb_ref, cos_ref, sin_ref,
    fac_ref, qt_ref, qmix_ref, qbase_ref, normed_ref,
):
    x = x_ref[...].astype(F32)
    scale = lax.rsqrt(jnp.mean(x * x, axis=-1, keepdims=True) + 1e-06)
    normed = (x * scale * gain_ref[...]).astype(BF16)
    normed_ref[...] = normed
    cos = cos_ref[...]
    sin = sin_ref[...]

    def rope(v):
        a, b = v[:HALF], v[HALF:]
        return jnp.concatenate([a * cos - b * sin, a * sin + b * cos], axis=0)

    kb = mm(normed, kb_ref[...]).T
    fac_ref[0:MIX, :] = mm_nt(kh_ref[...], normed).astype(BF16)
    for r in range(KV_RANK):
        at = MIX + r * HEAD_DIM
        fac_ref[at : at + HEAD_DIM, :] = rope(kb[r * HEAD_DIM : (r + 1) * HEAD_DIM]).astype(BF16)
    fac_ref[MIX + BASE : 2 * MIX + BASE, :] = mm_nt(vh_ref[...], normed).astype(BF16)
    fac_ref[2 * MIX + BASE :, :] = mm(normed, vb_ref[...]).T.astype(BF16)
    qmix = mm_nt(qh_ref[...], normed)
    qmix_ref[...] = qmix
    raw = mm(normed, qb_ref[...]).T
    base = [rope(raw[r * HEAD_DIM : (r + 1) * HEAD_DIM]) for r in range(Q_RANK)]
    for r in range(Q_RANK):
        qbase_ref[r * HEAD_DIM : (r + 1) * HEAD_DIM, :] = base[r]
    for h in range(HEADS):
        out = None
        for r in range(Q_RANK):
            part = qmix[h * Q_RANK + r : h * Q_RANK + r + 1, :] * base[r]
            out = part if out is None else out + part
        qt_ref[h * HEAD_DIM : (h + 1) * HEAD_DIM, :] = (
            (out * (1.0 / Q_RANK)).astype(BF16) * (HEAD_DIM ** -0.5)
        ).astype(BF16)


def project(x, gain, weights, cos, sin):
    local, d = x.shape
    width = HEADS * HEAD_DIM
    return kernel_call(
        project_kernel,
        "project",
        (
            ((FACTORS, local), BF16),
            ((width, local), BF16),
            ((QMIX, local), F32),
            ((QBASE, local), F32),
            ((local, d), BF16),
        ),
        [],
        0,
        16,
        2,
        x, gain, *weights, cos, sin,
        kept=(1, 2, 3, 4),
    )


def materialize(fac, offset, head):
    base = offset + MIX
    out = None
    for r in range(KV_RANK):
        row = offset + head * KV_RANK + r
        part = fac[row : row + 1, :] * fac[base + r * HEAD_DIM : base + (r + 1) * HEAD_DIM, :]
        out = part if out is None else out + part
    return (out * (1.0 / KV_RANK)).astype(BF16)


def materialize_quad(fac, offset, quad):
    return jnp.concatenate(
        [materialize(fac, offset, quad * QUAD + i) for i in range(QUAD)], axis=0
    )


def each_block(me, lo, hi, slots, do):
    for slot in range(slots):
        kb = jnp.bitwise_xor(me, slot)
        pl.when((kb >= lo) & (kb < hi))(functools.partial(do, slot, kb))


def block_factors(slot, near, far):
    return (far if slot & 1 else near)[slot >> 1].astype(F32)


def forward_kernel(
    span, qt_ref, near_ref, far_ref, info_ref, x_ref, wo_ref, gain_ref,
    mixed_ref, out_t_ref, lse_ref, hidden_ref, n2_ref,
    k_s, vt_s, qbd_s, acc_s, m_s, l_s, bias_s,
):
    slots, kb_size, _ = k_s.shape
    count = qt_ref.shape[1]
    lo, hi, me = span[0], span[1], span[2]

    def prepare(slot, kb):
        fac = block_factors(slot, near_ref, far_ref)
        for quad in range(QUADS):
            rows = slice(quad * QW, (quad + 1) * QW)
            k_s[kb, :, rows] = materialize_quad(fac, 0, quad).T
            vt_s[kb, rows, :] = materialize_quad(fac, MIX + BASE, quad)

    each_block(me, lo, hi, slots, prepare)
    qbd_s[...] = jnp.zeros_like(qbd_s)
    for h in range(HEADS):
        quad, i = h // QUAD, h % QUAD
        qbd_s[quad, i * HEAD_DIM : (i + 1) * HEAD_DIM, i * count : (i + 1) * count] = qt_ref[
            h * HEAD_DIM : (h + 1) * HEAD_DIM, :
        ]
    m_s[...] = jnp.full_like(m_s, NEG)
    l_s[...] = jnp.zeros_like(l_s)
    acc_s[...] = jnp.zeros_like(acc_s)
    first = info_ref[0:1, :]
    last = info_ref[1:2, :]

    def step(kb, _):
        places = kb * kb_size + lax.broadcasted_iota(jnp.int32, (kb_size, count), 0)
        bias_s[...] = jnp.where((places >= first) & (places <= last), 0.0, NEG)
        for quad in range(QUADS):
            s = mm(k_s[kb, :, quad * QW : (quad + 1) * QW], qbd_s[quad])
            ps = []
            alphas = []
            for i in range(QUAD):
                h = quad * QUAD + i
                sh = s[:, i * count : (i + 1) * count] + bias_s[...]
                old = m_s[h : h + 1, :]
                new = jnp.maximum(old, jnp.max(sh, axis=0, keepdims=True))
                alpha = jnp.exp(old - new)
                p = jnp.exp(sh - new)
                m_s[h : h + 1, :] = new
                l_s[h : h + 1, :] = l_s[h : h + 1, :] * alpha + jnp.sum(p, axis=0, keepdims=True)
                ps.append(p.astype(BF16))
                alphas.append(alpha)
            for j in range(QUAD // 2):
                both = jnp.concatenate(ps[2 * j : 2 * j + 2], axis=1)
                at = quad * QW + j * 2 * HEAD_DIM
                o = mm(vt_s[kb, at : at + 2 * HEAD_DIM, :], both)
                for i in range(2):
                    r = slice(at + i * HEAD_DIM, at + (i + 1) * HEAD_DIM)
                    acc_s[r, :] = (
                        acc_s[r, :] * alphas[2 * j + i]
                        + o[i * HEAD_DIM : (i + 1) * HEAD_DIM, i * count : (i + 1) * count]
                    )
        return 0

    lax.fori_loop(lo, hi, step, 0)
    lse_ref[...] = m_s[...] + jnp.log(l_s[...])
    for h in range(HEADS):
        rows = slice(h * HEAD_DIM, (h + 1) * HEAD_DIM)
        out_t_ref[rows, :] = acc_s[rows, :] * (1.0 / l_s[h : h + 1, :])

    mixed = out_t_ref[...].astype(BF16).T
    mixed_ref[...] = mixed
    hidden = x_ref[...].astype(F32) + mm(mixed, wo_ref[...])
    hidden_ref[...] = hidden
    scale = lax.rsqrt(jnp.mean(hidden * hidden, axis=-1, keepdims=True) + 1e-06)
    n2_ref[...] = (hidden * scale * gain_ref[...]).astype(BF16)


def attend_forward(span, qt, near, far, info, x, wo, gain):
    width, local = qt.shape
    kb = local
    blocks = 2 * near.shape[0]
    d = x.shape[1]
    return kernel_call(
        forward_kernel,
        "attend_forward",
        (
            ((local, width), BF16),
            ((width, local), F32),
            ((HEADS, local), F32),
            ((local, d), F32),
            ((local, d), BF16),
        ),
        [
            pltpu.VMEM((blocks, kb, width), BF16),
            pltpu.VMEM((blocks, width, kb), BF16),
            pltpu.VMEM((QUADS, QW, QUAD * local), BF16),
            pltpu.VMEM((width, local), F32),
            pltpu.VMEM((HEADS, local), F32),
            pltpu.VMEM((HEADS, local), F32),
            pltpu.VMEM((kb, local), F32),
        ],
        1,
        32,
        10,
        span, qt, near, far, info, x, wo, gain,
        kept=(0, 1, 2, 3),
    )


def ffn_kernel(first, final, *refs):
    at_y, n2_ref, up_ref, w_ref = refs[:4]
    prev = None if first else refs[4]
    sng_ref, branch_ref, sums = refs[-3:]
    n2 = n2_ref[...]
    up = up_ref[...]
    hid = w_ref.shape[1]
    gate = mm_nt(n2, w_ref[0])
    lifted = mm_nt(n2, w_ref[1])
    hidden_grad = mm_nt(up, w_ref[2])
    sigmoid = jax.nn.sigmoid(gate)
    silu = gate * sigmoid
    act = (silu * lifted).astype(BF16)
    gate_grad = (hidden_grad * lifted * (sigmoid * (1.0 + gate * (1.0 - sigmoid)))).astype(BF16)
    lift_grad = (hidden_grad * silu).astype(BF16)
    sng_ref[...] = (mm(gate_grad, w_ref[0]) + mm(lift_grad, w_ref[1])).astype(BF16)
    branch_ref[...] = mm(act, w_ref[2]).astype(BF16)
    for at, (left, right) in enumerate(((act, up), (gate_grad, n2), (lift_grad, n2))):
        grad = mm_tn(left, right)
        if not first:
            grad = grad + prev[at]
        if not final:
            sums[at] = grad
        else:
            half = hid // 2
            low = grad.astype(BF16)
            sums[at_y[0], at] = low[:half]
            sums[1 - at_y[0], at] = low[half:]


def feed_forward(at_y, n2, up, weights, prev=None, final=False):
    count, d = n2.shape
    hid = weights.shape[1]
    if final:
        grads = (((2, 3, hid // 2, d), BF16),)
    else:
        grads = ((weights.shape, F32),)
    args = (at_y, n2, up, weights) if prev is None else (at_y, n2, up, weights, prev)
    return kernel_call(
        functools.partial(ffn_kernel, prev is None, final),
        "feed_forward",
        (((count, d), BF16),) * 2 + grads,
        [],
        1,
        19,
        0.05,
        *args,
        kept=(1, 2) if final else (1,),
        aliases={} if prev is None or final else {4: 2},
    )


def residual_kernel(
    sa, sb, up_ref, hidden_ref, gain_ref, wo_ref, out_t_ref,
    res_ref, low_ref, dot_ref, delta_ref, gain_out,
):
    sng = sa[...].astype(F32) + sb[...].astype(F32)
    hidden = hidden_ref[...]
    scale = lax.rsqrt(jnp.mean(hidden * hidden, axis=-1, keepdims=True) + 1e-06)
    gain_out[...] = jnp.sum(sng * (hidden * scale), axis=0, keepdims=True)
    weighted = sng * gain_ref[...]
    inner = jnp.mean(hidden * weighted, axis=-1, keepdims=True)
    res = up_ref[...].astype(F32) + scale * weighted - hidden * (scale * scale * scale) * inner
    res_ref[...] = res
    low = res.astype(BF16)
    low_ref[...] = low
    dot = mm_nt(wo_ref[...], low).astype(BF16)
    dot_ref[...] = dot
    for h in range(HEADS):
        rows = slice(h * HEAD_DIM, (h + 1) * HEAD_DIM)
        delta_ref[h : h + 1, :] = jnp.sum(
            dot[rows].astype(F32) * out_t_ref[rows, :], axis=0, keepdims=True
        )


def residual(sa, sb, up, hidden, gain, wo, out_t, far=()):
    local, d = hidden.shape
    width = out_t.shape[0]
    return kernel_call(
        residual_kernel,
        "residual",
        (
            ((local, d), F32),
            ((local, d), BF16),
            ((width, local), BF16),
            ((HEADS, local), F32),
            ((1, d), F32),
        ),
        [],
        0,
        16,
        3,
        sa, sb, up, hidden, gain, wo, out_t,
        kept=(0, 2, 3),
        far=far,
    )


def backward_kernel(
    span, qt_ref, near_ref, far_ref, info_ref, dot_ref, lse_ref, delta_ref,
    qmix_ref, qbase_ref, cos_ref, sin_ref,
    dnear_ref, dfar_ref, dq_ref,
    k_s, kt_s, vt_s, dkt_s, dvt_s, qbd_s, qbdt_s, obd_s, obdt_s, dq_s, bias_s, lse_s, delta_s,
):
    slots, kb_size, _ = k_s.shape
    count = qt_ref.shape[1]
    lo, hi, me = span[0], span[1], span[2]
    dnear_ref[...] = jnp.zeros_like(dnear_ref)
    dfar_ref[...] = jnp.zeros_like(dfar_ref)

    def prepare(slot, kb):
        fac = block_factors(slot, near_ref, far_ref)
        for quad in range(QUADS):
            rows = slice(quad * QW, (quad + 1) * QW)
            kt = materialize_quad(fac, 0, quad)
            kt_s[kb, rows, :] = kt
            k_s[kb, :, rows] = kt.T
            vt_s[kb, rows, :] = materialize_quad(fac, MIX + BASE, quad)
            dkt_s[kb, rows, :] = jnp.zeros((QW, kb_size), F32)
            dvt_s[kb, rows, :] = jnp.zeros((QW, kb_size), F32)

    each_block(me, lo, hi, slots, prepare)
    qbdt_s[...] = jnp.zeros_like(qbdt_s)
    obdt_s[...] = jnp.zeros_like(obdt_s)

    for h in range(HEADS):
        quad, i = h // QUAD, h % QUAD
        to = slice(i * HEAD_DIM, (i + 1) * HEAD_DIM)
        at = slice(i * count, (i + 1) * count)
        rows = slice(h * HEAD_DIM, (h + 1) * HEAD_DIM)
        qbdt_s[quad, to, at] = qt_ref[rows, :]
        obdt_s[quad, to, at] = dot_ref[rows, :]
    for quad in range(QUADS):
        qbd_s[quad] = qbdt_s[quad].T
        obd_s[quad] = obdt_s[quad].T
    lse_t = lse_ref[:, :].T
    delta_t = delta_ref[:, :].T
    for h in range(HEADS):
        lse_s[h] = jnp.broadcast_to(lse_t[:, h : h + 1], (count, TILE))
        delta_s[h] = jnp.broadcast_to(delta_t[:, h : h + 1], (count, TILE))
    dq_s[...] = jnp.zeros_like(dq_s)
    info_t = info_ref[:, :].T
    first = info_t[:, 0:1]
    last = info_t[:, 1:2]

    def step(kb, _):
        places = kb * kb_size + lax.broadcasted_iota(jnp.int32, (count, kb_size), 1)
        bias_s[...] = jnp.where((places >= first) & (places <= last), 0.0, NEG)
        lane = lax.broadcasted_iota(jnp.int32, (count, QW), 1) // HEAD_DIM
        for quad in range(QUADS):
            rows = slice(quad * QW, (quad + 1) * QW)
            s = mm(qbd_s[quad], kt_s[kb, rows, :])
            dp = mm(obd_s[quad], vt_s[kb, rows, :])
            ps = []
            dss = []
            for i in range(QUAD):
                h = quad * QUAD + i
                at = slice(i * count, (i + 1) * count)
                lse = jnp.concatenate([lse_s[h]] * (kb_size // TILE), axis=1)
                delta = jnp.concatenate([delta_s[h]] * (kb_size // TILE), axis=1)
                p = jnp.exp((s[at] + bias_s[...]) - lse)
                ps.append(p.astype(BF16))
                dss.append((p * (dp[at] - delta)).astype(BF16))
            p4 = jnp.concatenate(ps, axis=0)
            ds4 = jnp.concatenate(dss, axis=0)
            dkt_s[kb, rows, :] += mm(qbdt_s[quad], ds4)
            dvt_s[kb, rows, :] += mm(obdt_s[quad], p4)
            dq = mm(ds4, k_s[kb, :, rows])
            out = dq[0:count]
            for i in range(1, QUAD):
                out = jnp.where(lane == i, dq[i * count : (i + 1) * count], out)
            dq_s[:, rows] += out
        return 0

    lax.fori_loop(lo, hi, step, 0)
    dqt = dq_s[...].T * (HEAD_DIM ** -0.5 / Q_RANK)
    qmix = qmix_ref[:, :]
    mixes = []
    for h in range(HEADS):
        part = dqt[h * HEAD_DIM : (h + 1) * HEAD_DIM, :]
        for r in range(Q_RANK):
            mixes.append(
                jnp.sum(
                    part * qbase_ref[r * HEAD_DIM : (r + 1) * HEAD_DIM, :], axis=0, keepdims=True
                )
            )
    dq_ref[:QMIX, :] = jnp.concatenate(mixes, axis=0).astype(BF16)
    cos = cos_ref[...]
    sin = sin_ref[...]
    for r in range(Q_RANK):
        out = None
        for h in range(HEADS):
            row = h * Q_RANK + r
            part = qmix[row : row + 1, :] * dqt[h * HEAD_DIM : (h + 1) * HEAD_DIM, :]
            out = part if out is None else out + part
        upper, lower = out[:HALF], out[HALF:]
        at = QMIX + r * HEAD_DIM
        dq_ref[at : at + HALF, :] = (upper * cos + lower * sin).astype(BF16)
        dq_ref[at + HALF : at + HEAD_DIM, :] = (lower * cos - upper * sin).astype(BF16)

    def fold(slot, kb):
        fac = block_factors(slot, near_ref, far_ref)
        to = dfar_ref if slot & 1 else dnear_ref
        for offset, grad in ((0, dkt_s), (MIX + BASE, dvt_s)):
            outs = [None] * KV_RANK
            mixes = []
            for h in range(HEADS):
                g = grad[kb, h * HEAD_DIM : (h + 1) * HEAD_DIM, :] * (1.0 / KV_RANK)
                for r in range(KV_RANK):
                    at = offset + MIX + r * HEAD_DIM
                    mixes.append(jnp.sum(g * fac[at : at + HEAD_DIM, :], axis=0, keepdims=True))
                    row = offset + h * KV_RANK + r
                    part = fac[row : row + 1, :] * g
                    outs[r] = part if outs[r] is None else outs[r] + part
            to[slot >> 1, offset : offset + MIX, :] = jnp.concatenate(mixes, axis=0).astype(BF16)
            for r in range(KV_RANK):
                at = offset + MIX + r * HEAD_DIM
                to[slot >> 1, at : at + HEAD_DIM, :] = outs[r].astype(BF16)

    each_block(me, lo, hi, slots, fold)


def attend_backward(micros, span, qt, near, far, info, dot, lse, delta, qmix, qbase, cos, sin):
    width, local = qt.shape
    kb = local
    blocks = 2 * near.shape[0]
    return kernel_call(
        backward_kernel,
        "attend_backward",
        (
            (near.shape, BF16),
            (near.shape, BF16),
            ((QMIX + QBASE, local), BF16),
        ),
        [
            pltpu.VMEM((blocks, kb, width), BF16),
            pltpu.VMEM((blocks, width, kb), BF16),
            pltpu.VMEM((blocks, width, kb), BF16),
            pltpu.VMEM((blocks, width, kb), F32),
            pltpu.VMEM((blocks, width, kb), F32),
            pltpu.VMEM((QUADS, QUAD * local, QW), BF16),
            pltpu.VMEM((QUADS, QW, QUAD * local), BF16),
            pltpu.VMEM((QUADS, QUAD * local, QW), BF16),
            pltpu.VMEM((QUADS, QW, QUAD * local), BF16),
            pltpu.VMEM((local, width), F32),
            pltpu.VMEM((local, kb), F32),
            pltpu.VMEM((HEADS, local, TILE), F32),
            pltpu.VMEM((HEADS, local, TILE), F32),
        ],
        1,
        56,
        micros,
        span, qt, near, far, info, dot, lse, delta, qmix, qbase, cos, sin,
        far=(1, 5, 6, 7, 8, 9),
    )


def share_kernel(*refs):
    me = refs[0]
    pieces = (refs[1:5], refs[5:9])
    dqs, coss, sins, normeds, gains = refs[9:11], refs[11:13], refs[13:15], refs[15:17], refs[17:19]
    lows = refs[19:21]
    near_ref, far_ref, all_s = refs[21:]
    query = QMIX + QBASE
    for b in range(2):
        first, second, third, fourth = (piece[...].astype(F32) for piece in pieces[b])
        total = (first + second) + (third + fourth)
        cos = coss[b][...]
        sin = sins[b][...]
        low_ref = lows[b]
        low_ref[:query, :] = dqs[b][...]
        low_ref[query:, :] = total.astype(BF16)
        for r in range(KV_RANK):
            at = MIX + r * HEAD_DIM
            upper, lower = total[at : at + HALF], total[at + HALF : at + HEAD_DIM]
            to = query + at
            low_ref[to : to + HALF, :] = (upper * cos + lower * sin).astype(BF16)
            low_ref[to + HALF : to + HEAD_DIM, :] = (lower * cos - upper * sin).astype(BF16)
    rows = query + FACTORS
    all_s[:rows, :] = mm(
        jnp.concatenate([low[...] for low in lows], axis=1),
        jnp.concatenate([normed[...] for normed in normeds], axis=0),
    )
    all_s[rows:, :] = jnp.concatenate(
        [gains[0][...] + gains[1][...], jnp.zeros((15, gains[0].shape[1]), F32)], axis=0
    )
    width = near_ref.shape[2]
    for is_far, ref in ((0, near_ref), (1, far_ref)):
        for slot in range(ref.shape[0]):
            at = pl.multiple_of(jnp.bitwise_xor(me[0], 2 * slot + is_far) * width, width)
            ref[slot] = all_s[:, pl.ds(at, width)].astype(BF16)


def share(me, pieces0, pieces1, dqs, cosine, sine, normeds, gains, slots):
    local, d = normeds[0].shape
    count = QMIX + QBASE + FACTORS
    return kernel_call(
        share_kernel,
        "share",
        (((count, local), BF16),) * 2 + (((slots // 2, count + 16, d // slots), BF16),) * 2,
        [pltpu.VMEM((count + 16, d), F32)],
        1,
        18,
        0.05,
        me, *pieces0, *pieces1, *dqs, cosine[0], cosine[1], sine[0], sine[1], *normeds, *gains,
        far=tuple(range(1, 17)),
    )


def finish_kernel(*refs):
    low_ref, x_ref, gain_ref, res_ref = refs[:4]
    weights = refs[4:10]
    grad_ref = refs[10]
    low = low_ref[...].T
    grad = None
    at = 0
    for ref in weights:
        if ref.shape[0] == x_ref.shape[1]:
            count = ref.shape[1]
            part = mm_nt(low[:, at : at + count], ref[...])
        else:
            count = ref.shape[0]
            part = mm(low[:, at : at + count], ref[...])
        grad = part if grad is None else grad + part
        at += count
    x = x_ref[...].astype(F32)
    scale = lax.rsqrt(jnp.mean(x * x, axis=-1, keepdims=True) + 1e-06)
    weighted = grad * gain_ref[...]
    inner = jnp.mean(x * weighted, axis=-1, keepdims=True)
    grad_ref[...] = res_ref[...] + (scale * weighted - x * (scale * scale * scale) * inner)


def finish(low, x, gain, res, weights):
    local, d = x.shape
    return kernel_call(
        finish_kernel,
        "finish",
        (((local, d), F32),),
        [],
        0,
        16,
        0.05,
        low, x, gain, res, *weights,
        far=(1, 3, 4, 5, 6, 7, 8, 9),
    )[0]


def output_weight_kernel(core, m0, m1, low0, low1, near_ref, far_ref, all_s):
    all_s[...] = mm_tn(m0[...], low0[...]) + mm_tn(m1[...], low1[...])
    count = near_ref.shape[1]
    for chip in range(near_ref.shape[0]):
        for at, ref in ((core[0], near_ref), (1 - core[0], far_ref)):
            row = pl.multiple_of((2 * chip + at) * count, count)
            ref[chip] = all_s[pl.ds(row, count), :].astype(BF16)


def output_weight_shares(core, mixed, lows, slots):
    width, d = mixed[0].shape[1], lows[0].shape[1]
    return kernel_call(
        output_weight_kernel,
        "output_weight_shares",
        (((slots // 2, width // slots, d), BF16),) * 2,
        [pltpu.VMEM((width, d), F32)],
        1,
        16,
        0.05,
        core, *mixed, *lows,
        far=(1, 2, 3, 4),
    )


def branch_kernel(n0, n1, f0, f1, mine_ref, theirs_ref):
    half = mine_ref.shape[0] // 2
    for b, (near, far) in enumerate(((n0, f0), (n1, f1))):
        total = (near[...].astype(F32) + far[...].astype(F32)).astype(BF16)
        mine_ref[b * half : (b + 1) * half, :] = total[:half]
        theirs_ref[b * half : (b + 1) * half, :] = total[half:]


def branch_sums(nears, fars):
    return kernel_call(
        branch_kernel,
        "branch_sums",
        ((nears[0].shape, BF16),) * 2,
        [],
        0,
        16,
        0.05,
        *nears, *fars,
        kept=(0, 1),
        far=(0, 1, 2, 3),
    )


highest = lax.Precision.HIGHEST
masked_score = -1e30


def rms_scale(values):
    return lax.rsqrt(jnp.mean(values * values, axis=-1, keepdims=True) + 1e-06)


def norm_backward(values, gain, scaled, upstream):
    weighted = upstream * gain
    inner = jnp.mean(values * weighted, axis=-1, keepdims=True)
    return scaled * weighted - values * (scaled * scaled * scaled) * inner


def rotate(values, cosine, sine):
    half = values.shape[-1] // 2
    first = values[..., :half]
    second = values[..., half:]
    return jnp.concatenate(
        [first * cosine - second * sine, first * sine + second * cosine], axis=-1
    )


def row_layout(lengths_row, places):
    ends = jnp.cumsum(lengths_row)
    passed = ends[None, :] <= places[:, None]
    segment = jnp.sum(passed.astype(jnp.int32), axis=1)
    start = jnp.max(jnp.where(passed, ends[None, :], 0), axis=1)
    valid = places < ends[-1]
    return (segment, places - start, valid)


def rope_tables(position):
    half = HEAD_DIM // 2
    frequency = 10000.0 ** (-jnp.arange(half, dtype=jnp.float32) / half)
    angle = position.astype(jnp.float32)[..., None] * frequency
    return (jnp.cos(angle), jnp.sin(angle))


def split_factors(factors):
    mix_width = HEADS * KV_RANK
    base_width = KV_RANK * HEAD_DIM
    count, rows = (factors.shape[0], factors.shape[1])
    key_mix = factors[..., :mix_width].reshape(count, rows, HEADS, KV_RANK)
    key_base = factors[..., mix_width : mix_width + base_width].reshape(
        count, rows, KV_RANK, HEAD_DIM
    )
    value_mix = factors[..., mix_width + base_width : 2 * mix_width + base_width].reshape(
        count, rows, HEADS, KV_RANK
    )
    value_base = factors[..., 2 * mix_width + base_width :].reshape(count, rows, KV_RANK, HEAD_DIM)
    return (key_mix, key_base, value_mix, value_base)


def pair_gradient(hidden_grad, gate, lifted):
    sigmoid = jax.nn.sigmoid(gate)
    gate_grad = hidden_grad * lifted * (sigmoid * (1.0 + gate * (1.0 - sigmoid)))
    lift_grad = hidden_grad * (gate * sigmoid)
    return jnp.concatenate([gate_grad, lift_grad], axis=-1).astype(jnp.bfloat16)


def general_body(
    tokens,
    lengths,
    cotangent,
    first_gain,
    query_heads,
    query_basis,
    key_heads,
    key_basis,
    value_heads,
    value_basis,
    output_weight,
    second_gain,
    gate_weight,
    up_weight,
    down_projection_weight,
):
    local, batch_rows, width = tokens.shape
    total = local * lax.axis_size("wide")
    offset = lax.axis_index("wide") * local
    places = jnp.arange(total, dtype=jnp.int32)
    segment, position, valid = jax.vmap(row_layout, in_axes=(0, None))(lengths, places)
    own_places = offset + jnp.arange(local, dtype=jnp.int32)
    own_segment = lax.dynamic_slice_in_dim(segment, offset, local, 1)
    own_position = lax.dynamic_slice_in_dim(position, offset, local, 1)
    own_valid = lax.dynamic_slice_in_dim(valid, offset, local, 1)
    cosine, sine = rope_tables(jnp.transpose(own_position))
    cosine = cosine[:, :, None, :]
    sine = sine[:, :, None, :]
    keep_rows = jnp.transpose(own_valid)[:, :, None]
    scale = HEAD_DIM ** (-0.5)
    block_rows = min(512, total)
    block_count = total // block_rows
    mix_width = HEADS * KV_RANK
    base_width = KV_RANK * HEAD_DIM
    flat_rows = local * batch_rows
    inputs = tokens.astype(jnp.float32)
    first_scale = rms_scale(inputs)
    normed = (inputs * first_scale * first_gain).astype(jnp.bfloat16)
    flat = normed.reshape(flat_rows, width)
    query_mix = jnp.dot(flat, query_heads, preferred_element_type=jnp.float32).reshape(
        local, batch_rows, HEADS, Q_RANK
    )
    query_raw = jnp.dot(flat, query_basis, preferred_element_type=jnp.float32).reshape(
        local, batch_rows, Q_RANK, HEAD_DIM
    )
    query_base = rotate(query_raw, cosine, sine)
    factor_weight = jnp.concatenate([key_heads, key_basis, value_heads, value_basis], axis=1)
    factor_raw = jnp.dot(flat, factor_weight, preferred_element_type=jnp.float32).reshape(
        local, batch_rows, -1
    )
    key_roped = rotate(
        factor_raw[..., mix_width : mix_width + base_width].reshape(
            local, batch_rows, KV_RANK, HEAD_DIM
        ),
        cosine,
        sine,
    ).reshape(local, batch_rows, base_width)
    factors = jnp.concatenate(
        [factor_raw[..., :mix_width], key_roped, factor_raw[..., mix_width + base_width :]], axis=-1
    ).astype(jnp.bfloat16)
    every = lax.all_gather(factors, "wide", axis=0, tiled=True)
    key_mix, key_base, value_mix, value_base = split_factors(every)
    keys = (
        jnp.einsum("trhk,trkd->trhd", key_mix, key_base, preferred_element_type=jnp.float32)
        / KV_RANK
    ).astype(jnp.bfloat16)
    values = (
        jnp.einsum("trhk,trkd->trhd", value_mix, value_base, preferred_element_type=jnp.float32)
        / KV_RANK
    ).astype(jnp.bfloat16)
    query = (
        jnp.einsum(
            "trhk,trkd->trhd",
            query_mix,
            query_base,
            precision=highest,
            preferred_element_type=jnp.float32,
        )
        / Q_RANK
    ).astype(jnp.bfloat16)

    def block_view(block):
        start = block * block_rows
        key_places = start + jnp.arange(block_rows, dtype=jnp.int32)
        key_segment = lax.dynamic_slice_in_dim(segment, start, block_rows, 1)
        key_valid = lax.dynamic_slice_in_dim(valid, start, block_rows, 1)
        causal = key_places[None, :] <= own_places[:, None]
        itself = key_places[None, :] == own_places[:, None]
        allowed = (
            causal[None]
            & (own_segment[:, :, None] == key_segment[:, None, :])
            & (key_valid[:, None, :] | itself[None])
        )
        key_block = lax.dynamic_slice_in_dim(keys, start, block_rows, 0)
        value_block = lax.dynamic_slice_in_dim(values, start, block_rows, 0)
        product = (
            jnp.einsum("qrhd,krhd->rhqk", query, key_block, preferred_element_type=jnp.float32)
            * scale
        )
        scores = jnp.where(allowed[:, None], product, masked_score)
        return (start, scores, key_block, value_block)

    def max_step(carry, block):
        top, mass = carry
        scores = block_view(block)[1]
        higher = jnp.maximum(top, jnp.max(scores, axis=-1))
        mass = mass * jnp.exp(top - higher) + jnp.sum(jnp.exp(scores - higher[..., None]), axis=-1)
        return ((higher, mass), None)

    start_top = jnp.full((batch_rows, HEADS, local), masked_score, jnp.float32)
    (top, mass), _ = lax.scan(
        max_step, (start_top, jnp.zeros_like(start_top)), jnp.arange(block_count)
    )
    log_total = top + jnp.log(mass)

    def out_step(carry, block):
        _, scores, _, value_block = block_view(block)
        chances = jnp.exp(scores - log_total[..., None]).astype(jnp.bfloat16)
        return (
            carry
            + jnp.einsum(
                "rhqk,krhd->qrhd", chances, value_block, preferred_element_type=jnp.float32
            ),
            None,
        )

    attended, _ = lax.scan(
        out_step,
        jnp.zeros((local, batch_rows, HEADS, HEAD_DIM), jnp.float32),
        jnp.arange(block_count),
    )
    mixed = attended.astype(jnp.bfloat16).reshape(flat_rows, HEADS * HEAD_DIM)
    hidden_state = inputs + jnp.dot(
        mixed, output_weight, preferred_element_type=jnp.float32
    ).reshape(local, batch_rows, width)
    second_scale = rms_scale(hidden_state)
    normed_second = (hidden_state * second_scale * second_gain).astype(jnp.bfloat16)
    normalized_token_rows = lax.all_gather(normed_second, "wide", axis=0, tiled=True)
    gate_lifted_hidden = jnp.concatenate([gate_weight, up_weight], axis=1)
    hidden_width = gate_weight.shape[1]
    projected_output = jnp.einsum(
        "zec,cx->zex", normalized_token_rows, gate_lifted_hidden, preferred_element_type=jnp.float32
    )
    gate = projected_output[..., :hidden_width]
    lifted = projected_output[..., hidden_width:]
    silu_hidden_output = (jax.nn.silu(gate) * lifted).astype(jnp.bfloat16)
    sequence_portion = silu_hidden_output
    branch = lax.psum_scatter(
        jnp.einsum(
            "zyu,uv->zyv",
            sequence_portion,
            down_projection_weight,
            preferred_element_type=jnp.float32,
        ).astype(jnp.bfloat16),
        "wide",
        scatter_dimension=0,
        tiled=True,
    ).astype(jnp.float32)
    output = jnp.where(keep_rows, hidden_state + branch, 0.0).astype(jnp.bfloat16)
    upstream = jnp.where(keep_rows, cotangent.astype(jnp.float32), 0.0)
    upstream_low = upstream.astype(jnp.bfloat16)
    upstream_token_gradient = lax.all_gather(upstream_low, "wide", axis=0, tiled=True)
    hidden_grad = jnp.einsum(
        "ajg,vg->ajv",
        upstream_token_gradient,
        down_projection_weight,
        preferred_element_type=jnp.float32,
    )
    pair_product_gradient = pair_gradient(hidden_grad, gate, lifted)
    down_gradient = jnp.einsum(
        "imj,ima->ja",
        silu_hidden_output,
        upstream_token_gradient,
        preferred_element_type=jnp.float32,
    )
    pair_weight_grad = jnp.einsum(
        "ipl,ipj->lj",
        normalized_token_rows,
        pair_product_gradient,
        preferred_element_type=jnp.float32,
    )
    sequence_portion = pair_product_gradient
    second_normed_grad = lax.psum_scatter(
        jnp.einsum(
            "ivu,bu->ivb", sequence_portion, gate_lifted_hidden, preferred_element_type=jnp.float32
        ),
        "wide",
        scatter_dimension=0,
        tiled=True,
    )
    second_gain_partial = jnp.sum(second_normed_grad * (hidden_state * second_scale), axis=(0, 1))
    residual_grad = upstream + norm_backward(
        hidden_state, second_gain, second_scale, second_normed_grad
    )
    residual_low = residual_grad.astype(jnp.bfloat16).reshape(flat_rows, width)
    output_weight_grad = jnp.einsum(
        "tk,td->kd", mixed, residual_low, preferred_element_type=jnp.float32
    )
    mixed_grad = (
        jnp.einsum("td,kd->tk", residual_low, output_weight, preferred_element_type=jnp.float32)
        .astype(jnp.bfloat16)
        .reshape(local, batch_rows, HEADS, HEAD_DIM)
    )

    def delta_step(carry, block):
        _, scores, _, value_block = block_view(block)
        chances = jnp.exp(scores - log_total[..., None])
        pressure = jnp.einsum(
            "qrhd,krhd->rhqk", mixed_grad, value_block, preferred_element_type=jnp.float32
        )
        return (carry + jnp.sum(chances * pressure, axis=-1), None)

    delta, _ = lax.scan(
        delta_step, jnp.zeros((batch_rows, HEADS, local), jnp.float32), jnp.arange(block_count)
    )

    def grad_step(carry, block):
        start, scores, key_block, value_block = block_view(block)
        chances = jnp.exp(scores - log_total[..., None])
        pressure = jnp.einsum(
            "qrhd,krhd->rhqk", mixed_grad, value_block, preferred_element_type=jnp.float32
        )
        score_grad = (chances * (pressure - delta[..., None])).astype(jnp.bfloat16)
        carry = (
            carry
            + jnp.einsum(
                "rhqk,krhd->qrhd", score_grad, key_block, preferred_element_type=jnp.float32
            )
            * scale
        )
        key_grad = (
            jnp.einsum("rhqk,qrhd->krhd", score_grad, query, preferred_element_type=jnp.float32)
            * scale
        )
        value_grad = jnp.einsum(
            "rhqk,qrhd->krhd",
            chances.astype(jnp.bfloat16),
            mixed_grad,
            preferred_element_type=jnp.float32,
        )
        block_mix, block_base, block_vmix, block_vbase = split_factors(
            lax.dynamic_slice_in_dim(every, start, block_rows, 0).astype(jnp.float32)
        )
        key_mix_grad = (
            jnp.einsum("krhd,krcd->krhc", key_grad, block_base, precision=highest) / KV_RANK
        )
        key_base_grad = (
            jnp.einsum("krhc,krhd->krcd", block_mix, key_grad, precision=highest) / KV_RANK
        )
        value_mix_grad = (
            jnp.einsum("krhd,krcd->krhc", value_grad, block_vbase, precision=highest) / KV_RANK
        )
        value_base_grad = (
            jnp.einsum("krhc,krhd->krcd", block_vmix, value_grad, precision=highest) / KV_RANK
        )
        block_grad = jnp.concatenate(
            [
                key_mix_grad.reshape(block_rows, batch_rows, mix_width),
                key_base_grad.reshape(block_rows, batch_rows, base_width),
                value_mix_grad.reshape(block_rows, batch_rows, mix_width),
                value_base_grad.reshape(block_rows, batch_rows, base_width),
            ],
            axis=-1,
        )
        return (carry, block_grad)

    query_grad, factor_blocks = lax.scan(
        grad_step,
        jnp.zeros((local, batch_rows, HEADS, HEAD_DIM), jnp.float32),
        jnp.arange(block_count),
    )
    factor_grads = factor_blocks.reshape(total, batch_rows, 2 * mix_width + 2 * base_width)
    own_factor_grads = lax.psum_scatter(
        factor_grads.astype(jnp.bfloat16), "wide", scatter_dimension=0, tiled=True
    ).astype(jnp.float32)
    key_base_back = rotate(
        own_factor_grads[..., mix_width : mix_width + base_width].reshape(
            local, batch_rows, KV_RANK, HEAD_DIM
        ),
        cosine,
        -sine,
    ).reshape(local, batch_rows, base_width)
    factor_low = (
        jnp.concatenate(
            [
                own_factor_grads[..., :mix_width],
                key_base_back,
                own_factor_grads[..., mix_width + base_width :],
            ],
            axis=-1,
        )
        .astype(jnp.bfloat16)
        .reshape(flat_rows, -1)
    )
    mix_grad = jnp.einsum("trhd,trcd->trhc", query_grad, query_base, precision=highest) / Q_RANK
    base_roped_grad = (
        jnp.einsum("trhc,trhd->trcd", query_mix, query_grad, precision=highest) / Q_RANK
    )
    base_grad = rotate(base_roped_grad, cosine, -sine)
    mix_low = mix_grad.astype(jnp.bfloat16).reshape(flat_rows, HEADS * Q_RANK)
    base_low = base_grad.astype(jnp.bfloat16).reshape(flat_rows, Q_RANK * HEAD_DIM)
    query_heads_grad = jnp.einsum("tk,tf->kf", flat, mix_low, preferred_element_type=jnp.float32)
    query_basis_grad = jnp.einsum("tk,tf->kf", flat, base_low, preferred_element_type=jnp.float32)
    factor_weight_grad = jnp.einsum(
        "tk,tf->kf", flat, factor_low, preferred_element_type=jnp.float32
    )
    first_normed_grad = (
        jnp.einsum("tf,kf->tk", mix_low, query_heads, preferred_element_type=jnp.float32)
        + jnp.einsum("tf,kf->tk", base_low, query_basis, preferred_element_type=jnp.float32)
        + jnp.einsum("tf,kf->tk", factor_low, factor_weight, preferred_element_type=jnp.float32)
    ).reshape(local, batch_rows, width)
    first_gain_partial = jnp.sum(first_normed_grad * (inputs * first_scale), axis=(0, 1))
    tokens_gradient = residual_grad + norm_backward(
        inputs, first_gain, first_scale, first_normed_grad
    )
    key_heads_grad = factor_weight_grad[:, :mix_width]
    key_basis_grad = factor_weight_grad[:, mix_width : mix_width + base_width]
    value_heads_grad = factor_weight_grad[:, mix_width + base_width : 2 * mix_width + base_width]
    value_basis_grad = factor_weight_grad[:, 2 * mix_width + base_width :]
    (
        first_share,
        qheads_share,
        qbasis_share,
        kheads_share,
        kbasis_share,
        vheads_share,
        vbasis_share,
        output_share,
        second_share,
    ) = (
        lax.psum_scatter(
            first_gain_partial.astype(jnp.bfloat16), "wide", scatter_dimension=0, tiled=True
        ).astype(jnp.float32),
        lax.psum_scatter(
            query_heads_grad.astype(jnp.bfloat16), "wide", scatter_dimension=0, tiled=True
        ).astype(jnp.float32),
        lax.psum_scatter(
            query_basis_grad.astype(jnp.bfloat16), "wide", scatter_dimension=0, tiled=True
        ).astype(jnp.float32),
        lax.psum_scatter(
            key_heads_grad.astype(jnp.bfloat16), "wide", scatter_dimension=0, tiled=True
        ).astype(jnp.float32),
        lax.psum_scatter(
            key_basis_grad.astype(jnp.bfloat16), "wide", scatter_dimension=0, tiled=True
        ).astype(jnp.float32),
        lax.psum_scatter(
            value_heads_grad.astype(jnp.bfloat16), "wide", scatter_dimension=0, tiled=True
        ).astype(jnp.float32),
        lax.psum_scatter(
            value_basis_grad.astype(jnp.bfloat16), "wide", scatter_dimension=0, tiled=True
        ).astype(jnp.float32),
        lax.psum_scatter(
            output_weight_grad.astype(jnp.bfloat16), "wide", scatter_dimension=0, tiled=True
        ).astype(jnp.float32),
        lax.psum_scatter(
            second_gain_partial.astype(jnp.bfloat16), "wide", scatter_dimension=0, tiled=True
        ).astype(jnp.float32),
    )
    gate_share = pair_weight_grad[:, :hidden_width]
    lift_share = pair_weight_grad[:, hidden_width:]
    totals = (
        lax.psum(first_share.astype(jnp.bfloat16), "batch").astype(jnp.float32),
        lax.psum(qheads_share.astype(jnp.bfloat16), "batch").astype(jnp.float32),
        lax.psum(qbasis_share.astype(jnp.bfloat16), "batch").astype(jnp.float32),
        lax.psum(kheads_share.astype(jnp.bfloat16), "batch").astype(jnp.float32),
        lax.psum(kbasis_share.astype(jnp.bfloat16), "batch").astype(jnp.float32),
        lax.psum(vheads_share.astype(jnp.bfloat16), "batch").astype(jnp.float32),
        lax.psum(vbasis_share.astype(jnp.bfloat16), "batch").astype(jnp.float32),
        lax.psum(output_share.astype(jnp.bfloat16), "batch").astype(jnp.float32),
        lax.psum(second_share.astype(jnp.bfloat16), "batch").astype(jnp.float32),
        lax.psum(gate_share.astype(jnp.bfloat16), "batch").astype(jnp.float32),
        lax.psum(lift_share.astype(jnp.bfloat16), "batch").astype(jnp.float32),
        lax.psum(down_gradient.astype(jnp.bfloat16), "batch").astype(jnp.float32),
    )
    return (
        output,
        tokens_gradient,
        totals[0],
        totals[1],
        totals[2],
        totals[3],
        totals[4],
        totals[5],
        totals[6],
        totals[7],
        totals[8],
        totals[9],
        totals[10],
        totals[11],
    )


def partners(distance, count):
    return [(i, i ^ distance) for i in range(count)]


def fence(*values):
    return lax.optimization_barrier(values)


def after(value, *others):
    return lax.optimization_barrier((value,) + others)[0]


def in_order(value):
    return with_layout_constraint(value, Layout(tuple(range(value.ndim))))


def body(
    tokens,
    lengths,
    cotangent,
    first_gain,
    query_heads,
    query_basis,
    key_heads,
    key_basis,
    value_heads,
    value_basis,
    output_weight,
    second_gain,
    gate_weight,
    up_weight,
    down_projection_weight,
):
    local, rows, width = tokens.shape
    wide = ("y", "x", "core")
    n = lax.axis_size(wide)
    depth = lax.axis_size("batch")
    me = lax.axis_index(wide).astype(jnp.int32)
    at_y = lax.axis_index("y").astype(jnp.int32).reshape(1)

    def swap(value, distance):
        return lax.ppermute(value, wide, partners(distance, n))

    def swap_batch(value, distance):
        return lax.ppermute(value, "batch", partners(distance, depth))

    core, across, along, diagonal = 1, 2, 4, 6
    chips = (across, along, diagonal)

    def send_chips(value):
        return [swap(value, distance) for distance in chips]

    def send_slots(sums):
        return [swap(sums[i + 1], chips[i]) for i in range(len(chips))]

    def add(*values):
        return sum(value.astype(F32) for value in values).astype(BF16)

    places = me * local + jnp.arange(local, dtype=jnp.int32)
    slots = lengths.shape[1]
    upto = jnp.arange(slots)[:, None] >= jnp.arange(slots)[None, :]
    ends = jnp.sum(jnp.where(upto[None], lengths[:, None, :], 0), axis=2)
    passed = ends[:, None, :] <= places[None, :, None]
    start = jnp.max(jnp.where(passed, ends[:, None, :], 0), axis=2)
    valid = places[None, :] < ends[:, -1:]
    position = places[None, :] - start
    first_seen = jnp.where(valid, start, places[None, :])
    frequency = 10000.0 ** (-jnp.arange(HALF, dtype=F32) / HALF)
    angle = position.astype(F32)[:, None, :] * frequency[None, :, None]
    cosine, sine = jnp.cos(angle), jnp.sin(angle)
    info = jnp.stack([first_seen, jnp.broadcast_to(places, (rows, local))], axis=1)
    info = jnp.concatenate([info, jnp.zeros((rows, 6, local), jnp.int32)], axis=1)
    spans = jnp.stack(
        [
            jnp.min(first_seen, axis=1) // local,
            jnp.broadcast_to(me + 1, (rows,)),
            jnp.broadcast_to(me, (rows,)),
        ],
        axis=1,
    ).astype(jnp.int32)

    gain1 = first_gain.reshape(1, width)
    gain2 = second_gain.reshape(1, width)
    projections = (query_heads, query_basis, key_heads, key_basis, value_heads, value_basis)
    narrow = tuple(w.T if w.shape[1] < TILE else w for w in projections)

    xs = [tokens[:, b, :] for b in range(rows)]
    projected = [project(xs[0], gain1, narrow, cosine[0], sine[0])]
    sent0 = send_chips(projected[0][0])
    x1 = after(xs[1], projected[0][0])
    projected.append(project(x1, gain1, narrow, cosine[1], sine[1]))
    sent1 = send_chips(projected[1][0])
    own_weights = jnp.stack(
        [after(gate_weight.T, projected[1][0]), up_weight.T, down_projection_weight]
    )
    other_weights = swap(own_weights, along)
    near = jnp.stack([projected[0][0]] + [after(got, own_weights) for got in sent0])
    far = swap(near, core)
    gathered = [(near, far)]
    seen = after(valid, near)
    ups = [jnp.where(seen[b][:, None], cotangent[:, b, :], 0) for b in range(rows)]
    up_pair = jnp.concatenate(ups, axis=0)
    up_got = swap(up_pair, across)

    def forward(b):
        outs = attend_forward(
            spans[b], projected[b][1], *gathered[b], info[b], xs[b], output_weight, gain2
        )
        return outs[:4], outs[4]

    gathered[0] = (near, after(far, up_pair))
    kept0, n20 = forward(0)
    n20, up_got, *sent1 = fence(n20, up_got, *sent1)
    n2_sent0 = swap(n20, across)
    near = jnp.stack([projected[1][0]] + list(sent1))
    far = swap(near, core)
    up_near = [
        jnp.concatenate([ups[b], up_got[b * local : (b + 1) * local]], axis=0)
        for b in range(rows)
    ]
    near, far, *up_near = fence(near, far, *up_near)
    gathered.append((near, far))
    up_far = [swap(up_near[b], core) for b in range(rows)]
    kept1, n21 = forward(1)
    n2_sent1 = swap(n21, across)
    n21, up_far0, up_far1, n2_sent0, other_weights = fence(
        n21, *up_far, n2_sent0, other_weights
    )
    weights = jnp.concatenate([own_weights, other_weights], axis=1)
    attended = (kept0, kept1)

    near0 = jnp.concatenate([n20, n2_sent0], axis=0)
    far0 = swap(near0, core)
    sn0, bn0, grads = feed_forward(at_y, near0, up_near[0], weights)
    sn0, bn0, grads, n2_sent1, far0 = fence(sn0, bn0, grads, n2_sent1, far0)
    near1 = jnp.concatenate([n21, n2_sent1], axis=0)
    far1 = swap(near1, core)
    sf0, bf0, grads = feed_forward(at_y, after(far0, near1), up_far0, weights, grads)
    sf0, bf0, grads, far1 = fence(sf0, bf0, grads, far1)
    sf0_got = swap(sf0, core)
    sn1, bn1, grads = feed_forward(at_y, near1, up_near[1], weights, grads)
    sn1, bn1, grads, sf0_got = fence(sn1, bn1, grads, sf0_got)
    sum0 = add(sn0, sf0_got)
    theirs = sum0[local:]
    across0 = swap(theirs, across)
    sf1, bf1, grads = feed_forward(
        at_y, after(far1, theirs), up_far1, weights, grads, True
    )
    sf1, bf1, grads, across0 = fence(sf1, bf1, grads, across0)
    block_part = lax.psum_scatter(
        grads.reshape(-1, width), ("y", "batch"), scatter_dimension=0, tiled=True
    )

    def residual_of(b, mine, got):
        mixed, out_t, lse, hidden = attended[b]
        return residual(
            mine, got, ups[b], hidden, gain2, output_weight, out_t, (0, 1, 2, 3, 5, 6)
        )

    sf1_got = swap(sf1, core)
    residual0 = residual_of(0, sum0[:local], across0)
    *residual0, sf1_got = fence(*residual0, sf1_got)
    sum1 = add(sn1, sf1_got)
    theirs = sum1[local:]

    def back(b, outs, *hold):
        res, low, dot, delta, gain_share = outs
        fac, qt, qmix, qbase, normed = projected[b]
        return attend_backward(
            (40, 0.1)[b], spans[b], qt, *gathered[b], info[b], after(dot, *hold), attended[b][2], delta,
            qmix, qbase, cosine[b], sine[b],
        )

    across1 = swap(theirs, across)
    bf_got = [swap(value, core) for value in (bf0, bf1)]
    dnear0, dfar0, dq0 = back(0, residual0, theirs)
    dnear0, dfar0, dq0, across1, *bf_got = fence(dnear0, dfar0, dq0, across1, *bf_got)
    dfar0_got = swap(dfar0, core)
    residual1 = residual_of(1, sum1[:local], across1)
    *residual1, dnear0, dfar0_got = fence(*residual1, dnear0, dfar0_got)
    residuals = (residual0, residual1)
    fsum0 = add(dnear0, dfar0_got)
    fparts0 = send_slots(fsum0)
    dnear1, dfar1, dq1 = back(1, residual1, fsum0)
    dnear1, dfar1, dq1, *fparts0 = fence(dnear1, dfar1, dq1, *fparts0)

    dfar1_got = swap(dfar1, core)
    dfar1_got, dnear1 = fence(dfar1_got, dnear1)
    fsum1 = add(dnear1, dfar1_got)
    fparts1 = send_slots(fsum1)
    wo_near, wo_far = output_weight_shares(
        lax.axis_index("core").astype(jnp.int32).reshape(1),
        [after(attended[0][0], fsum1), attended[1][0]],
        [residuals[b][1] for b in range(rows)],
        n,
    )
    wo_got = swap(wo_far, core)
    branch_mine, branch_theirs = branch_sums([after(bn0, wo_near), bn1], bf_got)
    block_part, fsum1, wo_near, branch_mine, branch_theirs = fence(
        block_part, fsum1, wo_near, branch_mine, branch_theirs
    )
    block_grad = lax.all_gather(block_part, "batch", axis=0, tiled=True)
    *fparts1, fsum1, wo_got = fence(*fparts1, fsum1, wo_got)
    low0, low1, near, far = share(
        me.reshape(1),
        [fsum0[0]] + list(fparts0),
        [fsum1[0]] + list(fparts1),
        (dq0, dq1),
        cosine,
        sine,
        [projected[b][4] for b in range(rows)],
        (residual0[4], residual1[4]),
        n,
    )
    far_got = swap(far, core)
    far_got, near = fence(far_got, near)
    small = add(near, far_got)
    small_sent = send_slots(small)
    wo_sum = add(wo_near, after(wo_got, small))
    wo_parts = lax.all_to_all(wo_sum, ("y", "x"), 0, 0, tiled=True)
    *small_sent, small = fence(*small_sent, small)
    small = add(small[0], *small_sent)
    small_got = swap_batch(small, 1)
    branch_got = swap(after(branch_theirs, small), across)
    grads = [
        finish(after((low0, low1)[b], small), xs[b], gain1, residuals[b][0], narrow)
        for b in range(rows)
    ]
    tokens_gradient = in_order(jnp.stack(grads, axis=1))
    columns = jnp.concatenate(
        [
            lax.dynamic_slice_in_dim(w, after(me, small) * (width // n), width // n, 0)
            for w in projections
        ],
        axis=1,
    ).astype(F32).T
    small_got, small, wo_parts, tokens_gradient, columns = fence(
        small_got, small, wo_parts, tokens_gradient, columns
    )
    small = add(small, small_got)
    small_got = swap_batch(small, depth - 1)
    wo_total = jnp.sum(after(wo_parts, small).astype(F32), axis=0).astype(BF16)
    wo_got = swap_batch(wo_total, 1)
    wo_got, wo_total, branch_got, block_grad = fence(wo_got, wo_total, branch_got, block_grad)
    wo_total = add(wo_total, wo_got)
    wo_got = swap_batch(wo_total, depth - 1)
    outputs = []
    for b in range(rows):
        mine = branch_mine[b * local : (b + 1) * local].astype(F32)
        got = after(branch_got, wo_total)[b * local : (b + 1) * local].astype(F32)
        outputs.append(
            jnp.where(valid[b][:, None], attended[b][3] + (mine + got), 0.0).astype(BF16)
        )
    output = in_order(jnp.stack(outputs, axis=1))
    small_got, output = fence(small_got, output)
    small = small.astype(F32) + small_got.astype(F32)
    hid = gate_weight.shape[1]
    down_grad = block_grad[:hid].astype(F32)
    gate_grad = block_grad[hid : 2 * hid].astype(F32).T
    lift_grad = block_grad[2 * hid :].astype(F32).T
    output_weight_grad = wo_total.astype(F32) + after(wo_got, small).astype(F32)
    count = width // n

    def pick(at, size):
        return small[at : at + size].T

    query_heads_grad = pick(0, QMIX)
    query_basis_grad = pick(QMIX, QBASE)
    at = QMIX + QBASE
    key_heads_grad = pick(at, MIX)
    key_basis_grad = pick(at + MIX, BASE)
    value_heads_grad = pick(at + MIX + BASE, MIX)
    value_basis_grad = pick(at + 2 * MIX + BASE, BASE)
    at = at + FACTORS
    second_gain_grad = small[at].reshape(count)
    weighted = small[:at] * columns
    own_gain = lax.dynamic_slice_in_dim(first_gain, me * count, count, 0)
    first_gain_grad = jnp.sum(weighted, axis=0) / own_gain

    return (
        output,
        tokens_gradient,
        first_gain_grad,
        query_heads_grad,
        query_basis_grad,
        key_heads_grad,
        key_basis_grad,
        value_heads_grad,
        value_basis_grad,
        output_weight_grad,
        second_gain_grad,
        gate_grad,
        lift_grad,
        down_grad,
    )


def solution(mesh):
    batch, wide = mesh.shape["batch"], mesh.shape["wide"]
    split = wide == 8 and batch == 4
    w = "wide"
    if split:
        mesh = jax.sharding.Mesh(
            mesh.devices.reshape(batch, 2, 2, 2), ("batch", "y", "x", "core")
        )
        w = ("y", "x", "core")
    rows = P(w, "batch", None)
    return jax.shard_map(
        body if split else general_body,
        mesh=mesh,
        in_specs=(rows, P("batch", None), rows)
        + (P(),) * 9
        + (P(None, w), P(None, w), P(w, None)),
        out_specs=(rows, rows, P(w))
        + (P(w, None),) * 7
        + (P(w), P(None, w), P(None, w), P(w, None)),
        check_vma=False,
    )
```

```python
import functools

import jax
import jax.numpy as jnp
from jax import lax
from jax.experimental import pallas as pl
from jax.experimental.pallas import tpu as pltpu
from jax.experimental.layout import Layout, with_layout_constraint
from jax.sharding import PartitionSpec as P

HEADS = 16
HEAD_DIM = 64
Q_RANK = 6
KV_RANK = 2
HALF = HEAD_DIM // 2
MIX = HEADS * KV_RANK
BASE = KV_RANK * HEAD_DIM
FACTORS = 2 * MIX + 2 * BASE
QMIX = HEADS * Q_RANK
QBASE = Q_RANK * HEAD_DIM
QUAD = 4
QUADS = HEADS // QUAD
QW = QUAD * HEAD_DIM
TILE = 128
F32 = jnp.float32
BF16 = jnp.bfloat16
NEG = -1e30
MIB = 1 << 20


def mm(a, b):
    return jnp.dot(a, b, preferred_element_type=F32)


def mm_nt(a, b):
    return lax.dot_general(a, b, (((1,), (1,)), ((), ())), preferred_element_type=F32)


def mm_tn(a, b):
    return lax.dot_general(a, b, (((0,), (0,)), ((), ())), preferred_element_type=F32)


def whole(count):
    return [pl.BlockSpec(memory_space=pltpu.VMEM)] * count


def streamed(shape):
    return pl.BlockSpec(shape, lambda *_, rank=len(shape): (0,) * rank)


def kernel_call(
    kernel, name, outs, scratch, smem, limit, micros, *args, kept=(), far=(), aliases={}
):
    specs = [
        pl.BlockSpec(memory_space=pltpu.SMEM)
        if i < smem
        else streamed(arg.shape)
        if i in far
        else pl.BlockSpec(memory_space=pltpu.VMEM)
        for i, arg in enumerate(args)
    ]
    return pl.pallas_call(
        kernel,
        out_shape=tuple(
            pltpu.HBM(s, t) if i in kept else jax.ShapeDtypeStruct(s, t)
            for i, (s, t) in enumerate(outs)
        ),
        in_specs=specs,
        out_specs=[
            streamed(s) if i in kept else pl.BlockSpec(memory_space=pltpu.VMEM)
            for i, (s, _) in enumerate(outs)
        ],
        scratch_shapes=scratch,
        compiler_params=pltpu.CompilerParams(vmem_limit_bytes=limit * MIB),
        cost_estimate=pl.CostEstimate(
            flops=int(micros * 1e9), transcendentals=0, bytes_accessed=int(micros * 1e6)
        ),
        input_output_aliases=aliases,
        name=name,
    )(
        *(
            pltpu.with_memory_space_constraint(arg, pltpu.HBM) if i in far else arg
            for i, arg in enumerate(args)
        )
    )


def project_kernel(
    x_ref, gain_ref, qh_ref, qb_ref, kh_ref, kb_ref, vh_ref, vb_ref, cos_ref, sin_ref,
    fac_ref, qt_ref, qmix_ref, qbase_ref, normed_ref,
):
    x = x_ref[...].astype(F32)
    scale = lax.rsqrt(jnp.mean(x * x, axis=-1, keepdims=True) + 1e-06)
    normed = (x * scale * gain_ref[...]).astype(BF16)
    normed_ref[...] = normed
    cos = cos_ref[...]
    sin = sin_ref[...]

    def rope(v):
        a, b = v[:HALF], v[HALF:]
        return jnp.concatenate([a * cos - b * sin, a * sin + b * cos], axis=0)

    kb = mm(normed, kb_ref[...]).T
    fac_ref[0:MIX, :] = mm_nt(kh_ref[...], normed).astype(BF16)
    for r in range(KV_RANK):
        at = MIX + r * HEAD_DIM
        fac_ref[at : at + HEAD_DIM, :] = rope(kb[r * HEAD_DIM : (r + 1) * HEAD_DIM]).astype(BF16)
    fac_ref[MIX + BASE : 2 * MIX + BASE, :] = mm_nt(vh_ref[...], normed).astype(BF16)
    fac_ref[2 * MIX + BASE :, :] = mm(normed, vb_ref[...]).T.astype(BF16)
    qmix = mm_nt(qh_ref[...], normed)
    qmix_ref[...] = qmix
    raw = mm(normed, qb_ref[...]).T
    base = [rope(raw[r * HEAD_DIM : (r + 1) * HEAD_DIM]) for r in range(Q_RANK)]
    for r in range(Q_RANK):
        qbase_ref[r * HEAD_DIM : (r + 1) * HEAD_DIM, :] = base[r]
    for h in range(HEADS):
        out = None
        for r in range(Q_RANK):
            part = qmix[h * Q_RANK + r : h * Q_RANK + r + 1, :] * base[r]
            out = part if out is None else out + part
        qt_ref[h * HEAD_DIM : (h + 1) * HEAD_DIM, :] = (
            (out * (1.0 / Q_RANK)).astype(BF16) * (HEAD_DIM ** -0.5)
        ).astype(BF16)


def project(x, gain, weights, cos, sin):
    local, d = x.shape
    width = HEADS * HEAD_DIM
    return kernel_call(
        project_kernel,
        "project",
        (
            ((FACTORS, local), BF16),
            ((width, local), BF16),
            ((QMIX, local), F32),
            ((QBASE, local), F32),
            ((local, d), BF16),
        ),
        [],
        0,
        16,
        2,
        x, gain, *weights, cos, sin,
        kept=(1, 2, 3, 4),
    )


def materialize(fac, offset, head):
    base = offset + MIX
    out = None
    for r in range(KV_RANK):
        row = offset + head * KV_RANK + r
        part = fac[row : row + 1, :] * fac[base + r * HEAD_DIM : base + (r + 1) * HEAD_DIM, :]
        out = part if out is None else out + part
    return (out * (1.0 / KV_RANK)).astype(BF16)


def materialize_quad(fac, offset, quad):
    return jnp.concatenate(
        [materialize(fac, offset, quad * QUAD + i) for i in range(QUAD)], axis=0
    )


def each_block(me, lo, hi, slots, do):
    for slot in range(slots):
        kb = jnp.bitwise_xor(me, slot)
        pl.when((kb >= lo) & (kb < hi))(functools.partial(do, slot, kb))


def block_factors(slot, near, far):
    return (far if slot & 1 else near)[slot >> 1].astype(F32)


def forward_kernel(
    span, qt_ref, near_ref, far_ref, info_ref, x_ref, wo_ref, gain_ref,
    mixed_ref, out_t_ref, lse_ref, hidden_ref, n2_ref,
    k_s, vt_s, qbd_s, acc_s, m_s, l_s, bias_s,
):
    slots, kb_size, _ = k_s.shape
    count = qt_ref.shape[1]
    lo, hi, me = span[0], span[1], span[2]

    def prepare(slot, kb):
        fac = block_factors(slot, near_ref, far_ref)
        for quad in range(QUADS):
            rows = slice(quad * QW, (quad + 1) * QW)
            k_s[kb, :, rows] = materialize_quad(fac, 0, quad).T
            vt_s[kb, rows, :] = materialize_quad(fac, MIX + BASE, quad)

    each_block(me, lo, hi, slots, prepare)
    qbd_s[...] = jnp.zeros_like(qbd_s)
    for h in range(HEADS):
        quad, i = h // QUAD, h % QUAD
        qbd_s[quad, i * HEAD_DIM : (i + 1) * HEAD_DIM, i * count : (i + 1) * count] = qt_ref[
            h * HEAD_DIM : (h + 1) * HEAD_DIM, :
        ]
    m_s[...] = jnp.full_like(m_s, NEG)
    l_s[...] = jnp.zeros_like(l_s)
    acc_s[...] = jnp.zeros_like(acc_s)
    first = info_ref[0:1, :]
    last = info_ref[1:2, :]

    def step(kb, _):
        places = kb * kb_size + lax.broadcasted_iota(jnp.int32, (kb_size, count), 0)
        bias_s[...] = jnp.where((places >= first) & (places <= last), 0.0, NEG)
        for quad in range(QUADS):
            s = mm(k_s[kb, :, quad * QW : (quad + 1) * QW], qbd_s[quad])
            ps = []
            alphas = []
            for i in range(QUAD):
                h = quad * QUAD + i
                sh = s[:, i * count : (i + 1) * count] + bias_s[...]
                old = m_s[h : h + 1, :]
                new = jnp.maximum(old, jnp.max(sh, axis=0, keepdims=True))
                alpha = jnp.exp(old - new)
                p = jnp.exp(sh - new)
                m_s[h : h + 1, :] = new
                l_s[h : h + 1, :] = l_s[h : h + 1, :] * alpha + jnp.sum(p, axis=0, keepdims=True)
                ps.append(p.astype(BF16))
                alphas.append(alpha)
            for j in range(QUAD // 2):
                both = jnp.concatenate(ps[2 * j : 2 * j + 2], axis=1)
                at = quad * QW + j * 2 * HEAD_DIM
                o = mm(vt_s[kb, at : at + 2 * HEAD_DIM, :], both)
                for i in range(2):
                    r = slice(at + i * HEAD_DIM, at + (i + 1) * HEAD_DIM)
                    acc_s[r, :] = (
                        acc_s[r, :] * alphas[2 * j + i]
                        + o[i * HEAD_DIM : (i + 1) * HEAD_DIM, i * count : (i + 1) * count]
                    )
        return 0

    lax.fori_loop(lo, hi, step, 0)
    lse_ref[...] = m_s[...] + jnp.log(l_s[...])
    for h in range(HEADS):
        rows = slice(h * HEAD_DIM, (h + 1) * HEAD_DIM)
        out_t_ref[rows, :] = acc_s[rows, :] * (1.0 / l_s[h : h + 1, :])

    mixed = out_t_ref[...].astype(BF16).T
    mixed_ref[...] = mixed
    hidden = x_ref[...].astype(F32) + mm(mixed, wo_ref[...])
    hidden_ref[...] = hidden
    scale = lax.rsqrt(jnp.mean(hidden * hidden, axis=-1, keepdims=True) + 1e-06)
    n2_ref[...] = (hidden * scale * gain_ref[...]).astype(BF16)


def attend_forward(span, qt, near, far, info, x, wo, gain):
    width, local = qt.shape
    kb = local
    blocks = 2 * near.shape[0]
    d = x.shape[1]
    return kernel_call(
        forward_kernel,
        "attend_forward",
        (
            ((local, width), BF16),
            ((width, local), F32),
            ((HEADS, local), F32),
            ((local, d), F32),
            ((local, d), BF16),
        ),
        [
            pltpu.VMEM((blocks, kb, width), BF16),
            pltpu.VMEM((blocks, width, kb), BF16),
            pltpu.VMEM((QUADS, QW, QUAD * local), BF16),
            pltpu.VMEM((width, local), F32),
            pltpu.VMEM((HEADS, local), F32),
            pltpu.VMEM((HEADS, local), F32),
            pltpu.VMEM((kb, local), F32),
        ],
        1,
        32,
        10,
        span, qt, near, far, info, x, wo, gain,
        kept=(0, 1, 2, 3),
    )


def ffn_kernel(first, final, *refs):
    at_y, n2_ref, up_ref, w_ref = refs[:4]
    prev = None if first else refs[4]
    sng_ref, branch_ref, sums = refs[-3:]
    n2 = n2_ref[...]
    up = up_ref[...]
    hid = w_ref.shape[1]
    gate = mm_nt(n2, w_ref[0])
    lifted = mm_nt(n2, w_ref[1])
    hidden_grad = mm_nt(up, w_ref[2])
    sigmoid = jax.nn.sigmoid(gate)
    silu = gate * sigmoid
    act = (silu * lifted).astype(BF16)
    gate_grad = (hidden_grad * lifted * (sigmoid * (1.0 + gate * (1.0 - sigmoid)))).astype(BF16)
    lift_grad = (hidden_grad * silu).astype(BF16)
    sng_ref[...] = (mm(gate_grad, w_ref[0]) + mm(lift_grad, w_ref[1])).astype(BF16)
    branch_ref[...] = mm(act, w_ref[2]).astype(BF16)
    for at, (left, right) in enumerate(((act, up), (gate_grad, n2), (lift_grad, n2))):
        grad = mm_tn(left, right)
        if not first:
            grad = grad + prev[at]
        if not final:
            sums[at] = grad
        else:
            half = hid // 2
            low = grad.astype(BF16)
            sums[at_y[0], at] = low[:half]
            sums[1 - at_y[0], at] = low[half:]


def feed_forward(at_y, n2, up, weights, prev=None, final=False):
    count, d = n2.shape
    hid = weights.shape[1]
    if final:
        grads = (((2, 3, hid // 2, d), BF16),)
    else:
        grads = ((weights.shape, F32),)
    args = (at_y, n2, up, weights) if prev is None else (at_y, n2, up, weights, prev)
    return kernel_call(
        functools.partial(ffn_kernel, prev is None, final),
        "feed_forward",
        (((count, d), BF16),) * 2 + grads,
        [],
        1,
        19,
        0.05,
        *args,
        kept=(1, 2) if final else (1,),
        aliases={} if prev is None or final else {4: 2},
    )


def residual_kernel(
    sa, sb, up_ref, hidden_ref, gain_ref, wo_ref, out_t_ref,
    res_ref, low_ref, dot_ref, delta_ref, gain_out,
):
    sng = sa[...].astype(F32) + sb[...].astype(F32)
    hidden = hidden_ref[...]
    scale = lax.rsqrt(jnp.mean(hidden * hidden, axis=-1, keepdims=True) + 1e-06)
    gain_out[...] = jnp.sum(sng * (hidden * scale), axis=0, keepdims=True)
    weighted = sng * gain_ref[...]
    inner = jnp.mean(hidden * weighted, axis=-1, keepdims=True)
    res = up_ref[...].astype(F32) + scale * weighted - hidden * (scale * scale * scale) * inner
    res_ref[...] = res
    low = res.astype(BF16)
    low_ref[...] = low
    dot = mm_nt(wo_ref[...], low).astype(BF16)
    dot_ref[...] = dot
    for h in range(HEADS):
        rows = slice(h * HEAD_DIM, (h + 1) * HEAD_DIM)
        delta_ref[h : h + 1, :] = jnp.sum(
            dot[rows].astype(F32) * out_t_ref[rows, :], axis=0, keepdims=True
        )


def residual(sa, sb, up, hidden, gain, wo, out_t, far=()):
    local, d = hidden.shape
    width = out_t.shape[0]
    return kernel_call(
        residual_kernel,
        "residual",
        (
            ((local, d), F32),
            ((local, d), BF16),
            ((width, local), BF16),
            ((HEADS, local), F32),
            ((1, d), F32),
        ),
        [],
        0,
        16,
        3,
        sa, sb, up, hidden, gain, wo, out_t,
        kept=(0, 2, 3),
        far=far,
    )


def backward_kernel(
    span, qt_ref, near_ref, far_ref, info_ref, dot_ref, lse_ref, delta_ref,
    qmix_ref, qbase_ref, cos_ref, sin_ref,
    dnear_ref, dfar_ref, dq_ref,
    k_s, kt_s, vt_s, dkt_s, dvt_s, qbd_s, qbdt_s, obd_s, obdt_s, dq_s, bias_s, lse_s, delta_s,
):
    slots, kb_size, _ = k_s.shape
    count = qt_ref.shape[1]
    lo, hi, me = span[0], span[1], span[2]
    dnear_ref[...] = jnp.zeros_like(dnear_ref)
    dfar_ref[...] = jnp.zeros_like(dfar_ref)

    def prepare(slot, kb):
        fac = block_factors(slot, near_ref, far_ref)
        for quad in range(QUADS):
            rows = slice(quad * QW, (quad + 1) * QW)
            kt = materialize_quad(fac, 0, quad)
            kt_s[kb, rows, :] = kt
            k_s[kb, :, rows] = kt.T
            vt_s[kb, rows, :] = materialize_quad(fac, MIX + BASE, quad)
            dkt_s[kb, rows, :] = jnp.zeros((QW, kb_size), F32)
            dvt_s[kb, rows, :] = jnp.zeros((QW, kb_size), F32)

    each_block(me, lo, hi, slots, prepare)
    qbdt_s[...] = jnp.zeros_like(qbdt_s)
    obdt_s[...] = jnp.zeros_like(obdt_s)

    for h in range(HEADS):
        quad, i = h // QUAD, h % QUAD
        to = slice(i * HEAD_DIM, (i + 1) * HEAD_DIM)
        at = slice(i * count, (i + 1) * count)
        rows = slice(h * HEAD_DIM, (h + 1) * HEAD_DIM)
        qbdt_s[quad, to, at] = qt_ref[rows, :]
        obdt_s[quad, to, at] = dot_ref[rows, :]
    for quad in range(QUADS):
        qbd_s[quad] = qbdt_s[quad].T
        obd_s[quad] = obdt_s[quad].T
    lse_t = lse_ref[:, :].T
    delta_t = delta_ref[:, :].T
    for h in range(HEADS):
        lse_s[h] = jnp.broadcast_to(lse_t[:, h : h + 1], (count, TILE))
        delta_s[h] = jnp.broadcast_to(delta_t[:, h : h + 1], (count, TILE))
    dq_s[...] = jnp.zeros_like(dq_s)
    info_t = info_ref[:, :].T
    first = info_t[:, 0:1]
    last = info_t[:, 1:2]

    def step(kb, _):
        places = kb * kb_size + lax.broadcasted_iota(jnp.int32, (count, kb_size), 1)
        bias_s[...] = jnp.where((places >= first) & (places <= last), 0.0, NEG)
        lane = lax.broadcasted_iota(jnp.int32, (count, QW), 1) // HEAD_DIM
        for quad in range(QUADS):
            rows = slice(quad * QW, (quad + 1) * QW)
            s = mm(qbd_s[quad], kt_s[kb, rows, :])
            dp = mm(obd_s[quad], vt_s[kb, rows, :])
            ps = []
            dss = []
            for i in range(QUAD):
                h = quad * QUAD + i
                at = slice(i * count, (i + 1) * count)
                lse = jnp.concatenate([lse_s[h]] * (kb_size // TILE), axis=1)
                delta = jnp.concatenate([delta_s[h]] * (kb_size // TILE), axis=1)
                p = jnp.exp((s[at] + bias_s[...]) - lse)
                ps.append(p.astype(BF16))
                dss.append((p * (dp[at] - delta)).astype(BF16))
            p4 = jnp.concatenate(ps, axis=0)
            ds4 = jnp.concatenate(dss, axis=0)
            dkt_s[kb, rows, :] += mm(qbdt_s[quad], ds4)
            dvt_s[kb, rows, :] += mm(obdt_s[quad], p4)
            dq = mm(ds4, k_s[kb, :, rows])
            out = dq[0:count]
            for i in range(1, QUAD):
                out = jnp.where(lane == i, dq[i * count : (i + 1) * count], out)
            dq_s[:, rows] += out
        return 0

    lax.fori_loop(lo, hi, step, 0)
    dqt = dq_s[...].T * (HEAD_DIM ** -0.5 / Q_RANK)
    qmix = qmix_ref[:, :]
    mixes = []
    for h in range(HEADS):
        part = dqt[h * HEAD_DIM : (h + 1) * HEAD_DIM, :]
        for r in range(Q_RANK):
            mixes.append(
                jnp.sum(
                    part * qbase_ref[r * HEAD_DIM : (r + 1) * HEAD_DIM, :], axis=0, keepdims=True
                )
            )
    dq_ref[:QMIX, :] = jnp.concatenate(mixes, axis=0).astype(BF16)
    cos = cos_ref[...]
    sin = sin_ref[...]
    for r in range(Q_RANK):
        out = None
        for h in range(HEADS):
            row = h * Q_RANK + r
            part = qmix[row : row + 1, :] * dqt[h * HEAD_DIM : (h + 1) * HEAD_DIM, :]
            out = part if out is None else out + part
        upper, lower = out[:HALF], out[HALF:]
        at = QMIX + r * HEAD_DIM
        dq_ref[at : at + HALF, :] = (upper * cos + lower * sin).astype(BF16)
        dq_ref[at + HALF : at + HEAD_DIM, :] = (lower * cos - upper * sin).astype(BF16)

    def fold(slot, kb):
        fac = block_factors(slot, near_ref, far_ref)
        to = dfar_ref if slot & 1 else dnear_ref
        for offset, grad in ((0, dkt_s), (MIX + BASE, dvt_s)):
            outs = [None] * KV_RANK
            mixes = []
            for h in range(HEADS):
                g = grad[kb, h * HEAD_DIM : (h + 1) * HEAD_DIM, :] * (1.0 / KV_RANK)
                for r in range(KV_RANK):
                    at = offset + MIX + r * HEAD_DIM
                    mixes.append(jnp.sum(g * fac[at : at + HEAD_DIM, :], axis=0, keepdims=True))
                    row = offset + h * KV_RANK + r
                    part = fac[row : row + 1, :] * g
                    outs[r] = part if outs[r] is None else outs[r] + part
            to[slot >> 1, offset : offset + MIX, :] = jnp.concatenate(mixes, axis=0).astype(BF16)
            for r in range(KV_RANK):
                at = offset + MIX + r * HEAD_DIM
                to[slot >> 1, at : at + HEAD_DIM, :] = outs[r].astype(BF16)

    each_block(me, lo, hi, slots, fold)


def attend_backward(micros, span, qt, near, far, info, dot, lse, delta, qmix, qbase, cos, sin):
    width, local = qt.shape
    kb = local
    blocks = 2 * near.shape[0]
    return kernel_call(
        backward_kernel,
        "attend_backward",
        (
            (near.shape, BF16),
            (near.shape, BF16),
            ((QMIX + QBASE, local), BF16),
        ),
        [
            pltpu.VMEM((blocks, kb, width), BF16),
            pltpu.VMEM((blocks, width, kb), BF16),
            pltpu.VMEM((blocks, width, kb), BF16),
            pltpu.VMEM((blocks, width, kb), F32),
            pltpu.VMEM((blocks, width, kb), F32),
            pltpu.VMEM((QUADS, QUAD * local, QW), BF16),
            pltpu.VMEM((QUADS, QW, QUAD * local), BF16),
            pltpu.VMEM((QUADS, QUAD * local, QW), BF16),
            pltpu.VMEM((QUADS, QW, QUAD * local), BF16),
            pltpu.VMEM((local, width), F32),
            pltpu.VMEM((local, kb), F32),
            pltpu.VMEM((HEADS, local, TILE), F32),
            pltpu.VMEM((HEADS, local, TILE), F32),
        ],
        1,
        56,
        micros,
        span, qt, near, far, info, dot, lse, delta, qmix, qbase, cos, sin,
        far=(1, 5, 6, 7, 8, 9),
    )


def share_kernel(*refs):
    me = refs[0]
    pieces = (refs[1:5], refs[5:9])
    dqs, coss, sins, normeds, gains = refs[9:11], refs[11:13], refs[13:15], refs[15:17], refs[17:19]
    lows = refs[19:21]
    near_ref, far_ref, all_s = refs[21:]
    query = QMIX + QBASE
    for b in range(2):
        first, second, third, fourth = (piece[...].astype(F32) for piece in pieces[b])
        total = (first + second) + (third + fourth)
        cos = coss[b][...]
        sin = sins[b][...]
        low_ref = lows[b]
        low_ref[:query, :] = dqs[b][...]
        low_ref[query:, :] = total.astype(BF16)
        for r in range(KV_RANK):
            at = MIX + r * HEAD_DIM
            upper, lower = total[at : at + HALF], total[at + HALF : at + HEAD_DIM]
            to = query + at
            low_ref[to : to + HALF, :] = (upper * cos + lower * sin).astype(BF16)
            low_ref[to + HALF : to + HEAD_DIM, :] = (lower * cos - upper * sin).astype(BF16)
    rows = query + FACTORS
    all_s[:rows, :] = mm(
        jnp.concatenate([low[...] for low in lows], axis=1),
        jnp.concatenate([normed[...] for normed in normeds], axis=0),
    )
    all_s[rows:, :] = jnp.concatenate(
        [gains[0][...] + gains[1][...], jnp.zeros((15, gains[0].shape[1]), F32)], axis=0
    )
    width = near_ref.shape[2]
    for is_far, ref in ((0, near_ref), (1, far_ref)):
        for slot in range(ref.shape[0]):
            at = pl.multiple_of(jnp.bitwise_xor(me[0], 2 * slot + is_far) * width, width)
            ref[slot] = all_s[:, pl.ds(at, width)].astype(BF16)


def share(me, pieces0, pieces1, dqs, cosine, sine, normeds, gains, slots):
    local, d = normeds[0].shape
    count = QMIX + QBASE + FACTORS
    return kernel_call(
        share_kernel,
        "share",
        (((count, local), BF16),) * 2 + (((slots // 2, count + 16, d // slots), BF16),) * 2,
        [pltpu.VMEM((count + 16, d), F32)],
        1,
        18,
        0.05,
        me, *pieces0, *pieces1, *dqs, cosine[0], cosine[1], sine[0], sine[1], *normeds, *gains,
        far=tuple(range(1, 17)),
    )


def finish_kernel(*refs):
    low_ref, x_ref, gain_ref, res_ref = refs[:4]
    weights = refs[4:10]
    grad_ref = refs[10]
    low = low_ref[...].T
    grad = None
    at = 0
    for ref in weights:
        if ref.shape[0] == x_ref.shape[1]:
            count = ref.shape[1]
            part = mm_nt(low[:, at : at + count], ref[...])
        else:
            count = ref.shape[0]
            part = mm(low[:, at : at + count], ref[...])
        grad = part if grad is None else grad + part
        at += count
    x = x_ref[...].astype(F32)
    scale = lax.rsqrt(jnp.mean(x * x, axis=-1, keepdims=True) + 1e-06)
    weighted = grad * gain_ref[...]
    inner = jnp.mean(x * weighted, axis=-1, keepdims=True)
    grad_ref[...] = res_ref[...] + (scale * weighted - x * (scale * scale * scale) * inner)


def finish(low, x, gain, res, weights):
    local, d = x.shape
    return kernel_call(
        finish_kernel,
        "finish",
        (((local, d), F32),),
        [],
        0,
        16,
        0.05,
        low, x, gain, res, *weights,
        far=(1, 3, 4, 5, 6, 7, 8, 9),
    )[0]


def output_weight_kernel(core, m0, m1, low0, low1, near_ref, far_ref, all_s):
    all_s[...] = mm_tn(m0[...], low0[...]) + mm_tn(m1[...], low1[...])
    count = near_ref.shape[1]
    for chip in range(near_ref.shape[0]):
        for at, ref in ((core[0], near_ref), (1 - core[0], far_ref)):
            row = pl.multiple_of((2 * chip + at) * count, count)
            ref[chip] = all_s[pl.ds(row, count), :].astype(BF16)


def output_weight_shares(core, mixed, lows, slots):
    width, d = mixed[0].shape[1], lows[0].shape[1]
    return kernel_call(
        output_weight_kernel,
        "output_weight_shares",
        (((slots // 2, width // slots, d), BF16),) * 2,
        [pltpu.VMEM((width, d), F32)],
        1,
        16,
        0.05,
        core, *mixed, *lows,
        far=(1, 2, 3, 4),
    )


def branch_kernel(n0, n1, f0, f1, mine_ref, theirs_ref):
    half = mine_ref.shape[0] // 2
    for b, (near, far) in enumerate(((n0, f0), (n1, f1))):
        total = (near[...].astype(F32) + far[...].astype(F32)).astype(BF16)
        mine_ref[b * half : (b + 1) * half, :] = total[:half]
        theirs_ref[b * half : (b + 1) * half, :] = total[half:]


def branch_sums(nears, fars):
    return kernel_call(
        branch_kernel,
        "branch_sums",
        ((nears[0].shape, BF16),) * 2,
        [],
        0,
        16,
        0.05,
        *nears, *fars,
        kept=(0, 1),
        far=(0, 1, 2, 3),
    )


highest = lax.Precision.HIGHEST
masked_score = -1e30


def rms_scale(values):
    return lax.rsqrt(jnp.mean(values * values, axis=-1, keepdims=True) + 1e-06)


def norm_backward(values, gain, scaled, upstream):
    weighted = upstream * gain
    inner = jnp.mean(values * weighted, axis=-1, keepdims=True)
    return scaled * weighted - values * (scaled * scaled * scaled) * inner


def rotate(values, cosine, sine):
    half = values.shape[-1] // 2
    first = values[..., :half]
    second = values[..., half:]
    return jnp.concatenate(
        [first * cosine - second * sine, first * sine + second * cosine], axis=-1
    )


def row_layout(lengths_row, places):
    ends = jnp.cumsum(lengths_row)
    passed = ends[None, :] <= places[:, None]
    segment = jnp.sum(passed.astype(jnp.int32), axis=1)
    start = jnp.max(jnp.where(passed, ends[None, :], 0), axis=1)
    valid = places < ends[-1]
    return (segment, places - start, valid)


def rope_tables(position):
    half = HEAD_DIM // 2
    frequency = 10000.0 ** (-jnp.arange(half, dtype=jnp.float32) / half)
    angle = position.astype(jnp.float32)[..., None] * frequency
    return (jnp.cos(angle), jnp.sin(angle))


def split_factors(factors):
    mix_width = HEADS * KV_RANK
    base_width = KV_RANK * HEAD_DIM
    count, rows = (factors.shape[0], factors.shape[1])
    key_mix = factors[..., :mix_width].reshape(count, rows, HEADS, KV_RANK)
    key_base = factors[..., mix_width : mix_width + base_width].reshape(
        count, rows, KV_RANK, HEAD_DIM
    )
    value_mix = factors[..., mix_width + base_width : 2 * mix_width + base_width].reshape(
        count, rows, HEADS, KV_RANK
    )
    value_base = factors[..., 2 * mix_width + base_width :].reshape(count, rows, KV_RANK, HEAD_DIM)
    return (key_mix, key_base, value_mix, value_base)


def pair_gradient(hidden_grad, gate, lifted):
    sigmoid = jax.nn.sigmoid(gate)
    gate_grad = hidden_grad * lifted * (sigmoid * (1.0 + gate * (1.0 - sigmoid)))
    lift_grad = hidden_grad * (gate * sigmoid)
    return jnp.concatenate([gate_grad, lift_grad], axis=-1).astype(jnp.bfloat16)


def general_body(
    tokens,
    lengths,
    cotangent,
    first_gain,
    query_heads,
    query_basis,
    key_heads,
    key_basis,
    value_heads,
    value_basis,
    output_weight,
    second_gain,
    gate_weight,
    up_weight,
    down_projection_weight,
):
    local, batch_rows, width = tokens.shape
    total = local * lax.axis_size("wide")
    offset = lax.axis_index("wide") * local
    places = jnp.arange(total, dtype=jnp.int32)
    segment, position, valid = jax.vmap(row_layout, in_axes=(0, None))(lengths, places)
    own_places = offset + jnp.arange(local, dtype=jnp.int32)
    own_segment = lax.dynamic_slice_in_dim(segment, offset, local, 1)
    own_position = lax.dynamic_slice_in_dim(position, offset, local, 1)
    own_valid = lax.dynamic_slice_in_dim(valid, offset, local, 1)
    cosine, sine = rope_tables(jnp.transpose(own_position))
    cosine = cosine[:, :, None, :]
    sine = sine[:, :, None, :]
    keep_rows = jnp.transpose(own_valid)[:, :, None]
    scale = HEAD_DIM ** (-0.5)
    block_rows = min(512, total)
    block_count = total // block_rows
    mix_width = HEADS * KV_RANK
    base_width = KV_RANK * HEAD_DIM
    flat_rows = local * batch_rows
    inputs = tokens.astype(jnp.float32)
    first_scale = rms_scale(inputs)
    normed = (inputs * first_scale * first_gain).astype(jnp.bfloat16)
    flat = normed.reshape(flat_rows, width)
    query_mix = jnp.dot(flat, query_heads, preferred_element_type=jnp.float32).reshape(
        local, batch_rows, HEADS, Q_RANK
    )
    query_raw = jnp.dot(flat, query_basis, preferred_element_type=jnp.float32).reshape(
        local, batch_rows, Q_RANK, HEAD_DIM
    )
    query_base = rotate(query_raw, cosine, sine)
    factor_weight = jnp.concatenate([key_heads, key_basis, value_heads, value_basis], axis=1)
    factor_raw = jnp.dot(flat, factor_weight, preferred_element_type=jnp.float32).reshape(
        local, batch_rows, -1
    )
    key_roped = rotate(
        factor_raw[..., mix_width : mix_width + base_width].reshape(
            local, batch_rows, KV_RANK, HEAD_DIM
        ),
        cosine,
        sine,
    ).reshape(local, batch_rows, base_width)
    factors = jnp.concatenate(
        [factor_raw[..., :mix_width], key_roped, factor_raw[..., mix_width + base_width :]], axis=-1
    ).astype(jnp.bfloat16)
    every = lax.all_gather(factors, "wide", axis=0, tiled=True)
    key_mix, key_base, value_mix, value_base = split_factors(every)
    keys = (
        jnp.einsum("trhk,trkd->trhd", key_mix, key_base, preferred_element_type=jnp.float32)
        / KV_RANK
    ).astype(jnp.bfloat16)
    values = (
        jnp.einsum("trhk,trkd->trhd", value_mix, value_base, preferred_element_type=jnp.float32)
        / KV_RANK
    ).astype(jnp.bfloat16)
    query = (
        jnp.einsum(
            "trhk,trkd->trhd",
            query_mix,
            query_base,
            precision=highest,
            preferred_element_type=jnp.float32,
        )
        / Q_RANK
    ).astype(jnp.bfloat16)

    def block_view(block):
        start = block * block_rows
        key_places = start + jnp.arange(block_rows, dtype=jnp.int32)
        key_segment = lax.dynamic_slice_in_dim(segment, start, block_rows, 1)
        key_valid = lax.dynamic_slice_in_dim(valid, start, block_rows, 1)
        causal = key_places[None, :] <= own_places[:, None]
        itself = key_places[None, :] == own_places[:, None]
        allowed = (
            causal[None]
            & (own_segment[:, :, None] == key_segment[:, None, :])
            & (key_valid[:, None, :] | itself[None])
        )
        key_block = lax.dynamic_slice_in_dim(keys, start, block_rows, 0)
        value_block = lax.dynamic_slice_in_dim(values, start, block_rows, 0)
        product = (
            jnp.einsum("qrhd,krhd->rhqk", query, key_block, preferred_element_type=jnp.float32)
            * scale
        )
        scores = jnp.where(allowed[:, None], product, masked_score)
        return (start, scores, key_block, value_block)

    def max_step(carry, block):
        top, mass = carry
        scores = block_view(block)[1]
        higher = jnp.maximum(top, jnp.max(scores, axis=-1))
        mass = mass * jnp.exp(top - higher) + jnp.sum(jnp.exp(scores - higher[..., None]), axis=-1)
        return ((higher, mass), None)

    start_top = jnp.full((batch_rows, HEADS, local), masked_score, jnp.float32)
    (top, mass), _ = lax.scan(
        max_step, (start_top, jnp.zeros_like(start_top)), jnp.arange(block_count)
    )
    log_total = top + jnp.log(mass)

    def out_step(carry, block):
        _, scores, _, value_block = block_view(block)
        chances = jnp.exp(scores - log_total[..., None]).astype(jnp.bfloat16)
        return (
            carry
            + jnp.einsum(
                "rhqk,krhd->qrhd", chances, value_block, preferred_element_type=jnp.float32
            ),
            None,
        )

    attended, _ = lax.scan(
        out_step,
        jnp.zeros((local, batch_rows, HEADS, HEAD_DIM), jnp.float32),
        jnp.arange(block_count),
    )
    mixed = attended.astype(jnp.bfloat16).reshape(flat_rows, HEADS * HEAD_DIM)
    hidden_state = inputs + jnp.dot(
        mixed, output_weight, preferred_element_type=jnp.float32
    ).reshape(local, batch_rows, width)
    second_scale = rms_scale(hidden_state)
    normed_second = (hidden_state * second_scale * second_gain).astype(jnp.bfloat16)
    normalized_token_rows = lax.all_gather(normed_second, "wide", axis=0, tiled=True)
    gate_lifted_hidden = jnp.concatenate([gate_weight, up_weight], axis=1)
    hidden_width = gate_weight.shape[1]
    projected_output = jnp.einsum(
        "zec,cx->zex", normalized_token_rows, gate_lifted_hidden, preferred_element_type=jnp.float32
    )
    gate = projected_output[..., :hidden_width]
    lifted = projected_output[..., hidden_width:]
    silu_hidden_output = (jax.nn.silu(gate) * lifted).astype(jnp.bfloat16)
    sequence_portion = silu_hidden_output
    branch = lax.psum_scatter(
        jnp.einsum(
            "zyu,uv->zyv",
            sequence_portion,
            down_projection_weight,
            preferred_element_type=jnp.float32,
        ).astype(jnp.bfloat16),
        "wide",
        scatter_dimension=0,
        tiled=True,
    ).astype(jnp.float32)
    output = jnp.where(keep_rows, hidden_state + branch, 0.0).astype(jnp.bfloat16)
    upstream = jnp.where(keep_rows, cotangent.astype(jnp.float32), 0.0)
    upstream_low = upstream.astype(jnp.bfloat16)
    upstream_token_gradient = lax.all_gather(upstream_low, "wide", axis=0, tiled=True)
    hidden_grad = jnp.einsum(
        "ajg,vg->ajv",
        upstream_token_gradient,
        down_projection_weight,
        preferred_element_type=jnp.float32,
    )
    pair_product_gradient = pair_gradient(hidden_grad, gate, lifted)
    down_gradient = jnp.einsum(
        "imj,ima->ja",
        silu_hidden_output,
        upstream_token_gradient,
        preferred_element_type=jnp.float32,
    )
    pair_weight_grad = jnp.einsum(
        "ipl,ipj->lj",
        normalized_token_rows,
        pair_product_gradient,
        preferred_element_type=jnp.float32,
    )
    sequence_portion = pair_product_gradient
    second_normed_grad = lax.psum_scatter(
        jnp.einsum(
            "ivu,bu->ivb", sequence_portion, gate_lifted_hidden, preferred_element_type=jnp.float32
        ),
        "wide",
        scatter_dimension=0,
        tiled=True,
    )
    second_gain_partial = jnp.sum(second_normed_grad * (hidden_state * second_scale), axis=(0, 1))
    residual_grad = upstream + norm_backward(
        hidden_state, second_gain, second_scale, second_normed_grad
    )
    residual_low = residual_grad.astype(jnp.bfloat16).reshape(flat_rows, width)
    output_weight_grad = jnp.einsum(
        "tk,td->kd", mixed, residual_low, preferred_element_type=jnp.float32
    )
    mixed_grad = (
        jnp.einsum("td,kd->tk", residual_low, output_weight, preferred_element_type=jnp.float32)
        .astype(jnp.bfloat16)
        .reshape(local, batch_rows, HEADS, HEAD_DIM)
    )

    def delta_step(carry, block):
        _, scores, _, value_block = block_view(block)
        chances = jnp.exp(scores - log_total[..., None])
        pressure = jnp.einsum(
            "qrhd,krhd->rhqk", mixed_grad, value_block, preferred_element_type=jnp.float32
        )
        return (carry + jnp.sum(chances * pressure, axis=-1), None)

    delta, _ = lax.scan(
        delta_step, jnp.zeros((batch_rows, HEADS, local), jnp.float32), jnp.arange(block_count)
    )

    def grad_step(carry, block):
        start, scores, key_block, value_block = block_view(block)
        chances = jnp.exp(scores - log_total[..., None])
        pressure = jnp.einsum(
            "qrhd,krhd->rhqk", mixed_grad, value_block, preferred_element_type=jnp.float32
        )
        score_grad = (chances * (pressure - delta[..., None])).astype(jnp.bfloat16)
        carry = (
            carry
            + jnp.einsum(
                "rhqk,krhd->qrhd", score_grad, key_block, preferred_element_type=jnp.float32
            )
            * scale
        )
        key_grad = (
            jnp.einsum("rhqk,qrhd->krhd", score_grad, query, preferred_element_type=jnp.float32)
            * scale
        )
        value_grad = jnp.einsum(
            "rhqk,qrhd->krhd",
            chances.astype(jnp.bfloat16),
            mixed_grad,
            preferred_element_type=jnp.float32,
        )
        block_mix, block_base, block_vmix, block_vbase = split_factors(
            lax.dynamic_slice_in_dim(every, start, block_rows, 0).astype(jnp.float32)
        )
        key_mix_grad = (
            jnp.einsum("krhd,krcd->krhc", key_grad, block_base, precision=highest) / KV_RANK
        )
        key_base_grad = (
            jnp.einsum("krhc,krhd->krcd", block_mix, key_grad, precision=highest) / KV_RANK
        )
        value_mix_grad = (
            jnp.einsum("krhd,krcd->krhc", value_grad, block_vbase, precision=highest) / KV_RANK
        )
        value_base_grad = (
            jnp.einsum("krhc,krhd->krcd", block_vmix, value_grad, precision=highest) / KV_RANK
        )
        block_grad = jnp.concatenate(
            [
                key_mix_grad.reshape(block_rows, batch_rows, mix_width),
                key_base_grad.reshape(block_rows, batch_rows, base_width),
                value_mix_grad.reshape(block_rows, batch_rows, mix_width),
                value_base_grad.reshape(block_rows, batch_rows, base_width),
            ],
            axis=-1,
        )
        return (carry, block_grad)

    query_grad, factor_blocks = lax.scan(
        grad_step,
        jnp.zeros((local, batch_rows, HEADS, HEAD_DIM), jnp.float32),
        jnp.arange(block_count),
    )
    factor_grads = factor_blocks.reshape(total, batch_rows, 2 * mix_width + 2 * base_width)
    own_factor_grads = lax.psum_scatter(
        factor_grads.astype(jnp.bfloat16), "wide", scatter_dimension=0, tiled=True
    ).astype(jnp.float32)
    key_base_back = rotate(
        own_factor_grads[..., mix_width : mix_width + base_width].reshape(
            local, batch_rows, KV_RANK, HEAD_DIM
        ),
        cosine,
        -sine,
    ).reshape(local, batch_rows, base_width)
    factor_low = (
        jnp.concatenate(
            [
                own_factor_grads[..., :mix_width],
                key_base_back,
                own_factor_grads[..., mix_width + base_width :],
            ],
            axis=-1,
        )
        .astype(jnp.bfloat16)
        .reshape(flat_rows, -1)
    )
    mix_grad = jnp.einsum("trhd,trcd->trhc", query_grad, query_base, precision=highest) / Q_RANK
    base_roped_grad = (
        jnp.einsum("trhc,trhd->trcd", query_mix, query_grad, precision=highest) / Q_RANK
    )
    base_grad = rotate(base_roped_grad, cosine, -sine)
    mix_low = mix_grad.astype(jnp.bfloat16).reshape(flat_rows, HEADS * Q_RANK)
    base_low = base_grad.astype(jnp.bfloat16).reshape(flat_rows, Q_RANK * HEAD_DIM)
    query_heads_grad = jnp.einsum("tk,tf->kf", flat, mix_low, preferred_element_type=jnp.float32)
    query_basis_grad = jnp.einsum("tk,tf->kf", flat, base_low, preferred_element_type=jnp.float32)
    factor_weight_grad = jnp.einsum(
        "tk,tf->kf", flat, factor_low, preferred_element_type=jnp.float32
    )
    first_normed_grad = (
        jnp.einsum("tf,kf->tk", mix_low, query_heads, preferred_element_type=jnp.float32)
        + jnp.einsum("tf,kf->tk", base_low, query_basis, preferred_element_type=jnp.float32)
        + jnp.einsum("tf,kf->tk", factor_low, factor_weight, preferred_element_type=jnp.float32)
    ).reshape(local, batch_rows, width)
    first_gain_partial = jnp.sum(first_normed_grad * (inputs * first_scale), axis=(0, 1))
    tokens_gradient = residual_grad + norm_backward(
        inputs, first_gain, first_scale, first_normed_grad
    )
    key_heads_grad = factor_weight_grad[:, :mix_width]
    key_basis_grad = factor_weight_grad[:, mix_width : mix_width + base_width]
    value_heads_grad = factor_weight_grad[:, mix_width + base_width : 2 * mix_width + base_width]
    value_basis_grad = factor_weight_grad[:, 2 * mix_width + base_width :]
    (
        first_share,
        qheads_share,
        qbasis_share,
        kheads_share,
        kbasis_share,
        vheads_share,
        vbasis_share,
        output_share,
        second_share,
    ) = (
        lax.psum_scatter(
            first_gain_partial.astype(jnp.bfloat16), "wide", scatter_dimension=0, tiled=True
        ).astype(jnp.float32),
        lax.psum_scatter(
            query_heads_grad.astype(jnp.bfloat16), "wide", scatter_dimension=0, tiled=True
        ).astype(jnp.float32),
        lax.psum_scatter(
            query_basis_grad.astype(jnp.bfloat16), "wide", scatter_dimension=0, tiled=True
        ).astype(jnp.float32),
        lax.psum_scatter(
            key_heads_grad.astype(jnp.bfloat16), "wide", scatter_dimension=0, tiled=True
        ).astype(jnp.float32),
        lax.psum_scatter(
            key_basis_grad.astype(jnp.bfloat16), "wide", scatter_dimension=0, tiled=True
        ).astype(jnp.float32),
        lax.psum_scatter(
            value_heads_grad.astype(jnp.bfloat16), "wide", scatter_dimension=0, tiled=True
        ).astype(jnp.float32),
        lax.psum_scatter(
            value_basis_grad.astype(jnp.bfloat16), "wide", scatter_dimension=0, tiled=True
        ).astype(jnp.float32),
        lax.psum_scatter(
            output_weight_grad.astype(jnp.bfloat16), "wide", scatter_dimension=0, tiled=True
        ).astype(jnp.float32),
        lax.psum_scatter(
            second_gain_partial.astype(jnp.bfloat16), "wide", scatter_dimension=0, tiled=True
        ).astype(jnp.float32),
    )
    gate_share = pair_weight_grad[:, :hidden_width]
    lift_share = pair_weight_grad[:, hidden_width:]
    totals = (
        lax.psum(first_share.astype(jnp.bfloat16), "batch").astype(jnp.float32),
        lax.psum(qheads_share.astype(jnp.bfloat16), "batch").astype(jnp.float32),
        lax.psum(qbasis_share.astype(jnp.bfloat16), "batch").astype(jnp.float32),
        lax.psum(kheads_share.astype(jnp.bfloat16), "batch").astype(jnp.float32),
        lax.psum(kbasis_share.astype(jnp.bfloat16), "batch").astype(jnp.float32),
        lax.psum(vheads_share.astype(jnp.bfloat16), "batch").astype(jnp.float32),
        lax.psum(vbasis_share.astype(jnp.bfloat16), "batch").astype(jnp.float32),
        lax.psum(output_share.astype(jnp.bfloat16), "batch").astype(jnp.float32),
        lax.psum(second_share.astype(jnp.bfloat16), "batch").astype(jnp.float32),
        lax.psum(gate_share.astype(jnp.bfloat16), "batch").astype(jnp.float32),
        lax.psum(lift_share.astype(jnp.bfloat16), "batch").astype(jnp.float32),
        lax.psum(down_gradient.astype(jnp.bfloat16), "batch").astype(jnp.float32),
    )
    return (
        output,
        tokens_gradient,
        totals[0],
        totals[1],
        totals[2],
        totals[3],
        totals[4],
        totals[5],
        totals[6],
        totals[7],
        totals[8],
        totals[9],
        totals[10],
        totals[11],
    )


def partners(distance, count):
    return [(i, i ^ distance) for i in range(count)]


def fence(*values):
    return lax.optimization_barrier(values)


def after(value, *others):
    return lax.optimization_barrier((value,) + others)[0]


def in_order(value):
    return with_layout_constraint(value, Layout(tuple(range(value.ndim))))


def body(
    tokens,
    lengths,
    cotangent,
    first_gain,
    query_heads,
    query_basis,
    key_heads,
    key_basis,
    value_heads,
    value_basis,
    output_weight,
    second_gain,
    gate_weight,
    up_weight,
    down_projection_weight,
):
    local, rows, width = tokens.shape
    wide = ("y", "x", "core")
    n = lax.axis_size(wide)
    depth = lax.axis_size("batch")
    me = lax.axis_index(wide).astype(jnp.int32)
    at_y = lax.axis_index("y").astype(jnp.int32).reshape(1)

    def swap(value, distance):
        return lax.ppermute(value, wide, partners(distance, n))

    def swap_batch(value, distance):
        return lax.ppermute(value, "batch", partners(distance, depth))

    core, across, along, diagonal = 1, 2, 4, 6
    chips = (across, along, diagonal)

    def send_chips(value):
        return [swap(value, distance) for distance in chips]

    def send_slots(sums):
        return [swap(sums[i + 1], chips[i]) for i in range(len(chips))]

    def add(*values):
        return sum(value.astype(F32) for value in values).astype(BF16)

    places = me * local + jnp.arange(local, dtype=jnp.int32)
    slots = lengths.shape[1]
    upto = jnp.arange(slots)[:, None] >= jnp.arange(slots)[None, :]
    ends = jnp.sum(jnp.where(upto[None], lengths[:, None, :], 0), axis=2)
    passed = ends[:, None, :] <= places[None, :, None]
    start = jnp.max(jnp.where(passed, ends[:, None, :], 0), axis=2)
    valid = places[None, :] < ends[:, -1:]
    position = places[None, :] - start
    first_seen = jnp.where(valid, start, places[None, :])
    frequency = 10000.0 ** (-jnp.arange(HALF, dtype=F32) / HALF)
    angle = position.astype(F32)[:, None, :] * frequency[None, :, None]
    cosine, sine = jnp.cos(angle), jnp.sin(angle)
    info = jnp.stack([first_seen, jnp.broadcast_to(places, (rows, local))], axis=1)
    info = jnp.concatenate([info, jnp.zeros((rows, 6, local), jnp.int32)], axis=1)
    spans = jnp.stack(
        [
            jnp.min(first_seen, axis=1) // local,
            jnp.broadcast_to(me + 1, (rows,)),
            jnp.broadcast_to(me, (rows,)),
        ],
        axis=1,
    ).astype(jnp.int32)

    gain1 = first_gain.reshape(1, width)
    gain2 = second_gain.reshape(1, width)
    projections = (query_heads, query_basis, key_heads, key_basis, value_heads, value_basis)
    narrow = tuple(w.T if w.shape[1] < TILE else w for w in projections)

    xs = [tokens[:, b, :] for b in range(rows)]
    projected = [project(xs[0], gain1, narrow, cosine[0], sine[0])]
    sent0 = send_chips(projected[0][0])
    x1 = after(xs[1], projected[0][0])
    projected.append(project(x1, gain1, narrow, cosine[1], sine[1]))
    sent1 = send_chips(projected[1][0])
    own_weights = jnp.stack(
        [after(gate_weight.T, projected[1][0]), up_weight.T, down_projection_weight]
    )
    other_weights = swap(own_weights, along)
    near = jnp.stack([projected[0][0]] + [after(got, own_weights) for got in sent0])
    far = swap(near, core)
    gathered = [(near, far)]
    seen = after(valid, near)
    ups = [jnp.where(seen[b][:, None], cotangent[:, b, :], 0) for b in range(rows)]
    up_pair = jnp.concatenate(ups, axis=0)
    up_got = swap(up_pair, across)

    def forward(b):
        outs = attend_forward(
            spans[b], projected[b][1], *gathered[b], info[b], xs[b], output_weight, gain2
        )
        return outs[:4], outs[4]

    gathered[0] = (near, after(far, up_pair))
    kept0, n20 = forward(0)
    n20, up_got, *sent1 = fence(n20, up_got, *sent1)
    n2_sent0 = swap(n20, across)
    near = jnp.stack([projected[1][0]] + list(sent1))
    far = swap(near, core)
    up_near = [
        jnp.concatenate([ups[b], up_got[b * local : (b + 1) * local]], axis=0)
        for b in range(rows)
    ]
    near, far, *up_near = fence(near, far, *up_near)
    gathered.append((near, far))
    up_far = [swap(up_near[b], core) for b in range(rows)]
    kept1, n21 = forward(1)
    n2_sent1 = swap(n21, across)
    n21, up_far0, up_far1, n2_sent0, other_weights = fence(
        n21, *up_far, n2_sent0, other_weights
    )
    weights = jnp.concatenate([own_weights, other_weights], axis=1)
    attended = (kept0, kept1)

    near0 = jnp.concatenate([n20, n2_sent0], axis=0)
    far0 = swap(near0, core)
    sn0, bn0, grads = feed_forward(at_y, near0, up_near[0], weights)
    sn0, bn0, grads, far0 = fence(sn0, bn0, grads, far0)
    sf0, bf0, grads = feed_forward(at_y, far0, up_far0, weights, grads)
    sf0, bf0, grads, n2_sent1 = fence(sf0, bf0, grads, n2_sent1)
    near1 = jnp.concatenate([n21, n2_sent1], axis=0)
    far1 = swap(near1, core)
    sf0_got = swap(sf0, core)
    sn1, bn1, grads = feed_forward(at_y, near1, up_near[1], weights, grads)
    sn1, bn1, grads, sf0_got, far1 = fence(sn1, bn1, grads, sf0_got, far1)
    sum0 = add(sn0, sf0_got)
    theirs = sum0[local:]
    across0 = swap(theirs, across)
    sf1, bf1, grads = feed_forward(
        at_y, after(far1, theirs), up_far1, weights, grads, True
    )
    sf1, bf1, grads, across0 = fence(sf1, bf1, grads, across0)
    block_part = lax.psum_scatter(
        grads.reshape(-1, width), ("y", "batch"), scatter_dimension=0, tiled=True
    )

    def residual_of(b, mine, got):
        mixed, out_t, lse, hidden = attended[b]
        return residual(
            mine, got, ups[b], hidden, gain2, output_weight, out_t, (0, 1, 2, 3, 5, 6)
        )

    sf1_got = swap(sf1, core)
    residual0 = residual_of(0, sum0[:local], across0)
    *residual0, sf1_got = fence(*residual0, sf1_got)
    sum1 = add(sn1, sf1_got)
    theirs = sum1[local:]

    def back(b, outs, *hold):
        res, low, dot, delta, gain_share = outs
        fac, qt, qmix, qbase, normed = projected[b]
        return attend_backward(
            (40, 0.1)[b], spans[b], qt, *gathered[b], info[b], after(dot, *hold), attended[b][2], delta,
            qmix, qbase, cosine[b], sine[b],
        )

    across1 = swap(theirs, across)
    bf_got = [swap(value, core) for value in (bf0, bf1)]
    dnear0, dfar0, dq0 = back(0, residual0, theirs)
    dnear0, dfar0, dq0, across1, *bf_got = fence(dnear0, dfar0, dq0, across1, *bf_got)
    dfar0_got = swap(dfar0, core)
    residual1 = residual_of(1, sum1[:local], across1)
    *residual1, dnear0, dfar0_got = fence(*residual1, dnear0, dfar0_got)
    residuals = (residual0, residual1)
    fsum0 = add(dnear0, dfar0_got)
    fparts0 = send_slots(fsum0)
    dnear1, dfar1, dq1 = back(1, residual1, fsum0)
    dnear1, dfar1, dq1, *fparts0 = fence(dnear1, dfar1, dq1, *fparts0)

    dfar1_got = swap(dfar1, core)
    dfar1_got, dnear1 = fence(dfar1_got, dnear1)
    fsum1 = add(dnear1, dfar1_got)
    fparts1 = send_slots(fsum1)
    wo_near, wo_far = output_weight_shares(
        lax.axis_index("core").astype(jnp.int32).reshape(1),
        [after(attended[0][0], fsum1), attended[1][0]],
        [residuals[b][1] for b in range(rows)],
        n,
    )
    wo_got = swap(wo_far, core)
    branch_mine, branch_theirs = branch_sums([after(bn0, wo_near), bn1], bf_got)
    block_part, fsum1, wo_near, branch_mine, branch_theirs = fence(
        block_part, fsum1, wo_near, branch_mine, branch_theirs
    )
    block_grad = lax.all_gather(block_part, "batch", axis=0, tiled=True)
    *fparts1, fsum1, wo_got = fence(*fparts1, fsum1, wo_got)
    low0, low1, near, far = share(
        me.reshape(1),
        [fsum0[0]] + list(fparts0),
        [fsum1[0]] + list(fparts1),
        (dq0, dq1),
        cosine,
        sine,
        [projected[b][4] for b in range(rows)],
        (residual0[4], residual1[4]),
        n,
    )
    far_got = swap(far, core)
    far_got, near = fence(far_got, near)
    small = add(near, far_got)
    small_sent = send_slots(small)
    wo_sum = add(wo_near, after(wo_got, small))
    wo_parts = lax.all_to_all(wo_sum, ("y", "x"), 0, 0, tiled=True)
    *small_sent, small = fence(*small_sent, small)
    small = add(small[0], *small_sent)
    small_got = swap_batch(small, 1)
    branch_got = swap(after(branch_theirs, small), across)
    grads = [
        finish(after((low0, low1)[b], small), xs[b], gain1, residuals[b][0], narrow)
        for b in range(rows)
    ]
    tokens_gradient = in_order(jnp.stack(grads, axis=1))
    columns = jnp.concatenate(
        [
            lax.dynamic_slice_in_dim(w, after(me, small) * (width // n), width // n, 0)
            for w in projections
        ],
        axis=1,
    ).astype(F32).T
    small_got, small, wo_parts, tokens_gradient, columns = fence(
        small_got, small, wo_parts, tokens_gradient, columns
    )
    small = add(small, small_got)
    small_got = swap_batch(small, depth - 1)
    wo_total = jnp.sum(after(wo_parts, small).astype(F32), axis=0).astype(BF16)
    wo_got = swap_batch(wo_total, 1)
    outputs = []
    for b in range(rows):
        mine = branch_mine[b * local : (b + 1) * local].astype(F32)
        got = after(branch_got, wo_total)[b * local : (b + 1) * local].astype(F32)
        outputs.append(
            jnp.where(valid[b][:, None], attended[b][3] + (mine + got), 0.0).astype(BF16)
        )
    output = in_order(jnp.stack(outputs, axis=1))
    wo_got, wo_total, output, block_grad = fence(wo_got, wo_total, output, block_grad)
    wo_total = add(wo_total, wo_got)
    wo_got = swap_batch(wo_total, depth - 1)
    small = small.astype(F32) + after(small_got, wo_total).astype(F32)
    hid = gate_weight.shape[1]
    down_grad = block_grad[:hid].astype(F32)
    gate_grad = block_grad[hid : 2 * hid].astype(F32).T
    lift_grad = block_grad[2 * hid :].astype(F32).T
    output_weight_grad = wo_total.astype(F32) + after(wo_got, small).astype(F32)
    count = width // n

    def pick(at, size):
        return small[at : at + size].T

    query_heads_grad = pick(0, QMIX)
    query_basis_grad = pick(QMIX, QBASE)
    at = QMIX + QBASE
    key_heads_grad = pick(at, MIX)
    key_basis_grad = pick(at + MIX, BASE)
    value_heads_grad = pick(at + MIX + BASE, MIX)
    value_basis_grad = pick(at + 2 * MIX + BASE, BASE)
    at = at + FACTORS
    second_gain_grad = small[at].reshape(count)
    weighted = small[:at] * columns
    own_gain = lax.dynamic_slice_in_dim(first_gain, me * count, count, 0)
    first_gain_grad = jnp.sum(weighted, axis=0) / own_gain

    return (
        output,
        tokens_gradient,
        first_gain_grad,
        query_heads_grad,
        query_basis_grad,
        key_heads_grad,
        key_basis_grad,
        value_heads_grad,
        value_basis_grad,
        output_weight_grad,
        second_gain_grad,
        gate_grad,
        lift_grad,
        down_grad,
    )


def solution(mesh):
    batch, wide = mesh.shape["batch"], mesh.shape["wide"]
    split = wide == 8 and batch == 4
    w = "wide"
    if split:
        mesh = jax.sharding.Mesh(
            mesh.devices.reshape(batch, 2, 2, 2), ("batch", "y", "x", "core")
        )
        w = ("y", "x", "core")
    rows = P(w, "batch", None)
    return jax.shard_map(
        body if split else general_body,
        mesh=mesh,
        in_specs=(rows, P("batch", None), rows)
        + (P(),) * 9
        + (P(None, w), P(None, w), P(w, None)),
        out_specs=(rows, rows, P(w))
        + (P(w, None),) * 7
        + (P(w), P(None, w), P(None, w), P(w, None)),
        check_vma=False,
    )
```

```python
import functools

import jax
import jax.numpy as jnp
from jax import lax
from jax.experimental import pallas as pl
from jax.experimental.pallas import tpu as pltpu
from jax.experimental.layout import Layout, with_layout_constraint
from jax.sharding import PartitionSpec as P

HEADS = 16
HEAD_DIM = 64
Q_RANK = 6
KV_RANK = 2
HALF = HEAD_DIM // 2
MIX = HEADS * KV_RANK
BASE = KV_RANK * HEAD_DIM
FACTORS = 2 * MIX + 2 * BASE
QMIX = HEADS * Q_RANK
QBASE = Q_RANK * HEAD_DIM
QUAD = 4
QUADS = HEADS // QUAD
QW = QUAD * HEAD_DIM
TILE = 128
F32 = jnp.float32
BF16 = jnp.bfloat16
NEG = -1e30
MIB = 1 << 20


def mm(a, b):
    return jnp.dot(a, b, preferred_element_type=F32)


def mm_nt(a, b):
    return lax.dot_general(a, b, (((1,), (1,)), ((), ())), preferred_element_type=F32)


def mm_tn(a, b):
    return lax.dot_general(a, b, (((0,), (0,)), ((), ())), preferred_element_type=F32)


def whole(count):
    return [pl.BlockSpec(memory_space=pltpu.VMEM)] * count


def streamed(shape):
    return pl.BlockSpec(shape, lambda *_, rank=len(shape): (0,) * rank)


def kernel_call(
    kernel, name, outs, scratch, smem, limit, micros, *args, kept=(), far=(), aliases={}
):
    specs = [
        pl.BlockSpec(memory_space=pltpu.SMEM)
        if i < smem
        else streamed(arg.shape)
        if i in far
        else pl.BlockSpec(memory_space=pltpu.VMEM)
        for i, arg in enumerate(args)
    ]
    return pl.pallas_call(
        kernel,
        out_shape=tuple(
            pltpu.HBM(s, t) if i in kept else jax.ShapeDtypeStruct(s, t)
            for i, (s, t) in enumerate(outs)
        ),
        in_specs=specs,
        out_specs=[
            streamed(s) if i in kept else pl.BlockSpec(memory_space=pltpu.VMEM)
            for i, (s, _) in enumerate(outs)
        ],
        scratch_shapes=scratch,
        compiler_params=pltpu.CompilerParams(vmem_limit_bytes=limit * MIB),
        cost_estimate=pl.CostEstimate(
            flops=int(micros * 1e9), transcendentals=0, bytes_accessed=int(micros * 1e6)
        ),
        input_output_aliases=aliases,
        name=name,
    )(
        *(
            pltpu.with_memory_space_constraint(arg, pltpu.HBM) if i in far else arg
            for i, arg in enumerate(args)
        )
    )


def project_kernel(
    x_ref, gain_ref, qh_ref, qb_ref, kh_ref, kb_ref, vh_ref, vb_ref, cos_ref, sin_ref,
    fac_ref, qt_ref, qmix_ref, qbase_ref, normed_ref,
):
    x = x_ref[...].astype(F32)
    scale = lax.rsqrt(jnp.mean(x * x, axis=-1, keepdims=True) + 1e-06)
    normed = (x * scale * gain_ref[...]).astype(BF16)
    normed_ref[...] = normed
    cos = cos_ref[...]
    sin = sin_ref[...]

    def rope(v):
        a, b = v[:HALF], v[HALF:]
        return jnp.concatenate([a * cos - b * sin, a * sin + b * cos], axis=0)

    kb = mm(normed, kb_ref[...]).T
    fac_ref[0:MIX, :] = mm_nt(kh_ref[...], normed).astype(BF16)
    for r in range(KV_RANK):
        at = MIX + r * HEAD_DIM
        fac_ref[at : at + HEAD_DIM, :] = rope(kb[r * HEAD_DIM : (r + 1) * HEAD_DIM]).astype(BF16)
    fac_ref[MIX + BASE : 2 * MIX + BASE, :] = mm_nt(vh_ref[...], normed).astype(BF16)
    fac_ref[2 * MIX + BASE :, :] = mm(normed, vb_ref[...]).T.astype(BF16)
    qmix = mm_nt(qh_ref[...], normed)
    qmix_ref[...] = qmix
    raw = mm(normed, qb_ref[...]).T
    base = [rope(raw[r * HEAD_DIM : (r + 1) * HEAD_DIM]) for r in range(Q_RANK)]
    for r in range(Q_RANK):
        qbase_ref[r * HEAD_DIM : (r + 1) * HEAD_DIM, :] = base[r]
    for h in range(HEADS):
        out = None
        for r in range(Q_RANK):
            part = qmix[h * Q_RANK + r : h * Q_RANK + r + 1, :] * base[r]
            out = part if out is None else out + part
        qt_ref[h * HEAD_DIM : (h + 1) * HEAD_DIM, :] = (
            (out * (1.0 / Q_RANK)).astype(BF16) * (HEAD_DIM ** -0.5)
        ).astype(BF16)


def project(x, gain, weights, cos, sin):
    local, d = x.shape
    width = HEADS * HEAD_DIM
    return kernel_call(
        project_kernel,
        "project",
        (
            ((FACTORS, local), BF16),
            ((width, local), BF16),
            ((QMIX, local), F32),
            ((QBASE, local), F32),
            ((local, d), BF16),
        ),
        [],
        0,
        16,
        2,
        x, gain, *weights, cos, sin,
        kept=(1, 2, 3, 4),
    )


def materialize(fac, offset, head):
    base = offset + MIX
    out = None
    for r in range(KV_RANK):
        row = offset + head * KV_RANK + r
        part = fac[row : row + 1, :] * fac[base + r * HEAD_DIM : base + (r + 1) * HEAD_DIM, :]
        out = part if out is None else out + part
    return (out * (1.0 / KV_RANK)).astype(BF16)


def materialize_quad(fac, offset, quad):
    return jnp.concatenate(
        [materialize(fac, offset, quad * QUAD + i) for i in range(QUAD)], axis=0
    )


def each_block(me, lo, hi, slots, do):
    for slot in range(slots):
        kb = jnp.bitwise_xor(me, slot)
        pl.when((kb >= lo) & (kb < hi))(functools.partial(do, slot, kb))


def block_factors(slot, near, far):
    return (far if slot & 1 else near)[slot >> 1].astype(F32)


def forward_kernel(
    span, qt_ref, near_ref, far_ref, info_ref, x_ref, wo_ref, gain_ref,
    mixed_ref, out_t_ref, lse_ref, hidden_ref, n2_ref,
    k_s, vt_s, qbd_s, acc_s, m_s, l_s, bias_s,
):
    slots, kb_size, _ = k_s.shape
    count = qt_ref.shape[1]
    lo, hi, me = span[0], span[1], span[2]

    def prepare(slot, kb):
        fac = block_factors(slot, near_ref, far_ref)
        for quad in range(QUADS):
            rows = slice(quad * QW, (quad + 1) * QW)
            k_s[kb, :, rows] = materialize_quad(fac, 0, quad).T
            vt_s[kb, rows, :] = materialize_quad(fac, MIX + BASE, quad)

    each_block(me, lo, hi, slots, prepare)
    qbd_s[...] = jnp.zeros_like(qbd_s)
    for h in range(HEADS):
        quad, i = h // QUAD, h % QUAD
        qbd_s[quad, i * HEAD_DIM : (i + 1) * HEAD_DIM, i * count : (i + 1) * count] = qt_ref[
            h * HEAD_DIM : (h + 1) * HEAD_DIM, :
        ]
    m_s[...] = jnp.full_like(m_s, NEG)
    l_s[...] = jnp.zeros_like(l_s)
    acc_s[...] = jnp.zeros_like(acc_s)
    first = info_ref[0:1, :]
    last = info_ref[1:2, :]

    def step(kb, _):
        places = kb * kb_size + lax.broadcasted_iota(jnp.int32, (kb_size, count), 0)
        bias_s[...] = jnp.where((places >= first) & (places <= last), 0.0, NEG)
        for quad in range(QUADS):
            s = mm(k_s[kb, :, quad * QW : (quad + 1) * QW], qbd_s[quad])
            ps = []
            alphas = []
            for i in range(QUAD):
                h = quad * QUAD + i
                sh = s[:, i * count : (i + 1) * count] + bias_s[...]
                old = m_s[h : h + 1, :]
                new = jnp.maximum(old, jnp.max(sh, axis=0, keepdims=True))
                alpha = jnp.exp(old - new)
                p = jnp.exp(sh - new)
                m_s[h : h + 1, :] = new
                l_s[h : h + 1, :] = l_s[h : h + 1, :] * alpha + jnp.sum(p, axis=0, keepdims=True)
                ps.append(p.astype(BF16))
                alphas.append(alpha)
            for j in range(QUAD // 2):
                both = jnp.concatenate(ps[2 * j : 2 * j + 2], axis=1)
                at = quad * QW + j * 2 * HEAD_DIM
                o = mm(vt_s[kb, at : at + 2 * HEAD_DIM, :], both)
                for i in range(2):
                    r = slice(at + i * HEAD_DIM, at + (i + 1) * HEAD_DIM)
                    acc_s[r, :] = (
                        acc_s[r, :] * alphas[2 * j + i]
                        + o[i * HEAD_DIM : (i + 1) * HEAD_DIM, i * count : (i + 1) * count]
                    )
        return 0

    lax.fori_loop(lo, hi, step, 0)
    lse_ref[...] = m_s[...] + jnp.log(l_s[...])
    for h in range(HEADS):
        rows = slice(h * HEAD_DIM, (h + 1) * HEAD_DIM)
        out_t_ref[rows, :] = acc_s[rows, :] * (1.0 / l_s[h : h + 1, :])

    mixed = out_t_ref[...].astype(BF16).T
    mixed_ref[...] = mixed
    hidden = x_ref[...].astype(F32) + mm(mixed, wo_ref[...])
    hidden_ref[...] = hidden
    scale = lax.rsqrt(jnp.mean(hidden * hidden, axis=-1, keepdims=True) + 1e-06)
    n2_ref[...] = (hidden * scale * gain_ref[...]).astype(BF16)


def attend_forward(span, qt, near, far, info, x, wo, gain):
    width, local = qt.shape
    kb = local
    blocks = 2 * near.shape[0]
    d = x.shape[1]
    return kernel_call(
        forward_kernel,
        "attend_forward",
        (
            ((local, width), BF16),
            ((width, local), F32),
            ((HEADS, local), F32),
            ((local, d), F32),
            ((local, d), BF16),
        ),
        [
            pltpu.VMEM((blocks, kb, width), BF16),
            pltpu.VMEM((blocks, width, kb), BF16),
            pltpu.VMEM((QUADS, QW, QUAD * local), BF16),
            pltpu.VMEM((width, local), F32),
            pltpu.VMEM((HEADS, local), F32),
            pltpu.VMEM((HEADS, local), F32),
            pltpu.VMEM((kb, local), F32),
        ],
        1,
        32,
        10,
        span, qt, near, far, info, x, wo, gain,
        kept=(0, 1, 2, 3),
    )


def ffn_kernel(first, final, *refs):
    at_y, n2_ref, up_ref, w_ref = refs[:4]
    prev = None if first else refs[4]
    sng_ref, branch_ref, sums = refs[-3:]
    n2 = n2_ref[...]
    up = up_ref[...]
    hid = w_ref.shape[1]
    gate = mm_nt(n2, w_ref[0])
    lifted = mm_nt(n2, w_ref[1])
    hidden_grad = mm_nt(up, w_ref[2])
    sigmoid = jax.nn.sigmoid(gate)
    silu = gate * sigmoid
    act = (silu * lifted).astype(BF16)
    gate_grad = (hidden_grad * lifted * (sigmoid * (1.0 + gate * (1.0 - sigmoid)))).astype(BF16)
    lift_grad = (hidden_grad * silu).astype(BF16)
    sng_ref[...] = (mm(gate_grad, w_ref[0]) + mm(lift_grad, w_ref[1])).astype(BF16)
    branch_ref[...] = mm(act, w_ref[2]).astype(BF16)
    for at, (left, right) in enumerate(((act, up), (gate_grad, n2), (lift_grad, n2))):
        grad = mm_tn(left, right)
        if not first:
            grad = grad + prev[at]
        if not final:
            sums[at] = grad
        else:
            half = hid // 2
            low = grad.astype(BF16)
            sums[at_y[0], at] = low[:half]
            sums[1 - at_y[0], at] = low[half:]


def feed_forward(at_y, n2, up, weights, prev=None, final=False):
    count, d = n2.shape
    hid = weights.shape[1]
    if final:
        grads = (((2, 3, hid // 2, d), BF16),)
    else:
        grads = ((weights.shape, F32),)
    args = (at_y, n2, up, weights) if prev is None else (at_y, n2, up, weights, prev)
    return kernel_call(
        functools.partial(ffn_kernel, prev is None, final),
        "feed_forward",
        (((count, d), BF16),) * 2 + grads,
        [],
        1,
        19,
        0.05,
        *args,
        kept=(1, 2) if final else (1,),
        aliases={} if prev is None or final else {4: 2},
    )


def residual_kernel(
    sa, sb, up_ref, hidden_ref, gain_ref, wo_ref, out_t_ref,
    res_ref, low_ref, dot_ref, delta_ref, gain_out,
):
    sng = sa[...].astype(F32) + sb[...].astype(F32)
    hidden = hidden_ref[...]
    scale = lax.rsqrt(jnp.mean(hidden * hidden, axis=-1, keepdims=True) + 1e-06)
    gain_out[...] = jnp.sum(sng * (hidden * scale), axis=0, keepdims=True)
    weighted = sng * gain_ref[...]
    inner = jnp.mean(hidden * weighted, axis=-1, keepdims=True)
    res = up_ref[...].astype(F32) + scale * weighted - hidden * (scale * scale * scale) * inner
    res_ref[...] = res
    low = res.astype(BF16)
    low_ref[...] = low
    dot = mm_nt(wo_ref[...], low).astype(BF16)
    dot_ref[...] = dot
    for h in range(HEADS):
        rows = slice(h * HEAD_DIM, (h + 1) * HEAD_DIM)
        delta_ref[h : h + 1, :] = jnp.sum(
            dot[rows].astype(F32) * out_t_ref[rows, :], axis=0, keepdims=True
        )


def residual(sa, sb, up, hidden, gain, wo, out_t, far=()):
    local, d = hidden.shape
    width = out_t.shape[0]
    return kernel_call(
        residual_kernel,
        "residual",
        (
            ((local, d), F32),
            ((local, d), BF16),
            ((width, local), BF16),
            ((HEADS, local), F32),
            ((1, d), F32),
        ),
        [],
        0,
        16,
        3,
        sa, sb, up, hidden, gain, wo, out_t,
        kept=(0, 2, 3),
        far=far,
    )


def backward_kernel(
    span, qt_ref, near_ref, far_ref, info_ref, dot_ref, lse_ref, delta_ref,
    qmix_ref, qbase_ref, cos_ref, sin_ref,
    dnear_ref, dfar_ref, dq_ref,
    k_s, kt_s, vt_s, dkt_s, dvt_s, qbd_s, qbdt_s, obd_s, obdt_s, dq_s, bias_s, lse_s, delta_s,
):
    slots, kb_size, _ = k_s.shape
    count = qt_ref.shape[1]
    lo, hi, me = span[0], span[1], span[2]
    dnear_ref[...] = jnp.zeros_like(dnear_ref)
    dfar_ref[...] = jnp.zeros_like(dfar_ref)

    def prepare(slot, kb):
        fac = block_factors(slot, near_ref, far_ref)
        for quad in range(QUADS):
            rows = slice(quad * QW, (quad + 1) * QW)
            kt = materialize_quad(fac, 0, quad)
            kt_s[kb, rows, :] = kt
            k_s[kb, :, rows] = kt.T
            vt_s[kb, rows, :] = materialize_quad(fac, MIX + BASE, quad)
            dkt_s[kb, rows, :] = jnp.zeros((QW, kb_size), F32)
            dvt_s[kb, rows, :] = jnp.zeros((QW, kb_size), F32)

    each_block(me, lo, hi, slots, prepare)
    qbdt_s[...] = jnp.zeros_like(qbdt_s)
    obdt_s[...] = jnp.zeros_like(obdt_s)

    for h in range(HEADS):
        quad, i = h // QUAD, h % QUAD
        to = slice(i * HEAD_DIM, (i + 1) * HEAD_DIM)
        at = slice(i * count, (i + 1) * count)
        rows = slice(h * HEAD_DIM, (h + 1) * HEAD_DIM)
        qbdt_s[quad, to, at] = qt_ref[rows, :]
        obdt_s[quad, to, at] = dot_ref[rows, :]
    for quad in range(QUADS):
        qbd_s[quad] = qbdt_s[quad].T
        obd_s[quad] = obdt_s[quad].T
    lse_t = lse_ref[:, :].T
    delta_t = delta_ref[:, :].T
    for h in range(HEADS):
        lse_s[h] = jnp.broadcast_to(lse_t[:, h : h + 1], (count, TILE))
        delta_s[h] = jnp.broadcast_to(delta_t[:, h : h + 1], (count, TILE))
    dq_s[...] = jnp.zeros_like(dq_s)
    info_t = info_ref[:, :].T
    first = info_t[:, 0:1]
    last = info_t[:, 1:2]

    def step(kb, _):
        places = kb * kb_size + lax.broadcasted_iota(jnp.int32, (count, kb_size), 1)
        bias_s[...] = jnp.where((places >= first) & (places <= last), 0.0, NEG)
        lane = lax.broadcasted_iota(jnp.int32, (count, QW), 1) // HEAD_DIM
        for quad in range(QUADS):
            rows = slice(quad * QW, (quad + 1) * QW)
            s = mm(qbd_s[quad], kt_s[kb, rows, :])
            dp = mm(obd_s[quad], vt_s[kb, rows, :])
            ps = []
            dss = []
            for i in range(QUAD):
                h = quad * QUAD + i
                at = slice(i * count, (i + 1) * count)
                lse = jnp.concatenate([lse_s[h]] * (kb_size // TILE), axis=1)
                delta = jnp.concatenate([delta_s[h]] * (kb_size // TILE), axis=1)
                p = jnp.exp((s[at] + bias_s[...]) - lse)
                ps.append(p.astype(BF16))
                dss.append((p * (dp[at] - delta)).astype(BF16))
            p4 = jnp.concatenate(ps, axis=0)
            ds4 = jnp.concatenate(dss, axis=0)
            dkt_s[kb, rows, :] += mm(qbdt_s[quad], ds4)
            dvt_s[kb, rows, :] += mm(obdt_s[quad], p4)
            dq = mm(ds4, k_s[kb, :, rows])
            out = dq[0:count]
            for i in range(1, QUAD):
                out = jnp.where(lane == i, dq[i * count : (i + 1) * count], out)
            dq_s[:, rows] += out
        return 0

    lax.fori_loop(lo, hi, step, 0)
    dqt = dq_s[...].T * (HEAD_DIM ** -0.5 / Q_RANK)
    qmix = qmix_ref[:, :]
    mixes = []
    for h in range(HEADS):
        part = dqt[h * HEAD_DIM : (h + 1) * HEAD_DIM, :]
        for r in range(Q_RANK):
            mixes.append(
                jnp.sum(
                    part * qbase_ref[r * HEAD_DIM : (r + 1) * HEAD_DIM, :], axis=0, keepdims=True
                )
            )
    dq_ref[:QMIX, :] = jnp.concatenate(mixes, axis=0).astype(BF16)
    cos = cos_ref[...]
    sin = sin_ref[...]
    for r in range(Q_RANK):
        out = None
        for h in range(HEADS):
            row = h * Q_RANK + r
            part = qmix[row : row + 1, :] * dqt[h * HEAD_DIM : (h + 1) * HEAD_DIM, :]
            out = part if out is None else out + part
        upper, lower = out[:HALF], out[HALF:]
        at = QMIX + r * HEAD_DIM
        dq_ref[at : at + HALF, :] = (upper * cos + lower * sin).astype(BF16)
        dq_ref[at + HALF : at + HEAD_DIM, :] = (lower * cos - upper * sin).astype(BF16)

    def fold(slot, kb):
        fac = block_factors(slot, near_ref, far_ref)
        to = dfar_ref if slot & 1 else dnear_ref
        for offset, grad in ((0, dkt_s), (MIX + BASE, dvt_s)):
            outs = [None] * KV_RANK
            mixes = []
            for h in range(HEADS):
                g = grad[kb, h * HEAD_DIM : (h + 1) * HEAD_DIM, :] * (1.0 / KV_RANK)
                for r in range(KV_RANK):
                    at = offset + MIX + r * HEAD_DIM
                    mixes.append(jnp.sum(g * fac[at : at + HEAD_DIM, :], axis=0, keepdims=True))
                    row = offset + h * KV_RANK + r
                    part = fac[row : row + 1, :] * g
                    outs[r] = part if outs[r] is None else outs[r] + part
            to[slot >> 1, offset : offset + MIX, :] = jnp.concatenate(mixes, axis=0).astype(BF16)
            for r in range(KV_RANK):
                at = offset + MIX + r * HEAD_DIM
                to[slot >> 1, at : at + HEAD_DIM, :] = outs[r].astype(BF16)

    each_block(me, lo, hi, slots, fold)


def attend_backward(micros, span, qt, near, far, info, dot, lse, delta, qmix, qbase, cos, sin):
    width, local = qt.shape
    kb = local
    blocks = 2 * near.shape[0]
    return kernel_call(
        backward_kernel,
        "attend_backward",
        (
            (near.shape, BF16),
            (near.shape, BF16),
            ((QMIX + QBASE, local), BF16),
        ),
        [
            pltpu.VMEM((blocks, kb, width), BF16),
            pltpu.VMEM((blocks, width, kb), BF16),
            pltpu.VMEM((blocks, width, kb), BF16),
            pltpu.VMEM((blocks, width, kb), F32),
            pltpu.VMEM((blocks, width, kb), F32),
            pltpu.VMEM((QUADS, QUAD * local, QW), BF16),
            pltpu.VMEM((QUADS, QW, QUAD * local), BF16),
            pltpu.VMEM((QUADS, QUAD * local, QW), BF16),
            pltpu.VMEM((QUADS, QW, QUAD * local), BF16),
            pltpu.VMEM((local, width), F32),
            pltpu.VMEM((local, kb), F32),
            pltpu.VMEM((HEADS, local, TILE), F32),
            pltpu.VMEM((HEADS, local, TILE), F32),
        ],
        1,
        56,
        micros,
        span, qt, near, far, info, dot, lse, delta, qmix, qbase, cos, sin,
        far=(1, 5, 6, 7, 8, 9),
    )


def share_kernel(*refs):
    me = refs[0]
    pieces = (refs[1:5], refs[5:9])
    dqs, coss, sins, normeds, gains = refs[9:11], refs[11:13], refs[13:15], refs[15:17], refs[17:19]
    lows = refs[19:21]
    near_ref, far_ref, all_s = refs[21:]
    query = QMIX + QBASE
    for b in range(2):
        first, second, third, fourth = (piece[...].astype(F32) for piece in pieces[b])
        total = (first + second) + (third + fourth)
        cos = coss[b][...]
        sin = sins[b][...]
        low_ref = lows[b]
        low_ref[:query, :] = dqs[b][...]
        low_ref[query:, :] = total.astype(BF16)
        for r in range(KV_RANK):
            at = MIX + r * HEAD_DIM
            upper, lower = total[at : at + HALF], total[at + HALF : at + HEAD_DIM]
            to = query + at
            low_ref[to : to + HALF, :] = (upper * cos + lower * sin).astype(BF16)
            low_ref[to + HALF : to + HEAD_DIM, :] = (lower * cos - upper * sin).astype(BF16)
    rows = query + FACTORS
    all_s[:rows, :] = mm(
        jnp.concatenate([low[...] for low in lows], axis=1),
        jnp.concatenate([normed[...] for normed in normeds], axis=0),
    )
    all_s[rows:, :] = jnp.concatenate(
        [gains[0][...] + gains[1][...], jnp.zeros((15, gains[0].shape[1]), F32)], axis=0
    )
    width = near_ref.shape[2]
    for is_far, ref in ((0, near_ref), (1, far_ref)):
        for slot in range(ref.shape[0]):
            at = pl.multiple_of(jnp.bitwise_xor(me[0], 2 * slot + is_far) * width, width)
            ref[slot] = all_s[:, pl.ds(at, width)].astype(BF16)


def share(me, pieces0, pieces1, dqs, cosine, sine, normeds, gains, slots):
    local, d = normeds[0].shape
    count = QMIX + QBASE + FACTORS
    return kernel_call(
        share_kernel,
        "share",
        (((count, local), BF16),) * 2 + (((slots // 2, count + 16, d // slots), BF16),) * 2,
        [pltpu.VMEM((count + 16, d), F32)],
        1,
        18,
        0.05,
        me, *pieces0, *pieces1, *dqs, cosine[0], cosine[1], sine[0], sine[1], *normeds, *gains,
        far=tuple(range(1, 17)),
        kept=(0, 1),
    )


def finish_kernel(*refs):
    low_ref, x_ref, gain_ref, res_ref = refs[:4]
    weights = refs[4:10]
    grad_ref = refs[10]
    low = low_ref[...].T
    grad = None
    at = 0
    for ref in weights:
        if ref.shape[0] == x_ref.shape[1]:
            count = ref.shape[1]
            part = mm_nt(low[:, at : at + count], ref[...])
        else:
            count = ref.shape[0]
            part = mm(low[:, at : at + count], ref[...])
        grad = part if grad is None else grad + part
        at += count
    x = x_ref[...].astype(F32)
    scale = lax.rsqrt(jnp.mean(x * x, axis=-1, keepdims=True) + 1e-06)
    weighted = grad * gain_ref[...]
    inner = jnp.mean(x * weighted, axis=-1, keepdims=True)
    grad_ref[...] = res_ref[...] + (scale * weighted - x * (scale * scale * scale) * inner)


def finish(low, x, gain, res, weights):
    local, d = x.shape
    return kernel_call(
        finish_kernel,
        "finish",
        (((local, d), F32),),
        [],
        0,
        16,
        0.05,
        low, x, gain, res, *weights,
        far=(1, 3, 4, 5, 6, 7, 8, 9),
    )[0]


def output_weight_kernel(core, m0, m1, low0, low1, near_ref, far_ref, all_s):
    all_s[...] = mm_tn(m0[...], low0[...]) + mm_tn(m1[...], low1[...])
    count = near_ref.shape[1]
    for chip in range(near_ref.shape[0]):
        for at, ref in ((core[0], near_ref), (1 - core[0], far_ref)):
            row = pl.multiple_of((2 * chip + at) * count, count)
            ref[chip] = all_s[pl.ds(row, count), :].astype(BF16)


def output_weight_shares(core, mixed, lows, slots):
    width, d = mixed[0].shape[1], lows[0].shape[1]
    return kernel_call(
        output_weight_kernel,
        "output_weight_shares",
        (((slots // 2, width // slots, d), BF16),) * 2,
        [pltpu.VMEM((width, d), F32)],
        1,
        16,
        0.05,
        core, *mixed, *lows,
        far=(1, 2, 3, 4),
    )


def branch_kernel(n0, n1, f0, f1, mine_ref, theirs_ref):
    half = mine_ref.shape[0] // 2
    for b, (near, far) in enumerate(((n0, f0), (n1, f1))):
        total = (near[...].astype(F32) + far[...].astype(F32)).astype(BF16)
        mine_ref[b * half : (b + 1) * half, :] = total[:half]
        theirs_ref[b * half : (b + 1) * half, :] = total[half:]


def branch_sums(nears, fars):
    return kernel_call(
        branch_kernel,
        "branch_sums",
        ((nears[0].shape, BF16),) * 2,
        [],
        0,
        16,
        0.05,
        *nears, *fars,
        kept=(0, 1),
        far=(0, 1, 2, 3),
    )


highest = lax.Precision.HIGHEST
masked_score = -1e30


def rms_scale(values):
    return lax.rsqrt(jnp.mean(values * values, axis=-1, keepdims=True) + 1e-06)


def norm_backward(values, gain, scaled, upstream):
    weighted = upstream * gain
    inner = jnp.mean(values * weighted, axis=-1, keepdims=True)
    return scaled * weighted - values * (scaled * scaled * scaled) * inner


def rotate(values, cosine, sine):
    half = values.shape[-1] // 2
    first = values[..., :half]
    second = values[..., half:]
    return jnp.concatenate(
        [first * cosine - second * sine, first * sine + second * cosine], axis=-1
    )


def row_layout(lengths_row, places):
    ends = jnp.cumsum(lengths_row)
    passed = ends[None, :] <= places[:, None]
    segment = jnp.sum(passed.astype(jnp.int32), axis=1)
    start = jnp.max(jnp.where(passed, ends[None, :], 0), axis=1)
    valid = places < ends[-1]
    return (segment, places - start, valid)


def rope_tables(position):
    half = HEAD_DIM // 2
    frequency = 10000.0 ** (-jnp.arange(half, dtype=jnp.float32) / half)
    angle = position.astype(jnp.float32)[..., None] * frequency
    return (jnp.cos(angle), jnp.sin(angle))


def split_factors(factors):
    mix_width = HEADS * KV_RANK
    base_width = KV_RANK * HEAD_DIM
    count, rows = (factors.shape[0], factors.shape[1])
    key_mix = factors[..., :mix_width].reshape(count, rows, HEADS, KV_RANK)
    key_base = factors[..., mix_width : mix_width + base_width].reshape(
        count, rows, KV_RANK, HEAD_DIM
    )
    value_mix = factors[..., mix_width + base_width : 2 * mix_width + base_width].reshape(
        count, rows, HEADS, KV_RANK
    )
    value_base = factors[..., 2 * mix_width + base_width :].reshape(count, rows, KV_RANK, HEAD_DIM)
    return (key_mix, key_base, value_mix, value_base)


def pair_gradient(hidden_grad, gate, lifted):
    sigmoid = jax.nn.sigmoid(gate)
    gate_grad = hidden_grad * lifted * (sigmoid * (1.0 + gate * (1.0 - sigmoid)))
    lift_grad = hidden_grad * (gate * sigmoid)
    return jnp.concatenate([gate_grad, lift_grad], axis=-1).astype(jnp.bfloat16)


def general_body(
    tokens,
    lengths,
    cotangent,
    first_gain,
    query_heads,
    query_basis,
    key_heads,
    key_basis,
    value_heads,
    value_basis,
    output_weight,
    second_gain,
    gate_weight,
    up_weight,
    down_projection_weight,
):
    local, batch_rows, width = tokens.shape
    total = local * lax.axis_size("wide")
    offset = lax.axis_index("wide") * local
    places = jnp.arange(total, dtype=jnp.int32)
    segment, position, valid = jax.vmap(row_layout, in_axes=(0, None))(lengths, places)
    own_places = offset + jnp.arange(local, dtype=jnp.int32)
    own_segment = lax.dynamic_slice_in_dim(segment, offset, local, 1)
    own_position = lax.dynamic_slice_in_dim(position, offset, local, 1)
    own_valid = lax.dynamic_slice_in_dim(valid, offset, local, 1)
    cosine, sine = rope_tables(jnp.transpose(own_position))
    cosine = cosine[:, :, None, :]
    sine = sine[:, :, None, :]
    keep_rows = jnp.transpose(own_valid)[:, :, None]
    scale = HEAD_DIM ** (-0.5)
    block_rows = min(512, total)
    block_count = total // block_rows
    mix_width = HEADS * KV_RANK
    base_width = KV_RANK * HEAD_DIM
    flat_rows = local * batch_rows
    inputs = tokens.astype(jnp.float32)
    first_scale = rms_scale(inputs)
    normed = (inputs * first_scale * first_gain).astype(jnp.bfloat16)
    flat = normed.reshape(flat_rows, width)
    query_mix = jnp.dot(flat, query_heads, preferred_element_type=jnp.float32).reshape(
        local, batch_rows, HEADS, Q_RANK
    )
    query_raw = jnp.dot(flat, query_basis, preferred_element_type=jnp.float32).reshape(
        local, batch_rows, Q_RANK, HEAD_DIM
    )
    query_base = rotate(query_raw, cosine, sine)
    factor_weight = jnp.concatenate([key_heads, key_basis, value_heads, value_basis], axis=1)
    factor_raw = jnp.dot(flat, factor_weight, preferred_element_type=jnp.float32).reshape(
        local, batch_rows, -1
    )
    key_roped = rotate(
        factor_raw[..., mix_width : mix_width + base_width].reshape(
            local, batch_rows, KV_RANK, HEAD_DIM
        ),
        cosine,
        sine,
    ).reshape(local, batch_rows, base_width)
    factors = jnp.concatenate(
        [factor_raw[..., :mix_width], key_roped, factor_raw[..., mix_width + base_width :]], axis=-1
    ).astype(jnp.bfloat16)
    every = lax.all_gather(factors, "wide", axis=0, tiled=True)
    key_mix, key_base, value_mix, value_base = split_factors(every)
    keys = (
        jnp.einsum("trhk,trkd->trhd", key_mix, key_base, preferred_element_type=jnp.float32)
        / KV_RANK
    ).astype(jnp.bfloat16)
    values = (
        jnp.einsum("trhk,trkd->trhd", value_mix, value_base, preferred_element_type=jnp.float32)
        / KV_RANK
    ).astype(jnp.bfloat16)
    query = (
        jnp.einsum(
            "trhk,trkd->trhd",
            query_mix,
            query_base,
            precision=highest,
            preferred_element_type=jnp.float32,
        )
        / Q_RANK
    ).astype(jnp.bfloat16)

    def block_view(block):
        start = block * block_rows
        key_places = start + jnp.arange(block_rows, dtype=jnp.int32)
        key_segment = lax.dynamic_slice_in_dim(segment, start, block_rows, 1)
        key_valid = lax.dynamic_slice_in_dim(valid, start, block_rows, 1)
        causal = key_places[None, :] <= own_places[:, None]
        itself = key_places[None, :] == own_places[:, None]
        allowed = (
            causal[None]
            & (own_segment[:, :, None] == key_segment[:, None, :])
            & (key_valid[:, None, :] | itself[None])
        )
        key_block = lax.dynamic_slice_in_dim(keys, start, block_rows, 0)
        value_block = lax.dynamic_slice_in_dim(values, start, block_rows, 0)
        product = (
            jnp.einsum("qrhd,krhd->rhqk", query, key_block, preferred_element_type=jnp.float32)
            * scale
        )
        scores = jnp.where(allowed[:, None], product, masked_score)
        return (start, scores, key_block, value_block)

    def max_step(carry, block):
        top, mass = carry
        scores = block_view(block)[1]
        higher = jnp.maximum(top, jnp.max(scores, axis=-1))
        mass = mass * jnp.exp(top - higher) + jnp.sum(jnp.exp(scores - higher[..., None]), axis=-1)
        return ((higher, mass), None)

    start_top = jnp.full((batch_rows, HEADS, local), masked_score, jnp.float32)
    (top, mass), _ = lax.scan(
        max_step, (start_top, jnp.zeros_like(start_top)), jnp.arange(block_count)
    )
    log_total = top + jnp.log(mass)

    def out_step(carry, block):
        _, scores, _, value_block = block_view(block)
        chances = jnp.exp(scores - log_total[..., None]).astype(jnp.bfloat16)
        return (
            carry
            + jnp.einsum(
                "rhqk,krhd->qrhd", chances, value_block, preferred_element_type=jnp.float32
            ),
            None,
        )

    attended, _ = lax.scan(
        out_step,
        jnp.zeros((local, batch_rows, HEADS, HEAD_DIM), jnp.float32),
        jnp.arange(block_count),
    )
    mixed = attended.astype(jnp.bfloat16).reshape(flat_rows, HEADS * HEAD_DIM)
    hidden_state = inputs + jnp.dot(
        mixed, output_weight, preferred_element_type=jnp.float32
    ).reshape(local, batch_rows, width)
    second_scale = rms_scale(hidden_state)
    normed_second = (hidden_state * second_scale * second_gain).astype(jnp.bfloat16)
    normalized_token_rows = lax.all_gather(normed_second, "wide", axis=0, tiled=True)
    gate_lifted_hidden = jnp.concatenate([gate_weight, up_weight], axis=1)
    hidden_width = gate_weight.shape[1]
    projected_output = jnp.einsum(
        "zec,cx->zex", normalized_token_rows, gate_lifted_hidden, preferred_element_type=jnp.float32
    )
    gate = projected_output[..., :hidden_width]
    lifted = projected_output[..., hidden_width:]
    silu_hidden_output = (jax.nn.silu(gate) * lifted).astype(jnp.bfloat16)
    sequence_portion = silu_hidden_output
    branch = lax.psum_scatter(
        jnp.einsum(
            "zyu,uv->zyv",
            sequence_portion,
            down_projection_weight,
            preferred_element_type=jnp.float32,
        ).astype(jnp.bfloat16),
        "wide",
        scatter_dimension=0,
        tiled=True,
    ).astype(jnp.float32)
    output = jnp.where(keep_rows, hidden_state + branch, 0.0).astype(jnp.bfloat16)
    upstream = jnp.where(keep_rows, cotangent.astype(jnp.float32), 0.0)
    upstream_low = upstream.astype(jnp.bfloat16)
    upstream_token_gradient = lax.all_gather(upstream_low, "wide", axis=0, tiled=True)
    hidden_grad = jnp.einsum(
        "ajg,vg->ajv",
        upstream_token_gradient,
        down_projection_weight,
        preferred_element_type=jnp.float32,
    )
    pair_product_gradient = pair_gradient(hidden_grad, gate, lifted)
    down_gradient = jnp.einsum(
        "imj,ima->ja",
        silu_hidden_output,
        upstream_token_gradient,
        preferred_element_type=jnp.float32,
    )
    pair_weight_grad = jnp.einsum(
        "ipl,ipj->lj",
        normalized_token_rows,
        pair_product_gradient,
        preferred_element_type=jnp.float32,
    )
    sequence_portion = pair_product_gradient
    second_normed_grad = lax.psum_scatter(
        jnp.einsum(
            "ivu,bu->ivb", sequence_portion, gate_lifted_hidden, preferred_element_type=jnp.float32
        ),
        "wide",
        scatter_dimension=0,
        tiled=True,
    )
    second_gain_partial = jnp.sum(second_normed_grad * (hidden_state * second_scale), axis=(0, 1))
    residual_grad = upstream + norm_backward(
        hidden_state, second_gain, second_scale, second_normed_grad
    )
    residual_low = residual_grad.astype(jnp.bfloat16).reshape(flat_rows, width)
    output_weight_grad = jnp.einsum(
        "tk,td->kd", mixed, residual_low, preferred_element_type=jnp.float32
    )
    mixed_grad = (
        jnp.einsum("td,kd->tk", residual_low, output_weight, preferred_element_type=jnp.float32)
        .astype(jnp.bfloat16)
        .reshape(local, batch_rows, HEADS, HEAD_DIM)
    )

    def delta_step(carry, block):
        _, scores, _, value_block = block_view(block)
        chances = jnp.exp(scores - log_total[..., None])
        pressure = jnp.einsum(
            "qrhd,krhd->rhqk", mixed_grad, value_block, preferred_element_type=jnp.float32
        )
        return (carry + jnp.sum(chances * pressure, axis=-1), None)

    delta, _ = lax.scan(
        delta_step, jnp.zeros((batch_rows, HEADS, local), jnp.float32), jnp.arange(block_count)
    )

    def grad_step(carry, block):
        start, scores, key_block, value_block = block_view(block)
        chances = jnp.exp(scores - log_total[..., None])
        pressure = jnp.einsum(
            "qrhd,krhd->rhqk", mixed_grad, value_block, preferred_element_type=jnp.float32
        )
        score_grad = (chances * (pressure - delta[..., None])).astype(jnp.bfloat16)
        carry = (
            carry
            + jnp.einsum(
                "rhqk,krhd->qrhd", score_grad, key_block, preferred_element_type=jnp.float32
            )
            * scale
        )
        key_grad = (
            jnp.einsum("rhqk,qrhd->krhd", score_grad, query, preferred_element_type=jnp.float32)
            * scale
        )
        value_grad = jnp.einsum(
            "rhqk,qrhd->krhd",
            chances.astype(jnp.bfloat16),
            mixed_grad,
            preferred_element_type=jnp.float32,
        )
        block_mix, block_base, block_vmix, block_vbase = split_factors(
            lax.dynamic_slice_in_dim(every, start, block_rows, 0).astype(jnp.float32)
        )
        key_mix_grad = (
            jnp.einsum("krhd,krcd->krhc", key_grad, block_base, precision=highest) / KV_RANK
        )
        key_base_grad = (
            jnp.einsum("krhc,krhd->krcd", block_mix, key_grad, precision=highest) / KV_RANK
        )
        value_mix_grad = (
            jnp.einsum("krhd,krcd->krhc", value_grad, block_vbase, precision=highest) / KV_RANK
        )
        value_base_grad = (
            jnp.einsum("krhc,krhd->krcd", block_vmix, value_grad, precision=highest) / KV_RANK
        )
        block_grad = jnp.concatenate(
            [
                key_mix_grad.reshape(block_rows, batch_rows, mix_width),
                key_base_grad.reshape(block_rows, batch_rows, base_width),
                value_mix_grad.reshape(block_rows, batch_rows, mix_width),
                value_base_grad.reshape(block_rows, batch_rows, base_width),
            ],
            axis=-1,
        )
        return (carry, block_grad)

    query_grad, factor_blocks = lax.scan(
        grad_step,
        jnp.zeros((local, batch_rows, HEADS, HEAD_DIM), jnp.float32),
        jnp.arange(block_count),
    )
    factor_grads = factor_blocks.reshape(total, batch_rows, 2 * mix_width + 2 * base_width)
    own_factor_grads = lax.psum_scatter(
        factor_grads.astype(jnp.bfloat16), "wide", scatter_dimension=0, tiled=True
    ).astype(jnp.float32)
    key_base_back = rotate(
        own_factor_grads[..., mix_width : mix_width + base_width].reshape(
            local, batch_rows, KV_RANK, HEAD_DIM
        ),
        cosine,
        -sine,
    ).reshape(local, batch_rows, base_width)
    factor_low = (
        jnp.concatenate(
            [
                own_factor_grads[..., :mix_width],
                key_base_back,
                own_factor_grads[..., mix_width + base_width :],
            ],
            axis=-1,
        )
        .astype(jnp.bfloat16)
        .reshape(flat_rows, -1)
    )
    mix_grad = jnp.einsum("trhd,trcd->trhc", query_grad, query_base, precision=highest) / Q_RANK
    base_roped_grad = (
        jnp.einsum("trhc,trhd->trcd", query_mix, query_grad, precision=highest) / Q_RANK
    )
    base_grad = rotate(base_roped_grad, cosine, -sine)
    mix_low = mix_grad.astype(jnp.bfloat16).reshape(flat_rows, HEADS * Q_RANK)
    base_low = base_grad.astype(jnp.bfloat16).reshape(flat_rows, Q_RANK * HEAD_DIM)
    query_heads_grad = jnp.einsum("tk,tf->kf", flat, mix_low, preferred_element_type=jnp.float32)
    query_basis_grad = jnp.einsum("tk,tf->kf", flat, base_low, preferred_element_type=jnp.float32)
    factor_weight_grad = jnp.einsum(
        "tk,tf->kf", flat, factor_low, preferred_element_type=jnp.float32
    )
    first_normed_grad = (
        jnp.einsum("tf,kf->tk", mix_low, query_heads, preferred_element_type=jnp.float32)
        + jnp.einsum("tf,kf->tk", base_low, query_basis, preferred_element_type=jnp.float32)
        + jnp.einsum("tf,kf->tk", factor_low, factor_weight, preferred_element_type=jnp.float32)
    ).reshape(local, batch_rows, width)
    first_gain_partial = jnp.sum(first_normed_grad * (inputs * first_scale), axis=(0, 1))
    tokens_gradient = residual_grad + norm_backward(
        inputs, first_gain, first_scale, first_normed_grad
    )
    key_heads_grad = factor_weight_grad[:, :mix_width]
    key_basis_grad = factor_weight_grad[:, mix_width : mix_width + base_width]
    value_heads_grad = factor_weight_grad[:, mix_width + base_width : 2 * mix_width + base_width]
    value_basis_grad = factor_weight_grad[:, 2 * mix_width + base_width :]
    (
        first_share,
        qheads_share,
        qbasis_share,
        kheads_share,
        kbasis_share,
        vheads_share,
        vbasis_share,
        output_share,
        second_share,
    ) = (
        lax.psum_scatter(
            first_gain_partial.astype(jnp.bfloat16), "wide", scatter_dimension=0, tiled=True
        ).astype(jnp.float32),
        lax.psum_scatter(
            query_heads_grad.astype(jnp.bfloat16), "wide", scatter_dimension=0, tiled=True
        ).astype(jnp.float32),
        lax.psum_scatter(
            query_basis_grad.astype(jnp.bfloat16), "wide", scatter_dimension=0, tiled=True
        ).astype(jnp.float32),
        lax.psum_scatter(
            key_heads_grad.astype(jnp.bfloat16), "wide", scatter_dimension=0, tiled=True
        ).astype(jnp.float32),
        lax.psum_scatter(
            key_basis_grad.astype(jnp.bfloat16), "wide", scatter_dimension=0, tiled=True
        ).astype(jnp.float32),
        lax.psum_scatter(
            value_heads_grad.astype(jnp.bfloat16), "wide", scatter_dimension=0, tiled=True
        ).astype(jnp.float32),
        lax.psum_scatter(
            value_basis_grad.astype(jnp.bfloat16), "wide", scatter_dimension=0, tiled=True
        ).astype(jnp.float32),
        lax.psum_scatter(
            output_weight_grad.astype(jnp.bfloat16), "wide", scatter_dimension=0, tiled=True
        ).astype(jnp.float32),
        lax.psum_scatter(
            second_gain_partial.astype(jnp.bfloat16), "wide", scatter_dimension=0, tiled=True
        ).astype(jnp.float32),
    )
    gate_share = pair_weight_grad[:, :hidden_width]
    lift_share = pair_weight_grad[:, hidden_width:]
    totals = (
        lax.psum(first_share.astype(jnp.bfloat16), "batch").astype(jnp.float32),
        lax.psum(qheads_share.astype(jnp.bfloat16), "batch").astype(jnp.float32),
        lax.psum(qbasis_share.astype(jnp.bfloat16), "batch").astype(jnp.float32),
        lax.psum(kheads_share.astype(jnp.bfloat16), "batch").astype(jnp.float32),
        lax.psum(kbasis_share.astype(jnp.bfloat16), "batch").astype(jnp.float32),
        lax.psum(vheads_share.astype(jnp.bfloat16), "batch").astype(jnp.float32),
        lax.psum(vbasis_share.astype(jnp.bfloat16), "batch").astype(jnp.float32),
        lax.psum(output_share.astype(jnp.bfloat16), "batch").astype(jnp.float32),
        lax.psum(second_share.astype(jnp.bfloat16), "batch").astype(jnp.float32),
        lax.psum(gate_share.astype(jnp.bfloat16), "batch").astype(jnp.float32),
        lax.psum(lift_share.astype(jnp.bfloat16), "batch").astype(jnp.float32),
        lax.psum(down_gradient.astype(jnp.bfloat16), "batch").astype(jnp.float32),
    )
    return (
        output,
        tokens_gradient,
        totals[0],
        totals[1],
        totals[2],
        totals[3],
        totals[4],
        totals[5],
        totals[6],
        totals[7],
        totals[8],
        totals[9],
        totals[10],
        totals[11],
    )


def partners(distance, count):
    return [(i, i ^ distance) for i in range(count)]


def fence(*values):
    return lax.optimization_barrier(values)


def after(value, *others):
    return lax.optimization_barrier((value,) + others)[0]


def in_order(value):
    return with_layout_constraint(value, Layout(tuple(range(value.ndim))))


def body(
    tokens,
    lengths,
    cotangent,
    first_gain,
    query_heads,
    query_basis,
    key_heads,
    key_basis,
    value_heads,
    value_basis,
    output_weight,
    second_gain,
    gate_weight,
    up_weight,
    down_projection_weight,
):
    local, rows, width = tokens.shape
    wide = ("y", "x", "core")
    n = lax.axis_size(wide)
    depth = lax.axis_size("batch")
    me = lax.axis_index(wide).astype(jnp.int32)
    at_y = lax.axis_index("y").astype(jnp.int32).reshape(1)

    def swap(value, distance):
        return lax.ppermute(value, wide, partners(distance, n))

    def swap_batch(value, distance):
        return lax.ppermute(value, "batch", partners(distance, depth))

    core, across, along, diagonal = 1, 2, 4, 6
    chips = (across, along, diagonal)

    def send_chips(value):
        return [swap(value, distance) for distance in chips]

    def send_slots(sums):
        return [swap(sums[i + 1], chips[i]) for i in range(len(chips))]

    def add(*values):
        return sum(value.astype(F32) for value in values).astype(BF16)

    places = me * local + jnp.arange(local, dtype=jnp.int32)
    slots = lengths.shape[1]
    upto = jnp.arange(slots)[:, None] >= jnp.arange(slots)[None, :]
    ends = jnp.sum(jnp.where(upto[None], lengths[:, None, :], 0), axis=2)
    passed = ends[:, None, :] <= places[None, :, None]
    start = jnp.max(jnp.where(passed, ends[:, None, :], 0), axis=2)
    valid = places[None, :] < ends[:, -1:]
    position = places[None, :] - start
    first_seen = jnp.where(valid, start, places[None, :])
    frequency = 10000.0 ** (-jnp.arange(HALF, dtype=F32) / HALF)
    angle = position.astype(F32)[:, None, :] * frequency[None, :, None]
    cosine, sine = jnp.cos(angle), jnp.sin(angle)
    info = jnp.stack([first_seen, jnp.broadcast_to(places, (rows, local))], axis=1)
    info = jnp.concatenate([info, jnp.zeros((rows, 6, local), jnp.int32)], axis=1)
    spans = jnp.stack(
        [
            jnp.min(first_seen, axis=1) // local,
            jnp.broadcast_to(me + 1, (rows,)),
            jnp.broadcast_to(me, (rows,)),
        ],
        axis=1,
    ).astype(jnp.int32)

    gain1 = first_gain.reshape(1, width)
    gain2 = second_gain.reshape(1, width)
    projections = (query_heads, query_basis, key_heads, key_basis, value_heads, value_basis)
    narrow = tuple(w.T if w.shape[1] < TILE else w for w in projections)

    xs = [tokens[:, b, :] for b in range(rows)]
    projected = [project(xs[0], gain1, narrow, cosine[0], sine[0])]
    sent0 = send_chips(projected[0][0])
    x1 = after(xs[1], projected[0][0])
    projected.append(project(x1, gain1, narrow, cosine[1], sine[1]))
    sent1 = send_chips(projected[1][0])
    own_weights = jnp.stack(
        [after(gate_weight.T, projected[1][0]), up_weight.T, down_projection_weight]
    )
    other_weights = swap(own_weights, along)
    near = jnp.stack([projected[0][0]] + [after(got, own_weights) for got in sent0])
    far = swap(near, core)
    gathered = [(near, far)]
    seen = after(valid, near)
    ups = [jnp.where(seen[b][:, None], cotangent[:, b, :], 0) for b in range(rows)]
    up_pair = jnp.concatenate(ups, axis=0)
    up_got = swap(up_pair, across)

    def forward(b):
        outs = attend_forward(
            spans[b], projected[b][1], *gathered[b], info[b], xs[b], output_weight, gain2
        )
        return outs[:4], outs[4]

    gathered[0] = (near, after(far, up_pair))
    kept0, n20 = forward(0)
    n20, up_got, *sent1 = fence(n20, up_got, *sent1)
    n2_sent0 = swap(n20, across)
    near = jnp.stack([projected[1][0]] + list(sent1))
    far = swap(near, core)
    up_near = [
        jnp.concatenate([ups[b], up_got[b * local : (b + 1) * local]], axis=0)
        for b in range(rows)
    ]
    near, far, *up_near = fence(near, far, *up_near)
    gathered.append((near, far))
    up_far = [swap(up_near[b], core) for b in range(rows)]
    kept1, n21 = forward(1)
    n2_sent1 = swap(n21, across)
    n21, up_far0, up_far1, n2_sent0, other_weights = fence(
        n21, *up_far, n2_sent0, other_weights
    )
    weights = jnp.concatenate([own_weights, other_weights], axis=1)
    attended = (kept0, kept1)

    near0 = jnp.concatenate([n20, n2_sent0], axis=0)
    far0 = swap(near0, core)
    sn0, bn0, grads = feed_forward(at_y, near0, up_near[0], weights)
    sn0, bn0, grads, far0 = fence(sn0, bn0, grads, far0)
    sf0, bf0, grads = feed_forward(at_y, far0, up_far0, weights, grads)
    sf0, bf0, grads, n2_sent1 = fence(sf0, bf0, grads, n2_sent1)
    near1 = jnp.concatenate([n21, n2_sent1], axis=0)
    far1 = swap(near1, core)
    sf0_got = swap(sf0, core)
    sn1, bn1, grads = feed_forward(at_y, near1, up_near[1], weights, grads)
    sn1, bn1, grads, sf0_got, far1 = fence(sn1, bn1, grads, sf0_got, far1)
    sum0 = add(sn0, sf0_got)
    theirs = sum0[local:]
    across0 = swap(theirs, across)
    sf1, bf1, grads = feed_forward(
        at_y, after(far1, theirs), up_far1, weights, grads, True
    )
    sf1, bf1, grads, across0 = fence(sf1, bf1, grads, across0)
    block_part = lax.psum_scatter(
        grads.reshape(-1, width), ("y", "batch"), scatter_dimension=0, tiled=True
    )

    def residual_of(b, mine, got):
        mixed, out_t, lse, hidden = attended[b]
        return residual(
            mine, got, ups[b], hidden, gain2, output_weight, out_t, (0, 1, 2, 3, 5, 6)
        )

    sf1_got = swap(sf1, core)
    residual0 = residual_of(0, sum0[:local], across0)
    *residual0, sf1_got = fence(*residual0, sf1_got)
    sum1 = add(sn1, sf1_got)
    theirs = sum1[local:]

    def back(b, outs, *hold):
        res, low, dot, delta, gain_share = outs
        fac, qt, qmix, qbase, normed = projected[b]
        return attend_backward(
            (40, 0.1)[b], spans[b], qt, *gathered[b], info[b], after(dot, *hold), attended[b][2], delta,
            qmix, qbase, cosine[b], sine[b],
        )

    across1 = swap(theirs, across)
    bf_got = [swap(value, core) for value in (bf0, bf1)]
    dnear0, dfar0, dq0 = back(0, residual0, theirs)
    dnear0, dfar0, dq0, across1, *bf_got = fence(dnear0, dfar0, dq0, across1, *bf_got)
    dfar0_got = swap(dfar0, core)
    residual1 = residual_of(1, sum1[:local], across1)
    *residual1, dnear0, dfar0_got = fence(*residual1, dnear0, dfar0_got)
    residuals = (residual0, residual1)
    fsum0 = add(dnear0, dfar0_got)
    fparts0 = send_slots(fsum0)
    dnear1, dfar1, dq1 = back(1, residual1, fsum0)
    dnear1, dfar1, dq1, *fparts0 = fence(dnear1, dfar1, dq1, *fparts0)

    dfar1_got = swap(dfar1, core)
    dfar1_got, dnear1 = fence(dfar1_got, dnear1)
    fsum1 = add(dnear1, dfar1_got)
    fparts1 = send_slots(fsum1)
    wo_near, wo_far = output_weight_shares(
        lax.axis_index("core").astype(jnp.int32).reshape(1),
        [after(attended[0][0], fsum1), attended[1][0]],
        [residuals[b][1] for b in range(rows)],
        n,
    )
    wo_got = swap(wo_far, core)
    branch_mine, branch_theirs = branch_sums([after(bn0, wo_near), bn1], bf_got)
    block_part, fsum1, wo_near, branch_mine, branch_theirs = fence(
        block_part, fsum1, wo_near, branch_mine, branch_theirs
    )
    block_grad = lax.all_gather(block_part, "batch", axis=0, tiled=True)
    *fparts1, fsum1, wo_got = fence(*fparts1, fsum1, wo_got)
    low0, low1, near, far = share(
        me.reshape(1),
        [fsum0[0]] + list(fparts0),
        [fsum1[0]] + list(fparts1),
        (dq0, dq1),
        cosine,
        sine,
        [projected[b][4] for b in range(rows)],
        (residual0[4], residual1[4]),
        n,
    )
    far_got = swap(far, core)
    far_got, near = fence(far_got, near)
    small = add(near, far_got)
    small_sent = send_slots(small)
    wo_sum = add(wo_near, after(wo_got, small))
    wo_parts = lax.all_to_all(wo_sum, ("y", "x"), 0, 0, tiled=True)
    *small_sent, small = fence(*small_sent, small)
    small = add(small[0], *small_sent)
    small_got = swap_batch(small, 1)
    branch_got = swap(after(branch_theirs, small), across)
    grads = [
        finish(after((low0, low1)[b], small), xs[b], gain1, residuals[b][0], narrow)
        for b in range(rows)
    ]
    tokens_gradient = in_order(jnp.stack(grads, axis=1))
    columns = jnp.concatenate(
        [
            lax.dynamic_slice_in_dim(w, after(me, small) * (width // n), width // n, 0)
            for w in projections
        ],
        axis=1,
    ).astype(F32).T
    small_got, small, wo_parts, tokens_gradient, columns = fence(
        small_got, small, wo_parts, tokens_gradient, columns
    )
    small = add(small, small_got)
    small_got = swap_batch(small, depth - 1)
    wo_total = jnp.sum(after(wo_parts, small).astype(F32), axis=0).astype(BF16)
    wo_got = swap_batch(wo_total, 1)
    outputs = []
    for b in range(rows):
        mine = branch_mine[b * local : (b + 1) * local].astype(F32)
        got = after(branch_got, wo_total)[b * local : (b + 1) * local].astype(F32)
        outputs.append(
            jnp.where(valid[b][:, None], attended[b][3] + (mine + got), 0.0).astype(BF16)
        )
    output = in_order(jnp.stack(outputs, axis=1))
    wo_got, wo_total, output, block_grad = fence(wo_got, wo_total, output, block_grad)
    wo_total = add(wo_total, wo_got)
    wo_got = swap_batch(wo_total, depth - 1)
    small = small.astype(F32) + after(small_got, wo_total).astype(F32)
    hid = gate_weight.shape[1]
    down_grad = block_grad[:hid].astype(F32)
    gate_grad = block_grad[hid : 2 * hid].astype(F32).T
    lift_grad = block_grad[2 * hid :].astype(F32).T
    output_weight_grad = wo_total.astype(F32) + after(wo_got, small).astype(F32)
    count = width // n

    def pick(at, size):
        return small[at : at + size].T

    query_heads_grad = pick(0, QMIX)
    query_basis_grad = pick(QMIX, QBASE)
    at = QMIX + QBASE
    key_heads_grad = pick(at, MIX)
    key_basis_grad = pick(at + MIX, BASE)
    value_heads_grad = pick(at + MIX + BASE, MIX)
    value_basis_grad = pick(at + 2 * MIX + BASE, BASE)
    at = at + FACTORS
    second_gain_grad = small[at].reshape(count)
    weighted = small[:at] * columns
    own_gain = lax.dynamic_slice_in_dim(first_gain, me * count, count, 0)
    first_gain_grad = jnp.sum(weighted, axis=0) / own_gain

    return (
        output,
        tokens_gradient,
        first_gain_grad,
        query_heads_grad,
        query_basis_grad,
        key_heads_grad,
        key_basis_grad,
        value_heads_grad,
        value_basis_grad,
        output_weight_grad,
        second_gain_grad,
        gate_grad,
        lift_grad,
        down_grad,
    )


def solution(mesh):
    batch, wide = mesh.shape["batch"], mesh.shape["wide"]
    split = wide == 8 and batch == 4
    w = "wide"
    if split:
        mesh = jax.sharding.Mesh(
            mesh.devices.reshape(batch, 2, 2, 2), ("batch", "y", "x", "core")
        )
        w = ("y", "x", "core")
    rows = P(w, "batch", None)
    return jax.shard_map(
        body if split else general_body,
        mesh=mesh,
        in_specs=(rows, P("batch", None), rows)
        + (P(),) * 9
        + (P(None, w), P(None, w), P(w, None)),
        out_specs=(rows, rows, P(w))
        + (P(w, None),) * 7
        + (P(w), P(None, w), P(None, w), P(w, None)),
        check_vma=False,
    )
```

```python
import functools

import jax
import jax.numpy as jnp
from jax import lax
from jax.experimental import pallas as pl
from jax.experimental.pallas import tpu as pltpu
from jax.experimental.layout import Layout, with_layout_constraint
from jax.sharding import PartitionSpec as P

HEADS = 16
HEAD_DIM = 64
Q_RANK = 6
KV_RANK = 2
HALF = HEAD_DIM // 2
MIX = HEADS * KV_RANK
BASE = KV_RANK * HEAD_DIM
FACTORS = 2 * MIX + 2 * BASE
QMIX = HEADS * Q_RANK
QBASE = Q_RANK * HEAD_DIM
QUAD = 4
QUADS = HEADS // QUAD
QW = QUAD * HEAD_DIM
TILE = 128
F32 = jnp.float32
BF16 = jnp.bfloat16
NEG = -1e30
MIB = 1 << 20


def mm(a, b):
    return jnp.dot(a, b, preferred_element_type=F32)


def mm_nt(a, b):
    return lax.dot_general(a, b, (((1,), (1,)), ((), ())), preferred_element_type=F32)


def mm_tn(a, b):
    return lax.dot_general(a, b, (((0,), (0,)), ((), ())), preferred_element_type=F32)


def whole(count):
    return [pl.BlockSpec(memory_space=pltpu.VMEM)] * count


def streamed(shape):
    return pl.BlockSpec(shape, lambda *_, rank=len(shape): (0,) * rank)


def kernel_call(
    kernel, name, outs, scratch, smem, limit, micros, *args, kept=(), far=(), aliases={}
):
    specs = [
        pl.BlockSpec(memory_space=pltpu.SMEM)
        if i < smem
        else streamed(arg.shape)
        if i in far
        else pl.BlockSpec(memory_space=pltpu.VMEM)
        for i, arg in enumerate(args)
    ]
    return pl.pallas_call(
        kernel,
        out_shape=tuple(
            pltpu.HBM(s, t) if i in kept else jax.ShapeDtypeStruct(s, t)
            for i, (s, t) in enumerate(outs)
        ),
        in_specs=specs,
        out_specs=[
            streamed(s) if i in kept else pl.BlockSpec(memory_space=pltpu.VMEM)
            for i, (s, _) in enumerate(outs)
        ],
        scratch_shapes=scratch,
        compiler_params=pltpu.CompilerParams(vmem_limit_bytes=limit * MIB),
        cost_estimate=pl.CostEstimate(
            flops=int(micros * 1e9), transcendentals=0, bytes_accessed=int(micros * 1e6)
        ),
        input_output_aliases=aliases,
        name=name,
    )(
        *(
            pltpu.with_memory_space_constraint(arg, pltpu.HBM) if i in far else arg
            for i, arg in enumerate(args)
        )
    )


def project_kernel(
    x_ref, gain_ref, qh_ref, qb_ref, kh_ref, kb_ref, vh_ref, vb_ref, cos_ref, sin_ref,
    fac_ref, qt_ref, qmix_ref, qbase_ref, normed_ref,
):
    x = x_ref[...].astype(F32)
    scale = lax.rsqrt(jnp.mean(x * x, axis=-1, keepdims=True) + 1e-06)
    normed = (x * scale * gain_ref[...]).astype(BF16)
    normed_ref[...] = normed
    cos = cos_ref[...]
    sin = sin_ref[...]

    def rope(v):
        a, b = v[:HALF], v[HALF:]
        return jnp.concatenate([a * cos - b * sin, a * sin + b * cos], axis=0)

    kb = mm(normed, kb_ref[...]).T
    fac_ref[0:MIX, :] = mm_nt(kh_ref[...], normed).astype(BF16)
    for r in range(KV_RANK):
        at = MIX + r * HEAD_DIM
        fac_ref[at : at + HEAD_DIM, :] = rope(kb[r * HEAD_DIM : (r + 1) * HEAD_DIM]).astype(BF16)
    fac_ref[MIX + BASE : 2 * MIX + BASE, :] = mm_nt(vh_ref[...], normed).astype(BF16)
    fac_ref[2 * MIX + BASE :, :] = mm(normed, vb_ref[...]).T.astype(BF16)
    qmix = mm_nt(qh_ref[...], normed)
    qmix_ref[...] = qmix
    raw = mm(normed, qb_ref[...]).T
    base = [rope(raw[r * HEAD_DIM : (r + 1) * HEAD_DIM]) for r in range(Q_RANK)]
    for r in range(Q_RANK):
        qbase_ref[r * HEAD_DIM : (r + 1) * HEAD_DIM, :] = base[r]
    for h in range(HEADS):
        out = None
        for r in range(Q_RANK):
            part = qmix[h * Q_RANK + r : h * Q_RANK + r + 1, :] * base[r]
            out = part if out is None else out + part
        qt_ref[h * HEAD_DIM : (h + 1) * HEAD_DIM, :] = (
            (out * (1.0 / Q_RANK)).astype(BF16) * (HEAD_DIM ** -0.5)
        ).astype(BF16)


def project(x, gain, weights, cos, sin):
    local, d = x.shape
    width = HEADS * HEAD_DIM
    return kernel_call(
        project_kernel,
        "project",
        (
            ((FACTORS, local), BF16),
            ((width, local), BF16),
            ((QMIX, local), F32),
            ((QBASE, local), F32),
            ((local, d), BF16),
        ),
        [],
        0,
        16,
        2,
        x, gain, *weights, cos, sin,
        kept=(1, 2, 3, 4),
    )


def materialize(fac, offset, head):
    base = offset + MIX
    out = None
    for r in range(KV_RANK):
        row = offset + head * KV_RANK + r
        part = fac[row : row + 1, :] * fac[base + r * HEAD_DIM : base + (r + 1) * HEAD_DIM, :]
        out = part if out is None else out + part
    return (out * (1.0 / KV_RANK)).astype(BF16)


def materialize_quad(fac, offset, quad):
    return jnp.concatenate(
        [materialize(fac, offset, quad * QUAD + i) for i in range(QUAD)], axis=0
    )


def each_block(me, lo, hi, slots, do):
    for slot in range(slots):
        kb = jnp.bitwise_xor(me, slot)
        pl.when((kb >= lo) & (kb < hi))(functools.partial(do, slot, kb))


def block_factors(slot, near, far):
    return (far if slot & 1 else near)[slot >> 1].astype(F32)


def forward_kernel(
    span, qt_ref, near_ref, far_ref, info_ref, x_ref, wo_ref, gain_ref,
    mixed_ref, out_t_ref, lse_ref, hidden_ref, n2_ref,
    k_s, vt_s, qbd_s, acc_s, m_s, l_s, bias_s,
):
    slots, kb_size, _ = k_s.shape
    count = qt_ref.shape[1]
    lo, hi, me = span[0], span[1], span[2]

    def prepare(slot, kb):
        fac = block_factors(slot, near_ref, far_ref)
        for quad in range(QUADS):
            rows = slice(quad * QW, (quad + 1) * QW)
            k_s[kb, :, rows] = materialize_quad(fac, 0, quad).T
            vt_s[kb, rows, :] = materialize_quad(fac, MIX + BASE, quad)

    each_block(me, lo, hi, slots, prepare)
    qbd_s[...] = jnp.zeros_like(qbd_s)
    for h in range(HEADS):
        quad, i = h // QUAD, h % QUAD
        qbd_s[quad, i * HEAD_DIM : (i + 1) * HEAD_DIM, i * count : (i + 1) * count] = qt_ref[
            h * HEAD_DIM : (h + 1) * HEAD_DIM, :
        ]
    m_s[...] = jnp.full_like(m_s, NEG)
    l_s[...] = jnp.zeros_like(l_s)
    acc_s[...] = jnp.zeros_like(acc_s)
    first = info_ref[0:1, :]
    last = info_ref[1:2, :]

    def step(kb, _):
        places = kb * kb_size + lax.broadcasted_iota(jnp.int32, (kb_size, count), 0)
        bias_s[...] = jnp.where((places >= first) & (places <= last), 0.0, NEG)
        for quad in range(QUADS):
            s = mm(k_s[kb, :, quad * QW : (quad + 1) * QW], qbd_s[quad])
            ps = []
            alphas = []
            for i in range(QUAD):
                h = quad * QUAD + i
                sh = s[:, i * count : (i + 1) * count] + bias_s[...]
                old = m_s[h : h + 1, :]
                new = jnp.maximum(old, jnp.max(sh, axis=0, keepdims=True))
                alpha = jnp.exp(old - new)
                p = jnp.exp(sh - new)
                m_s[h : h + 1, :] = new
                l_s[h : h + 1, :] = l_s[h : h + 1, :] * alpha + jnp.sum(p, axis=0, keepdims=True)
                ps.append(p.astype(BF16))
                alphas.append(alpha)
            for j in range(QUAD // 2):
                both = jnp.concatenate(ps[2 * j : 2 * j + 2], axis=1)
                at = quad * QW + j * 2 * HEAD_DIM
                o = mm(vt_s[kb, at : at + 2 * HEAD_DIM, :], both)
                for i in range(2):
                    r = slice(at + i * HEAD_DIM, at + (i + 1) * HEAD_DIM)
                    acc_s[r, :] = (
                        acc_s[r, :] * alphas[2 * j + i]
                        + o[i * HEAD_DIM : (i + 1) * HEAD_DIM, i * count : (i + 1) * count]
                    )
        return 0

    lax.fori_loop(lo, hi, step, 0)
    lse_ref[...] = m_s[...] + jnp.log(l_s[...])
    for h in range(HEADS):
        rows = slice(h * HEAD_DIM, (h + 1) * HEAD_DIM)
        out_t_ref[rows, :] = acc_s[rows, :] * (1.0 / l_s[h : h + 1, :])

    mixed = out_t_ref[...].astype(BF16).T
    mixed_ref[...] = mixed
    hidden = x_ref[...].astype(F32) + mm(mixed, wo_ref[...])
    hidden_ref[...] = hidden
    scale = lax.rsqrt(jnp.mean(hidden * hidden, axis=-1, keepdims=True) + 1e-06)
    n2_ref[...] = (hidden * scale * gain_ref[...]).astype(BF16)


def attend_forward(span, qt, near, far, info, x, wo, gain):
    width, local = qt.shape
    kb = local
    blocks = 2 * near.shape[0]
    d = x.shape[1]
    return kernel_call(
        forward_kernel,
        "attend_forward",
        (
            ((local, width), BF16),
            ((width, local), F32),
            ((HEADS, local), F32),
            ((local, d), F32),
            ((local, d), BF16),
        ),
        [
            pltpu.VMEM((blocks, kb, width), BF16),
            pltpu.VMEM((blocks, width, kb), BF16),
            pltpu.VMEM((QUADS, QW, QUAD * local), BF16),
            pltpu.VMEM((width, local), F32),
            pltpu.VMEM((HEADS, local), F32),
            pltpu.VMEM((HEADS, local), F32),
            pltpu.VMEM((kb, local), F32),
        ],
        1,
        32,
        10,
        span, qt, near, far, info, x, wo, gain,
        kept=(0, 1, 2, 3),
    )


def ffn_kernel(first, final, *refs):
    at_y, n2_ref, up_ref, w_ref = refs[:4]
    prev = None if first else refs[4]
    sng_ref, branch_ref, sums = refs[-3:]
    n2 = n2_ref[...]
    up = up_ref[...]
    hid = w_ref.shape[1]
    gate = mm_nt(n2, w_ref[0])
    lifted = mm_nt(n2, w_ref[1])
    hidden_grad = mm_nt(up, w_ref[2])
    sigmoid = jax.nn.sigmoid(gate)
    silu = gate * sigmoid
    act = (silu * lifted).astype(BF16)
    gate_grad = (hidden_grad * lifted * (sigmoid * (1.0 + gate * (1.0 - sigmoid)))).astype(BF16)
    lift_grad = (hidden_grad * silu).astype(BF16)
    sng_ref[...] = (mm(gate_grad, w_ref[0]) + mm(lift_grad, w_ref[1])).astype(BF16)
    branch_ref[...] = mm(act, w_ref[2]).astype(BF16)
    for at, (left, right) in enumerate(((act, up), (gate_grad, n2), (lift_grad, n2))):
        grad = mm_tn(left, right)
        if not first:
            grad = grad + prev[at]
        if not final:
            sums[at] = grad
        else:
            half = hid // 2
            low = grad.astype(BF16)
            sums[at_y[0], at] = low[:half]
            sums[1 - at_y[0], at] = low[half:]


def feed_forward(at_y, n2, up, weights, prev=None, final=False):
    count, d = n2.shape
    hid = weights.shape[1]
    if final:
        grads = (((2, 3, hid // 2, d), BF16),)
    else:
        grads = ((weights.shape, F32),)
    args = (at_y, n2, up, weights) if prev is None else (at_y, n2, up, weights, prev)
    return kernel_call(
        functools.partial(ffn_kernel, prev is None, final),
        "feed_forward",
        (((count, d), BF16),) * 2 + grads,
        [],
        1,
        19,
        0.05,
        *args,
        kept=(1, 2) if final else (1,),
        aliases={} if prev is None or final else {4: 2},
    )


def residual_kernel(
    sa, sb, up_ref, hidden_ref, gain_ref, wo_ref, out_t_ref,
    res_ref, low_ref, dot_ref, delta_ref, gain_out,
):
    sng = sa[...].astype(F32) + sb[...].astype(F32)
    hidden = hidden_ref[...]
    scale = lax.rsqrt(jnp.mean(hidden * hidden, axis=-1, keepdims=True) + 1e-06)
    gain_out[...] = jnp.sum(sng * (hidden * scale), axis=0, keepdims=True)
    weighted = sng * gain_ref[...]
    inner = jnp.mean(hidden * weighted, axis=-1, keepdims=True)
    res = up_ref[...].astype(F32) + scale * weighted - hidden * (scale * scale * scale) * inner
    res_ref[...] = res
    low = res.astype(BF16)
    low_ref[...] = low
    dot = mm_nt(wo_ref[...], low).astype(BF16)
    dot_ref[...] = dot
    for h in range(HEADS):
        rows = slice(h * HEAD_DIM, (h + 1) * HEAD_DIM)
        delta_ref[h : h + 1, :] = jnp.sum(
            dot[rows].astype(F32) * out_t_ref[rows, :], axis=0, keepdims=True
        )


def residual(sa, sb, up, hidden, gain, wo, out_t, far=()):
    local, d = hidden.shape
    width = out_t.shape[0]
    return kernel_call(
        residual_kernel,
        "residual",
        (
            ((local, d), F32),
            ((local, d), BF16),
            ((width, local), BF16),
            ((HEADS, local), F32),
            ((1, d), F32),
        ),
        [],
        0,
        16,
        3,
        sa, sb, up, hidden, gain, wo, out_t,
        kept=(0, 2, 3),
        far=far,
    )


def backward_kernel(
    span, qt_ref, near_ref, far_ref, info_ref, dot_ref, lse_ref, delta_ref,
    qmix_ref, qbase_ref, cos_ref, sin_ref,
    dnear_ref, dfar_ref, dq_ref,
    k_s, kt_s, vt_s, dkt_s, dvt_s, qbd_s, qbdt_s, obd_s, obdt_s, dq_s, bias_s, lse_s, delta_s,
):
    slots, kb_size, _ = k_s.shape
    count = qt_ref.shape[1]
    lo, hi, me = span[0], span[1], span[2]
    dnear_ref[...] = jnp.zeros_like(dnear_ref)
    dfar_ref[...] = jnp.zeros_like(dfar_ref)

    def prepare(slot, kb):
        fac = block_factors(slot, near_ref, far_ref)
        for quad in range(QUADS):
            rows = slice(quad * QW, (quad + 1) * QW)
            kt = materialize_quad(fac, 0, quad)
            kt_s[kb, rows, :] = kt
            k_s[kb, :, rows] = kt.T
            vt_s[kb, rows, :] = materialize_quad(fac, MIX + BASE, quad)
            dkt_s[kb, rows, :] = jnp.zeros((QW, kb_size), F32)
            dvt_s[kb, rows, :] = jnp.zeros((QW, kb_size), F32)

    each_block(me, lo, hi, slots, prepare)
    qbdt_s[...] = jnp.zeros_like(qbdt_s)
    obdt_s[...] = jnp.zeros_like(obdt_s)

    for h in range(HEADS):
        quad, i = h // QUAD, h % QUAD
        to = slice(i * HEAD_DIM, (i + 1) * HEAD_DIM)
        at = slice(i * count, (i + 1) * count)
        rows = slice(h * HEAD_DIM, (h + 1) * HEAD_DIM)
        qbdt_s[quad, to, at] = qt_ref[rows, :]
        obdt_s[quad, to, at] = dot_ref[rows, :]
    for quad in range(QUADS):
        qbd_s[quad] = qbdt_s[quad].T
        obd_s[quad] = obdt_s[quad].T
    lse_t = lse_ref[:, :].T
    delta_t = delta_ref[:, :].T
    for h in range(HEADS):
        lse_s[h] = jnp.broadcast_to(lse_t[:, h : h + 1], (count, TILE))
        delta_s[h] = jnp.broadcast_to(delta_t[:, h : h + 1], (count, TILE))
    dq_s[...] = jnp.zeros_like(dq_s)
    info_t = info_ref[:, :].T
    first = info_t[:, 0:1]
    last = info_t[:, 1:2]

    def step(kb, _):
        places = kb * kb_size + lax.broadcasted_iota(jnp.int32, (count, kb_size), 1)
        bias_s[...] = jnp.where((places >= first) & (places <= last), 0.0, NEG)
        lane = lax.broadcasted_iota(jnp.int32, (count, QW), 1) // HEAD_DIM
        for quad in range(QUADS):
            rows = slice(quad * QW, (quad + 1) * QW)
            s = mm(qbd_s[quad], kt_s[kb, rows, :])
            dp = mm(obd_s[quad], vt_s[kb, rows, :])
            ps = []
            dss = []
            for i in range(QUAD):
                h = quad * QUAD + i
                at = slice(i * count, (i + 1) * count)
                lse = jnp.concatenate([lse_s[h]] * (kb_size // TILE), axis=1)
                delta = jnp.concatenate([delta_s[h]] * (kb_size // TILE), axis=1)
                p = jnp.exp((s[at] + bias_s[...]) - lse)
                ps.append(p.astype(BF16))
                dss.append((p * (dp[at] - delta)).astype(BF16))
            p4 = jnp.concatenate(ps, axis=0)
            ds4 = jnp.concatenate(dss, axis=0)
            dkt_s[kb, rows, :] += mm(qbdt_s[quad], ds4)
            dvt_s[kb, rows, :] += mm(obdt_s[quad], p4)
            dq = mm(ds4, k_s[kb, :, rows])
            out = dq[0:count]
            for i in range(1, QUAD):
                out = jnp.where(lane == i, dq[i * count : (i + 1) * count], out)
            dq_s[:, rows] += out
        return 0

    lax.fori_loop(lo, hi, step, 0)
    dqt = dq_s[...].T * (HEAD_DIM ** -0.5 / Q_RANK)
    qmix = qmix_ref[:, :]
    mixes = []
    for h in range(HEADS):
        part = dqt[h * HEAD_DIM : (h + 1) * HEAD_DIM, :]
        for r in range(Q_RANK):
            mixes.append(
                jnp.sum(
                    part * qbase_ref[r * HEAD_DIM : (r + 1) * HEAD_DIM, :], axis=0, keepdims=True
                )
            )
    dq_ref[:QMIX, :] = jnp.concatenate(mixes, axis=0).astype(BF16)
    cos = cos_ref[...]
    sin = sin_ref[...]
    for r in range(Q_RANK):
        out = None
        for h in range(HEADS):
            row = h * Q_RANK + r
            part = qmix[row : row + 1, :] * dqt[h * HEAD_DIM : (h + 1) * HEAD_DIM, :]
            out = part if out is None else out + part
        upper, lower = out[:HALF], out[HALF:]
        at = QMIX + r * HEAD_DIM
        dq_ref[at : at + HALF, :] = (upper * cos + lower * sin).astype(BF16)
        dq_ref[at + HALF : at + HEAD_DIM, :] = (lower * cos - upper * sin).astype(BF16)

    def fold(slot, kb):
        fac = block_factors(slot, near_ref, far_ref)
        to = dfar_ref if slot & 1 else dnear_ref
        for offset, grad in ((0, dkt_s), (MIX + BASE, dvt_s)):
            outs = [None] * KV_RANK
            mixes = []
            for h in range(HEADS):
                g = grad[kb, h * HEAD_DIM : (h + 1) * HEAD_DIM, :] * (1.0 / KV_RANK)
                for r in range(KV_RANK):
                    at = offset + MIX + r * HEAD_DIM
                    mixes.append(jnp.sum(g * fac[at : at + HEAD_DIM, :], axis=0, keepdims=True))
                    row = offset + h * KV_RANK + r
                    part = fac[row : row + 1, :] * g
                    outs[r] = part if outs[r] is None else outs[r] + part
            to[slot >> 1, offset : offset + MIX, :] = jnp.concatenate(mixes, axis=0).astype(BF16)
            for r in range(KV_RANK):
                at = offset + MIX + r * HEAD_DIM
                to[slot >> 1, at : at + HEAD_DIM, :] = outs[r].astype(BF16)

    each_block(me, lo, hi, slots, fold)


def attend_backward(micros, span, qt, near, far, info, dot, lse, delta, qmix, qbase, cos, sin):
    width, local = qt.shape
    kb = local
    blocks = 2 * near.shape[0]
    return kernel_call(
        backward_kernel,
        "attend_backward",
        (
            (near.shape, BF16),
            (near.shape, BF16),
            ((QMIX + QBASE, local), BF16),
        ),
        [
            pltpu.VMEM((blocks, kb, width), BF16),
            pltpu.VMEM((blocks, width, kb), BF16),
            pltpu.VMEM((blocks, width, kb), BF16),
            pltpu.VMEM((blocks, width, kb), F32),
            pltpu.VMEM((blocks, width, kb), F32),
            pltpu.VMEM((QUADS, QUAD * local, QW), BF16),
            pltpu.VMEM((QUADS, QW, QUAD * local), BF16),
            pltpu.VMEM((QUADS, QUAD * local, QW), BF16),
            pltpu.VMEM((QUADS, QW, QUAD * local), BF16),
            pltpu.VMEM((local, width), F32),
            pltpu.VMEM((local, kb), F32),
            pltpu.VMEM((HEADS, local, TILE), F32),
            pltpu.VMEM((HEADS, local, TILE), F32),
        ],
        1,
        56,
        micros,
        span, qt, near, far, info, dot, lse, delta, qmix, qbase, cos, sin,
        far=(1, 5, 6, 7, 8, 9),
    )


def share_kernel(*refs):
    me = refs[0]
    pieces = (refs[1:5], refs[5:9])
    dqs, coss, sins, normeds, gains = refs[9:11], refs[11:13], refs[13:15], refs[15:17], refs[17:19]
    lows = refs[19:21]
    near_ref, far_ref, all_s = refs[21:]
    query = QMIX + QBASE
    for b in range(2):
        first, second, third, fourth = (piece[...].astype(F32) for piece in pieces[b])
        total = (first + second) + (third + fourth)
        cos = coss[b][...]
        sin = sins[b][...]
        low_ref = lows[b]
        low_ref[:query, :] = dqs[b][...]
        low_ref[query:, :] = total.astype(BF16)
        for r in range(KV_RANK):
            at = MIX + r * HEAD_DIM
            upper, lower = total[at : at + HALF], total[at + HALF : at + HEAD_DIM]
            to = query + at
            low_ref[to : to + HALF, :] = (upper * cos + lower * sin).astype(BF16)
            low_ref[to + HALF : to + HEAD_DIM, :] = (lower * cos - upper * sin).astype(BF16)
    rows = query + FACTORS
    all_s[:rows, :] = mm(
        jnp.concatenate([low[...] for low in lows], axis=1),
        jnp.concatenate([normed[...] for normed in normeds], axis=0),
    )
    all_s[rows:, :] = jnp.concatenate(
        [gains[0][...] + gains[1][...], jnp.zeros((15, gains[0].shape[1]), F32)], axis=0
    )
    width = near_ref.shape[2]
    for is_far, ref in ((0, near_ref), (1, far_ref)):
        for slot in range(ref.shape[0]):
            at = pl.multiple_of(jnp.bitwise_xor(me[0], 2 * slot + is_far) * width, width)
            ref[slot] = all_s[:, pl.ds(at, width)].astype(BF16)


def share(me, pieces0, pieces1, dqs, cosine, sine, normeds, gains, slots):
    local, d = normeds[0].shape
    count = QMIX + QBASE + FACTORS
    return kernel_call(
        share_kernel,
        "share",
        (((count, local), BF16),) * 2 + (((slots // 2, count + 16, d // slots), BF16),) * 2,
        [pltpu.VMEM((count + 16, d), F32)],
        1,
        18,
        0.05,
        me, *pieces0, *pieces1, *dqs, cosine[0], cosine[1], sine[0], sine[1], *normeds, *gains,
        far=tuple(range(1, 17)),
        kept=(0, 1),
    )


def finish_kernel(*refs):
    low_ref, x_ref, gain_ref, res_ref = refs[:4]
    weights = refs[4:10]
    grad_ref = refs[10]
    low = low_ref[...].T
    grad = None
    at = 0
    for ref in weights:
        if ref.shape[0] == x_ref.shape[1]:
            count = ref.shape[1]
            part = mm_nt(low[:, at : at + count], ref[...])
        else:
            count = ref.shape[0]
            part = mm(low[:, at : at + count], ref[...])
        grad = part if grad is None else grad + part
        at += count
    x = x_ref[...].astype(F32)
    scale = lax.rsqrt(jnp.mean(x * x, axis=-1, keepdims=True) + 1e-06)
    weighted = grad * gain_ref[...]
    inner = jnp.mean(x * weighted, axis=-1, keepdims=True)
    grad_ref[...] = res_ref[...] + (scale * weighted - x * (scale * scale * scale) * inner)


def finish(low, x, gain, res, weights):
    local, d = x.shape
    return kernel_call(
        finish_kernel,
        "finish",
        (((local, d), F32),),
        [],
        0,
        16,
        0.05,
        low, x, gain, res, *weights,
        far=(1, 3, 4, 5, 6, 7, 8, 9),
    )[0]


def output_weight_kernel(core, m0, m1, low0, low1, near_ref, far_ref, all_s):
    all_s[...] = mm_tn(m0[...], low0[...]) + mm_tn(m1[...], low1[...])
    count = near_ref.shape[1]
    for chip in range(near_ref.shape[0]):
        for at, ref in ((core[0], near_ref), (1 - core[0], far_ref)):
            row = pl.multiple_of((2 * chip + at) * count, count)
            ref[chip] = all_s[pl.ds(row, count), :].astype(BF16)


def output_weight_shares(core, mixed, lows, slots):
    width, d = mixed[0].shape[1], lows[0].shape[1]
    return kernel_call(
        output_weight_kernel,
        "output_weight_shares",
        (((slots // 2, width // slots, d), BF16),) * 2,
        [pltpu.VMEM((width, d), F32)],
        1,
        16,
        0.05,
        core, *mixed, *lows,
        far=(1, 2, 3, 4),
    )


def branch_kernel(n0, n1, f0, f1, mine_ref, theirs_ref):
    half = mine_ref.shape[0] // 2
    for b, (near, far) in enumerate(((n0, f0), (n1, f1))):
        total = (near[...].astype(F32) + far[...].astype(F32)).astype(BF16)
        mine_ref[b * half : (b + 1) * half, :] = total[:half]
        theirs_ref[b * half : (b + 1) * half, :] = total[half:]


def branch_sums(nears, fars):
    return kernel_call(
        branch_kernel,
        "branch_sums",
        ((nears[0].shape, BF16),) * 2,
        [],
        0,
        16,
        0.05,
        *nears, *fars,
        kept=(0, 1),
        far=(0, 1, 2, 3),
    )


highest = lax.Precision.HIGHEST
masked_score = -1e30


def rms_scale(values):
    return lax.rsqrt(jnp.mean(values * values, axis=-1, keepdims=True) + 1e-06)


def norm_backward(values, gain, scaled, upstream):
    weighted = upstream * gain
    inner = jnp.mean(values * weighted, axis=-1, keepdims=True)
    return scaled * weighted - values * (scaled * scaled * scaled) * inner


def rotate(values, cosine, sine):
    half = values.shape[-1] // 2
    first = values[..., :half]
    second = values[..., half:]
    return jnp.concatenate(
        [first * cosine - second * sine, first * sine + second * cosine], axis=-1
    )


def row_layout(lengths_row, places):
    ends = jnp.cumsum(lengths_row)
    passed = ends[None, :] <= places[:, None]
    segment = jnp.sum(passed.astype(jnp.int32), axis=1)
    start = jnp.max(jnp.where(passed, ends[None, :], 0), axis=1)
    valid = places < ends[-1]
    return (segment, places - start, valid)


def rope_tables(position):
    half = HEAD_DIM // 2
    frequency = 10000.0 ** (-jnp.arange(half, dtype=jnp.float32) / half)
    angle = position.astype(jnp.float32)[..., None] * frequency
    return (jnp.cos(angle), jnp.sin(angle))


def split_factors(factors):
    mix_width = HEADS * KV_RANK
    base_width = KV_RANK * HEAD_DIM
    count, rows = (factors.shape[0], factors.shape[1])
    key_mix = factors[..., :mix_width].reshape(count, rows, HEADS, KV_RANK)
    key_base = factors[..., mix_width : mix_width + base_width].reshape(
        count, rows, KV_RANK, HEAD_DIM
    )
    value_mix = factors[..., mix_width + base_width : 2 * mix_width + base_width].reshape(
        count, rows, HEADS, KV_RANK
    )
    value_base = factors[..., 2 * mix_width + base_width :].reshape(count, rows, KV_RANK, HEAD_DIM)
    return (key_mix, key_base, value_mix, value_base)


def pair_gradient(hidden_grad, gate, lifted):
    sigmoid = jax.nn.sigmoid(gate)
    gate_grad = hidden_grad * lifted * (sigmoid * (1.0 + gate * (1.0 - sigmoid)))
    lift_grad = hidden_grad * (gate * sigmoid)
    return jnp.concatenate([gate_grad, lift_grad], axis=-1).astype(jnp.bfloat16)


def general_body(
    tokens,
    lengths,
    cotangent,
    first_gain,
    query_heads,
    query_basis,
    key_heads,
    key_basis,
    value_heads,
    value_basis,
    output_weight,
    second_gain,
    gate_weight,
    up_weight,
    down_projection_weight,
):
    local, batch_rows, width = tokens.shape
    total = local * lax.axis_size("wide")
    offset = lax.axis_index("wide") * local
    places = jnp.arange(total, dtype=jnp.int32)
    segment, position, valid = jax.vmap(row_layout, in_axes=(0, None))(lengths, places)
    own_places = offset + jnp.arange(local, dtype=jnp.int32)
    own_segment = lax.dynamic_slice_in_dim(segment, offset, local, 1)
    own_position = lax.dynamic_slice_in_dim(position, offset, local, 1)
    own_valid = lax.dynamic_slice_in_dim(valid, offset, local, 1)
    cosine, sine = rope_tables(jnp.transpose(own_position))
    cosine = cosine[:, :, None, :]
    sine = sine[:, :, None, :]
    keep_rows = jnp.transpose(own_valid)[:, :, None]
    scale = HEAD_DIM ** (-0.5)
    block_rows = min(512, total)
    block_count = total // block_rows
    mix_width = HEADS * KV_RANK
    base_width = KV_RANK * HEAD_DIM
    flat_rows = local * batch_rows
    inputs = tokens.astype(jnp.float32)
    first_scale = rms_scale(inputs)
    normed = (inputs * first_scale * first_gain).astype(jnp.bfloat16)
    flat = normed.reshape(flat_rows, width)
    query_mix = jnp.dot(flat, query_heads, preferred_element_type=jnp.float32).reshape(
        local, batch_rows, HEADS, Q_RANK
    )
    query_raw = jnp.dot(flat, query_basis, preferred_element_type=jnp.float32).reshape(
        local, batch_rows, Q_RANK, HEAD_DIM
    )
    query_base = rotate(query_raw, cosine, sine)
    factor_weight = jnp.concatenate([key_heads, key_basis, value_heads, value_basis], axis=1)
    factor_raw = jnp.dot(flat, factor_weight, preferred_element_type=jnp.float32).reshape(
        local, batch_rows, -1
    )
    key_roped = rotate(
        factor_raw[..., mix_width : mix_width + base_width].reshape(
            local, batch_rows, KV_RANK, HEAD_DIM
        ),
        cosine,
        sine,
    ).reshape(local, batch_rows, base_width)
    factors = jnp.concatenate(
        [factor_raw[..., :mix_width], key_roped, factor_raw[..., mix_width + base_width :]], axis=-1
    ).astype(jnp.bfloat16)
    every = lax.all_gather(factors, "wide", axis=0, tiled=True)
    key_mix, key_base, value_mix, value_base = split_factors(every)
    keys = (
        jnp.einsum("trhk,trkd->trhd", key_mix, key_base, preferred_element_type=jnp.float32)
        / KV_RANK
    ).astype(jnp.bfloat16)
    values = (
        jnp.einsum("trhk,trkd->trhd", value_mix, value_base, preferred_element_type=jnp.float32)
        / KV_RANK
    ).astype(jnp.bfloat16)
    query = (
        jnp.einsum(
            "trhk,trkd->trhd",
            query_mix,
            query_base,
            precision=highest,
            preferred_element_type=jnp.float32,
        )
        / Q_RANK
    ).astype(jnp.bfloat16)

    def block_view(block):
        start = block * block_rows
        key_places = start + jnp.arange(block_rows, dtype=jnp.int32)
        key_segment = lax.dynamic_slice_in_dim(segment, start, block_rows, 1)
        key_valid = lax.dynamic_slice_in_dim(valid, start, block_rows, 1)
        causal = key_places[None, :] <= own_places[:, None]
        itself = key_places[None, :] == own_places[:, None]
        allowed = (
            causal[None]
            & (own_segment[:, :, None] == key_segment[:, None, :])
            & (key_valid[:, None, :] | itself[None])
        )
        key_block = lax.dynamic_slice_in_dim(keys, start, block_rows, 0)
        value_block = lax.dynamic_slice_in_dim(values, start, block_rows, 0)
        product = (
            jnp.einsum("qrhd,krhd->rhqk", query, key_block, preferred_element_type=jnp.float32)
            * scale
        )
        scores = jnp.where(allowed[:, None], product, masked_score)
        return (start, scores, key_block, value_block)

    def max_step(carry, block):
        top, mass = carry
        scores = block_view(block)[1]
        higher = jnp.maximum(top, jnp.max(scores, axis=-1))
        mass = mass * jnp.exp(top - higher) + jnp.sum(jnp.exp(scores - higher[..., None]), axis=-1)
        return ((higher, mass), None)

    start_top = jnp.full((batch_rows, HEADS, local), masked_score, jnp.float32)
    (top, mass), _ = lax.scan(
        max_step, (start_top, jnp.zeros_like(start_top)), jnp.arange(block_count)
    )
    log_total = top + jnp.log(mass)

    def out_step(carry, block):
        _, scores, _, value_block = block_view(block)
        chances = jnp.exp(scores - log_total[..., None]).astype(jnp.bfloat16)
        return (
            carry
            + jnp.einsum(
                "rhqk,krhd->qrhd", chances, value_block, preferred_element_type=jnp.float32
            ),
            None,
        )

    attended, _ = lax.scan(
        out_step,
        jnp.zeros((local, batch_rows, HEADS, HEAD_DIM), jnp.float32),
        jnp.arange(block_count),
    )
    mixed = attended.astype(jnp.bfloat16).reshape(flat_rows, HEADS * HEAD_DIM)
    hidden_state = inputs + jnp.dot(
        mixed, output_weight, preferred_element_type=jnp.float32
    ).reshape(local, batch_rows, width)
    second_scale = rms_scale(hidden_state)
    normed_second = (hidden_state * second_scale * second_gain).astype(jnp.bfloat16)
    normalized_token_rows = lax.all_gather(normed_second, "wide", axis=0, tiled=True)
    gate_lifted_hidden = jnp.concatenate([gate_weight, up_weight], axis=1)
    hidden_width = gate_weight.shape[1]
    projected_output = jnp.einsum(
        "zec,cx->zex", normalized_token_rows, gate_lifted_hidden, preferred_element_type=jnp.float32
    )
    gate = projected_output[..., :hidden_width]
    lifted = projected_output[..., hidden_width:]
    silu_hidden_output = (jax.nn.silu(gate) * lifted).astype(jnp.bfloat16)
    sequence_portion = silu_hidden_output
    branch = lax.psum_scatter(
        jnp.einsum(
            "zyu,uv->zyv",
            sequence_portion,
            down_projection_weight,
            preferred_element_type=jnp.float32,
        ).astype(jnp.bfloat16),
        "wide",
        scatter_dimension=0,
        tiled=True,
    ).astype(jnp.float32)
    output = jnp.where(keep_rows, hidden_state + branch, 0.0).astype(jnp.bfloat16)
    upstream = jnp.where(keep_rows, cotangent.astype(jnp.float32), 0.0)
    upstream_low = upstream.astype(jnp.bfloat16)
    upstream_token_gradient = lax.all_gather(upstream_low, "wide", axis=0, tiled=True)
    hidden_grad = jnp.einsum(
        "ajg,vg->ajv",
        upstream_token_gradient,
        down_projection_weight,
        preferred_element_type=jnp.float32,
    )
    pair_product_gradient = pair_gradient(hidden_grad, gate, lifted)
    down_gradient = jnp.einsum(
        "imj,ima->ja",
        silu_hidden_output,
        upstream_token_gradient,
        preferred_element_type=jnp.float32,
    )
    pair_weight_grad = jnp.einsum(
        "ipl,ipj->lj",
        normalized_token_rows,
        pair_product_gradient,
        preferred_element_type=jnp.float32,
    )
    sequence_portion = pair_product_gradient
    second_normed_grad = lax.psum_scatter(
        jnp.einsum(
            "ivu,bu->ivb", sequence_portion, gate_lifted_hidden, preferred_element_type=jnp.float32
        ),
        "wide",
        scatter_dimension=0,
        tiled=True,
    )
    second_gain_partial = jnp.sum(second_normed_grad * (hidden_state * second_scale), axis=(0, 1))
    residual_grad = upstream + norm_backward(
        hidden_state, second_gain, second_scale, second_normed_grad
    )
    residual_low = residual_grad.astype(jnp.bfloat16).reshape(flat_rows, width)
    output_weight_grad = jnp.einsum(
        "tk,td->kd", mixed, residual_low, preferred_element_type=jnp.float32
    )
    mixed_grad = (
        jnp.einsum("td,kd->tk", residual_low, output_weight, preferred_element_type=jnp.float32)
        .astype(jnp.bfloat16)
        .reshape(local, batch_rows, HEADS, HEAD_DIM)
    )

    def delta_step(carry, block):
        _, scores, _, value_block = block_view(block)
        chances = jnp.exp(scores - log_total[..., None])
        pressure = jnp.einsum(
            "qrhd,krhd->rhqk", mixed_grad, value_block, preferred_element_type=jnp.float32
        )
        return (carry + jnp.sum(chances * pressure, axis=-1), None)

    delta, _ = lax.scan(
        delta_step, jnp.zeros((batch_rows, HEADS, local), jnp.float32), jnp.arange(block_count)
    )

    def grad_step(carry, block):
        start, scores, key_block, value_block = block_view(block)
        chances = jnp.exp(scores - log_total[..., None])
        pressure = jnp.einsum(
            "qrhd,krhd->rhqk", mixed_grad, value_block, preferred_element_type=jnp.float32
        )
        score_grad = (chances * (pressure - delta[..., None])).astype(jnp.bfloat16)
        carry = (
            carry
            + jnp.einsum(
                "rhqk,krhd->qrhd", score_grad, key_block, preferred_element_type=jnp.float32
            )
            * scale
        )
        key_grad = (
            jnp.einsum("rhqk,qrhd->krhd", score_grad, query, preferred_element_type=jnp.float32)
            * scale
        )
        value_grad = jnp.einsum(
            "rhqk,qrhd->krhd",
            chances.astype(jnp.bfloat16),
            mixed_grad,
            preferred_element_type=jnp.float32,
        )
        block_mix, block_base, block_vmix, block_vbase = split_factors(
            lax.dynamic_slice_in_dim(every, start, block_rows, 0).astype(jnp.float32)
        )
        key_mix_grad = (
            jnp.einsum("krhd,krcd->krhc", key_grad, block_base, precision=highest) / KV_RANK
        )
        key_base_grad = (
            jnp.einsum("krhc,krhd->krcd", block_mix, key_grad, precision=highest) / KV_RANK
        )
        value_mix_grad = (
            jnp.einsum("krhd,krcd->krhc", value_grad, block_vbase, precision=highest) / KV_RANK
        )
        value_base_grad = (
            jnp.einsum("krhc,krhd->krcd", block_vmix, value_grad, precision=highest) / KV_RANK
        )
        block_grad = jnp.concatenate(
            [
                key_mix_grad.reshape(block_rows, batch_rows, mix_width),
                key_base_grad.reshape(block_rows, batch_rows, base_width),
                value_mix_grad.reshape(block_rows, batch_rows, mix_width),
                value_base_grad.reshape(block_rows, batch_rows, base_width),
            ],
            axis=-1,
        )
        return (carry, block_grad)

    query_grad, factor_blocks = lax.scan(
        grad_step,
        jnp.zeros((local, batch_rows, HEADS, HEAD_DIM), jnp.float32),
        jnp.arange(block_count),
    )
    factor_grads = factor_blocks.reshape(total, batch_rows, 2 * mix_width + 2 * base_width)
    own_factor_grads = lax.psum_scatter(
        factor_grads.astype(jnp.bfloat16), "wide", scatter_dimension=0, tiled=True
    ).astype(jnp.float32)
    key_base_back = rotate(
        own_factor_grads[..., mix_width : mix_width + base_width].reshape(
            local, batch_rows, KV_RANK, HEAD_DIM
        ),
        cosine,
        -sine,
    ).reshape(local, batch_rows, base_width)
    factor_low = (
        jnp.concatenate(
            [
                own_factor_grads[..., :mix_width],
                key_base_back,
                own_factor_grads[..., mix_width + base_width :],
            ],
            axis=-1,
        )
        .astype(jnp.bfloat16)
        .reshape(flat_rows, -1)
    )
    mix_grad = jnp.einsum("trhd,trcd->trhc", query_grad, query_base, precision=highest) / Q_RANK
    base_roped_grad = (
        jnp.einsum("trhc,trhd->trcd", query_mix, query_grad, precision=highest) / Q_RANK
    )
    base_grad = rotate(base_roped_grad, cosine, -sine)
    mix_low = mix_grad.astype(jnp.bfloat16).reshape(flat_rows, HEADS * Q_RANK)
    base_low = base_grad.astype(jnp.bfloat16).reshape(flat_rows, Q_RANK * HEAD_DIM)
    query_heads_grad = jnp.einsum("tk,tf->kf", flat, mix_low, preferred_element_type=jnp.float32)
    query_basis_grad = jnp.einsum("tk,tf->kf", flat, base_low, preferred_element_type=jnp.float32)
    factor_weight_grad = jnp.einsum(
        "tk,tf->kf", flat, factor_low, preferred_element_type=jnp.float32
    )
    first_normed_grad = (
        jnp.einsum("tf,kf->tk", mix_low, query_heads, preferred_element_type=jnp.float32)
        + jnp.einsum("tf,kf->tk", base_low, query_basis, preferred_element_type=jnp.float32)
        + jnp.einsum("tf,kf->tk", factor_low, factor_weight, preferred_element_type=jnp.float32)
    ).reshape(local, batch_rows, width)
    first_gain_partial = jnp.sum(first_normed_grad * (inputs * first_scale), axis=(0, 1))
    tokens_gradient = residual_grad + norm_backward(
        inputs, first_gain, first_scale, first_normed_grad
    )
    key_heads_grad = factor_weight_grad[:, :mix_width]
    key_basis_grad = factor_weight_grad[:, mix_width : mix_width + base_width]
    value_heads_grad = factor_weight_grad[:, mix_width + base_width : 2 * mix_width + base_width]
    value_basis_grad = factor_weight_grad[:, 2 * mix_width + base_width :]
    (
        first_share,
        qheads_share,
        qbasis_share,
        kheads_share,
        kbasis_share,
        vheads_share,
        vbasis_share,
        output_share,
        second_share,
    ) = (
        lax.psum_scatter(
            first_gain_partial.astype(jnp.bfloat16), "wide", scatter_dimension=0, tiled=True
        ).astype(jnp.float32),
        lax.psum_scatter(
            query_heads_grad.astype(jnp.bfloat16), "wide", scatter_dimension=0, tiled=True
        ).astype(jnp.float32),
        lax.psum_scatter(
            query_basis_grad.astype(jnp.bfloat16), "wide", scatter_dimension=0, tiled=True
        ).astype(jnp.float32),
        lax.psum_scatter(
            key_heads_grad.astype(jnp.bfloat16), "wide", scatter_dimension=0, tiled=True
        ).astype(jnp.float32),
        lax.psum_scatter(
            key_basis_grad.astype(jnp.bfloat16), "wide", scatter_dimension=0, tiled=True
        ).astype(jnp.float32),
        lax.psum_scatter(
            value_heads_grad.astype(jnp.bfloat16), "wide", scatter_dimension=0, tiled=True
        ).astype(jnp.float32),
        lax.psum_scatter(
            value_basis_grad.astype(jnp.bfloat16), "wide", scatter_dimension=0, tiled=True
        ).astype(jnp.float32),
        lax.psum_scatter(
            output_weight_grad.astype(jnp.bfloat16), "wide", scatter_dimension=0, tiled=True
        ).astype(jnp.float32),
        lax.psum_scatter(
            second_gain_partial.astype(jnp.bfloat16), "wide", scatter_dimension=0, tiled=True
        ).astype(jnp.float32),
    )
    gate_share = pair_weight_grad[:, :hidden_width]
    lift_share = pair_weight_grad[:, hidden_width:]
    totals = (
        lax.psum(first_share.astype(jnp.bfloat16), "batch").astype(jnp.float32),
        lax.psum(qheads_share.astype(jnp.bfloat16), "batch").astype(jnp.float32),
        lax.psum(qbasis_share.astype(jnp.bfloat16), "batch").astype(jnp.float32),
        lax.psum(kheads_share.astype(jnp.bfloat16), "batch").astype(jnp.float32),
        lax.psum(kbasis_share.astype(jnp.bfloat16), "batch").astype(jnp.float32),
        lax.psum(vheads_share.astype(jnp.bfloat16), "batch").astype(jnp.float32),
        lax.psum(vbasis_share.astype(jnp.bfloat16), "batch").astype(jnp.float32),
        lax.psum(output_share.astype(jnp.bfloat16), "batch").astype(jnp.float32),
        lax.psum(second_share.astype(jnp.bfloat16), "batch").astype(jnp.float32),
        lax.psum(gate_share.astype(jnp.bfloat16), "batch").astype(jnp.float32),
        lax.psum(lift_share.astype(jnp.bfloat16), "batch").astype(jnp.float32),
        lax.psum(down_gradient.astype(jnp.bfloat16), "batch").astype(jnp.float32),
    )
    return (
        output,
        tokens_gradient,
        totals[0],
        totals[1],
        totals[2],
        totals[3],
        totals[4],
        totals[5],
        totals[6],
        totals[7],
        totals[8],
        totals[9],
        totals[10],
        totals[11],
    )


def partners(distance, count):
    return [(i, i ^ distance) for i in range(count)]


def fence(*values):
    return lax.optimization_barrier(values)


def after(value, *others):
    return lax.optimization_barrier((value,) + others)[0]


def in_order(value):
    return with_layout_constraint(value, Layout(tuple(range(value.ndim))))


def body(
    tokens,
    lengths,
    cotangent,
    first_gain,
    query_heads,
    query_basis,
    key_heads,
    key_basis,
    value_heads,
    value_basis,
    output_weight,
    second_gain,
    gate_weight,
    up_weight,
    down_projection_weight,
):
    local, rows, width = tokens.shape
    wide = ("y", "x", "core")
    n = lax.axis_size(wide)
    depth = lax.axis_size("batch")
    me = lax.axis_index(wide).astype(jnp.int32)
    at_y = lax.axis_index("y").astype(jnp.int32).reshape(1)

    def swap(value, distance):
        return lax.ppermute(value, wide, partners(distance, n))

    def swap_batch(value, distance):
        return lax.ppermute(value, "batch", partners(distance, depth))

    core, across, along, diagonal = 1, 2, 4, 6
    chips = (across, along, diagonal)

    def send_chips(value):
        return [swap(value, distance) for distance in chips]

    def send_slots(sums):
        return [swap(sums[i + 1], chips[i]) for i in range(len(chips))]

    def add(*values):
        return sum(value.astype(F32) for value in values).astype(BF16)

    places = me * local + jnp.arange(local, dtype=jnp.int32)
    slots = lengths.shape[1]
    upto = jnp.arange(slots)[:, None] >= jnp.arange(slots)[None, :]
    ends = jnp.sum(jnp.where(upto[None], lengths[:, None, :], 0), axis=2)
    passed = ends[:, None, :] <= places[None, :, None]
    start = jnp.max(jnp.where(passed, ends[:, None, :], 0), axis=2)
    valid = places[None, :] < ends[:, -1:]
    position = places[None, :] - start
    first_seen = jnp.where(valid, start, places[None, :])
    frequency = 10000.0 ** (-jnp.arange(HALF, dtype=F32) / HALF)
    angle = position.astype(F32)[:, None, :] * frequency[None, :, None]
    cosine, sine = jnp.cos(angle), jnp.sin(angle)
    info = jnp.stack([first_seen, jnp.broadcast_to(places, (rows, local))], axis=1)
    info = jnp.concatenate([info, jnp.zeros((rows, 6, local), jnp.int32)], axis=1)
    spans = jnp.stack(
        [
            jnp.min(first_seen, axis=1) // local,
            jnp.broadcast_to(me + 1, (rows,)),
            jnp.broadcast_to(me, (rows,)),
        ],
        axis=1,
    ).astype(jnp.int32)

    gain1 = first_gain.reshape(1, width)
    gain2 = second_gain.reshape(1, width)
    projections = (query_heads, query_basis, key_heads, key_basis, value_heads, value_basis)
    narrow = tuple(w.T if w.shape[1] < TILE else w for w in projections)

    xs = [tokens[:, b, :] for b in range(rows)]
    projected = [project(xs[0], gain1, narrow, cosine[0], sine[0])]
    sent0 = send_chips(projected[0][0])
    x1 = after(xs[1], projected[0][0])
    projected.append(project(x1, gain1, narrow, cosine[1], sine[1]))
    sent1 = send_chips(projected[1][0])
    own_weights = jnp.stack(
        [after(gate_weight.T, projected[1][0]), up_weight.T, down_projection_weight]
    )
    other_weights = swap(own_weights, along)
    near = jnp.stack([projected[0][0]] + [after(got, own_weights) for got in sent0])
    far = swap(near, core)
    gathered = [(near, far)]
    seen = after(valid, near)
    ups = [jnp.where(seen[b][:, None], cotangent[:, b, :], 0) for b in range(rows)]
    up_pair = jnp.concatenate(ups, axis=0)
    up_got = swap(up_pair, across)

    def forward(b):
        outs = attend_forward(
            spans[b], projected[b][1], *gathered[b], info[b], xs[b], output_weight, gain2
        )
        return outs[:4], outs[4]

    gathered[0] = (near, after(far, up_pair))
    kept0, n20 = forward(0)
    n20, up_got, *sent1 = fence(n20, up_got, *sent1)
    n2_sent0 = swap(n20, across)
    near = jnp.stack([projected[1][0]] + list(sent1))
    far = swap(near, core)
    up_near = [
        jnp.concatenate([ups[b], up_got[b * local : (b + 1) * local]], axis=0)
        for b in range(rows)
    ]
    near, far, *up_near = fence(near, far, *up_near)
    gathered.append((near, far))
    up_far = [swap(up_near[b], core) for b in range(rows)]
    kept1, n21 = forward(1)
    n2_sent1 = swap(n21, across)
    n21, up_far0, up_far1, n2_sent0, other_weights = fence(
        n21, *up_far, n2_sent0, other_weights
    )
    weights = jnp.concatenate([own_weights, other_weights], axis=1)
    attended = (kept0, kept1)

    near0 = jnp.concatenate([n20, n2_sent0], axis=0)
    far0 = swap(near0, core)
    sn0, bn0, grads = feed_forward(at_y, near0, up_near[0], weights)
    sn0, bn0, grads, far0 = fence(sn0, bn0, grads, far0)
    sf0, bf0, grads = feed_forward(at_y, far0, up_far0, weights, grads)
    sf0, bf0, grads, n2_sent1 = fence(sf0, bf0, grads, n2_sent1)
    near1 = jnp.concatenate([n21, n2_sent1], axis=0)
    far1 = swap(near1, core)
    sf0_got = swap(sf0, core)
    sn1, bn1, grads = feed_forward(at_y, near1, up_near[1], weights, grads)
    sn1, bn1, grads, sf0_got, far1 = fence(sn1, bn1, grads, sf0_got, far1)
    sum0 = add(sn0, sf0_got)
    theirs = sum0[local:]
    across0 = swap(theirs, across)
    sf1, bf1, grads = feed_forward(
        at_y, after(far1, theirs), up_far1, weights, grads, True
    )
    sf1, bf1, grads, across0 = fence(sf1, bf1, grads, across0)
    block_part = lax.psum_scatter(
        grads.reshape(-1, width), ("y", "batch"), scatter_dimension=0, tiled=True
    )

    def residual_of(b, mine, got):
        mixed, out_t, lse, hidden = attended[b]
        return residual(
            mine, got, ups[b], hidden, gain2, output_weight, out_t, (0, 1, 2, 3, 5, 6)
        )

    sf1_got = swap(sf1, core)
    residual0 = residual_of(0, sum0[:local], across0)
    *residual0, sf1_got = fence(*residual0, sf1_got)
    sum1 = add(sn1, sf1_got)
    theirs = sum1[local:]

    def back(b, outs, *hold):
        res, low, dot, delta, gain_share = outs
        fac, qt, qmix, qbase, normed = projected[b]
        return attend_backward(
            (40, 0.1)[b], spans[b], qt, *gathered[b], info[b], after(dot, *hold), attended[b][2], delta,
            qmix, qbase, cosine[b], sine[b],
        )

    across1 = swap(theirs, across)
    bf_got = [swap(value, core) for value in (bf0, bf1)]
    dnear0, dfar0, dq0 = back(0, residual0, theirs)
    dnear0, dfar0, dq0, across1, *bf_got = fence(dnear0, dfar0, dq0, across1, *bf_got)
    dfar0_got = swap(dfar0, core)
    residual1 = residual_of(1, sum1[:local], across1)
    *residual1, dnear0, dfar0_got = fence(*residual1, dnear0, dfar0_got)
    residuals = (residual0, residual1)
    fsum0 = add(dnear0, dfar0_got)
    fparts0 = send_slots(fsum0)
    dnear1, dfar1, dq1 = back(1, residual1, fsum0)
    dnear1, dfar1, dq1, *fparts0 = fence(dnear1, dfar1, dq1, *fparts0)

    dfar1_got = swap(dfar1, core)
    dfar1_got, dnear1 = fence(dfar1_got, dnear1)
    fsum1 = add(dnear1, dfar1_got)
    fparts1 = send_slots(fsum1)
    *fparts1, fsum1 = fence(*fparts1, fsum1)
    low0, low1, near, far = share(
        me.reshape(1),
        [fsum0[0]] + list(fparts0),
        [fsum1[0]] + list(fparts1),
        (dq0, dq1),
        cosine,
        sine,
        [projected[b][4] for b in range(rows)],
        (residual0[4], residual1[4]),
        n,
    )
    far_got = swap(far, core)
    block_part, far = fence(block_part, far)
    block_grad = lax.all_gather(block_part, "batch", axis=0, tiled=True)
    far_got, near = fence(far_got, near)
    small = add(near, far_got)
    small_sent = send_slots(small)
    wo_near, wo_far = output_weight_shares(
        lax.axis_index("core").astype(jnp.int32).reshape(1),
        [after(attended[0][0], small), attended[1][0]],
        [residuals[b][1] for b in range(rows)],
        n,
    )
    wo_got = swap(wo_far, core)
    branch_mine, branch_theirs = branch_sums([after(bn0, wo_near), bn1], bf_got)
    wo_sum = add(wo_near, after(wo_got, branch_mine))
    wo_parts = lax.all_to_all(wo_sum, ("y", "x"), 0, 0, tiled=True)
    *small_sent, small, branch_mine, wo_sum = fence(*small_sent, small, branch_mine, wo_sum)
    small = add(small[0], *small_sent)
    small_got = swap_batch(small, 1)
    branch_got = swap(after(branch_theirs, small), across)
    grads = [
        finish(after((low0, low1)[b], small), xs[b], gain1, residuals[b][0], narrow)
        for b in range(rows)
    ]
    tokens_gradient = in_order(jnp.stack(grads, axis=1))
    columns = jnp.concatenate(
        [
            lax.dynamic_slice_in_dim(w, after(me, small) * (width // n), width // n, 0)
            for w in projections
        ],
        axis=1,
    ).astype(F32).T
    small_got, small, wo_parts, tokens_gradient, columns = fence(
        small_got, small, wo_parts, tokens_gradient, columns
    )
    small = add(small, small_got)
    small_got = swap_batch(small, depth - 1)
    wo_total = jnp.sum(after(wo_parts, small).astype(F32), axis=0).astype(BF16)
    wo_got = swap_batch(wo_total, 1)
    outputs = []
    for b in range(rows):
        mine = branch_mine[b * local : (b + 1) * local].astype(F32)
        got = after(branch_got, wo_total)[b * local : (b + 1) * local].astype(F32)
        outputs.append(
            jnp.where(valid[b][:, None], attended[b][3] + (mine + got), 0.0).astype(BF16)
        )
    output = in_order(jnp.stack(outputs, axis=1))
    wo_got, wo_total, output, block_grad = fence(wo_got, wo_total, output, block_grad)
    wo_total = add(wo_total, wo_got)
    wo_got = swap_batch(wo_total, depth - 1)
    small = small.astype(F32) + after(small_got, wo_total).astype(F32)
    hid = gate_weight.shape[1]
    down_grad = block_grad[:hid].astype(F32)
    gate_grad = block_grad[hid : 2 * hid].astype(F32).T
    lift_grad = block_grad[2 * hid :].astype(F32).T
    output_weight_grad = wo_total.astype(F32) + after(wo_got, small).astype(F32)
    count = width // n

    def pick(at, size):
        return small[at : at + size].T

    query_heads_grad = pick(0, QMIX)
    query_basis_grad = pick(QMIX, QBASE)
    at = QMIX + QBASE
    key_heads_grad = pick(at, MIX)
    key_basis_grad = pick(at + MIX, BASE)
    value_heads_grad = pick(at + MIX + BASE, MIX)
    value_basis_grad = pick(at + 2 * MIX + BASE, BASE)
    at = at + FACTORS
    second_gain_grad = small[at].reshape(count)
    weighted = small[:at] * columns
    own_gain = lax.dynamic_slice_in_dim(first_gain, me * count, count, 0)
    first_gain_grad = jnp.sum(weighted, axis=0) / own_gain

    return (
        output,
        tokens_gradient,
        first_gain_grad,
        query_heads_grad,
        query_basis_grad,
        key_heads_grad,
        key_basis_grad,
        value_heads_grad,
        value_basis_grad,
        output_weight_grad,
        second_gain_grad,
        gate_grad,
        lift_grad,
        down_grad,
    )


def solution(mesh):
    batch, wide = mesh.shape["batch"], mesh.shape["wide"]
    split = wide == 8 and batch == 4
    w = "wide"
    if split:
        mesh = jax.sharding.Mesh(
            mesh.devices.reshape(batch, 2, 2, 2), ("batch", "y", "x", "core")
        )
        w = ("y", "x", "core")
    rows = P(w, "batch", None)
    return jax.shard_map(
        body if split else general_body,
        mesh=mesh,
        in_specs=(rows, P("batch", None), rows)
        + (P(),) * 9
        + (P(None, w), P(None, w), P(w, None)),
        out_specs=(rows, rows, P(w))
        + (P(w, None),) * 7
        + (P(w), P(None, w), P(None, w), P(w, None)),
        check_vma=False,
    )
```
